128 devices in a mesh: dp: 32 (over x, z_hi, y), tensor: 4 (over z_lo, core).
Axes of the slice: x: 4, y: 4, z: 4 (z_hi: 2, z_lo: 2; z = z_hi * 2 + z_lo), core: 2. Of those that a mesh axis runs over, the one named last changes fastest.
Arguments:
- tokens_in: bfloat16 [16384, 1024], P(('dp', 'tensor')), may hold values from -6 to 6
- image_starts: int32 [11], replicated, may hold values from 0 to 15014, as said below
- norm_gain: float32 [2, 2, 1024], replicated, may hold values from 0.5 to 1.5
- norm_bias: float32 [2, 2, 1024], replicated, may hold values from -1.5 to 1.5
- qkv_weight: bfloat16 [2, 1024, 3, 1024], P(None, None, None, 'tensor'), may hold values from -0.1875 to 0.1875
- qv_bias: float32 [2, 2, 1024], P(None, None, 'tensor'), may hold values from -0.1 to 0.1
- proj_weight: bfloat16 [2, 1024, 1024], P(None, 'tensor'), may hold values from -4 to 4
- out_bias: float32 [2, 2, 1024], replicated, may hold values from -1.5 to 1.5
- layer_scale: float32 [2, 2, 1024], replicated, may hold values from 0.5 to 1.5
- fc1_weight: bfloat16 [2, 1024, 4096], P(None, None, 'tensor'), may hold values from -0.1875 to 0.1875
- fc1_bias: float32 [2, 4096], P(None, 'tensor'), may hold values from -1.5 to 1.5
- fc2_weight: bfloat16 [2, 4096, 1024], P(None, 'tensor'), may hold values from -0.125 to 0.125
- out_grad: float32 [16384, 1024], P(('dp', 'tensor')), may hold values from -6 to 6
Outputs:
- tokens_out: bfloat16 [16384, 1024], P(('dp', 'tensor'))
- tokens_grad: float32 [16384, 1024], P(('dp', 'tensor'))
- norm_gain_grad: float32 [2, 2, 1024], replicated
- norm_bias_grad: float32 [2, 2, 1024], replicated
- qkv_weight_grad: float32 [2, 1024, 3, 1024], P(None, 'dp', None, 'tensor')
- qv_bias_grad: float32 [2, 2, 1024], P(None, None, 'tensor')
- proj_weight_grad: float32 [2, 1024, 1024], P(None, 'tensor', 'dp')
- out_bias_grad: float32 [2, 2, 1024], replicated
- layer_scale_grad: float32 [2, 2, 1024], replicated
- fc1_weight_grad: float32 [2, 1024, 4096], P(None, 'dp', 'tensor')
- fc1_bias_grad: float32 [2, 4096], P(None, 'tensor')
- fc2_weight_grad: float32 [2, 4096, 1024], P(None, 'tensor', 'dp')
The draws below stay inside these ranges and needn't reach their ends.
Inputs may be any that keep to these rules, and one draw needn't show every extreme that they name: `image_starts`: starts increase; every image is 1370 consecutive tokens and images do not intersect; the last image ends at the last token.
All inputs are finite; a program needn't handle non-finite values.
Results may differ from the reference program's by a relative error of at most 0.024.
Values may be sent and summed in bfloat16 or wider, within the bound.
A program may use at most 320 MiB of HBM per device.

```python
import jax
import jax.numpy as jnp
from jax import lax

D = 1024
HEADS = 16
HEAD_DIM = 64
FF = 4096
LAYERS = 2
IMG_LEN = 1370
STRETCH = 512
TOKENS = 16384
NIMG = 11


def draw_image_starts(key, part):
    key = jax.random.fold_in(key, 7)
    spare_rows = TOKENS - NIMG * IMG_LEN
    drawn_offsets = jnp.sort(jax.random.randint(key, (NIMG,), 0, spare_rows + 1))
    drawn_offsets = drawn_offsets.at[NIMG - 1].set(spare_rows)
    return (drawn_offsets + jnp.arange(NIMG, dtype=jnp.int32) * IMG_LEN).astype(jnp.int32)


def levels(key, dims, shards, low, top_value):
    loudness = 1.0
    for position, parts in shards:
        heights = jax.random.uniform(jax.random.fold_in(jax.random.fold_in(key, 6), position), (parts,), jnp.float32, low / len(shards), top_value / len(shards))
        loudness = loudness * jnp.repeat(jnp.exp(heights), dims[position] // parts).reshape((-1,) + (1,) * (len(dims) - 1 - position))
    return loudness


def noise(key, shape, deviation, most, split=(), held_as=jnp.bfloat16):
    values = deviation * jax.random.normal(key, shape, jnp.float32)
    if split:
        values = values * levels(key, shape, split, -0.22, 0.18)
    return jnp.clip(values, -most, most).astype(held_as)


def setup_inputs(seed: int = 0) -> dict:
    splits = jax.random.split(jax.random.key(seed), 14)
    return {
        "tokens_in": noise(splits[0], (TOKENS, D), 1.0, 6.0, ((0, 128),)),
        "image_starts": draw_image_starts(jax.random.fold_in(splits[13], 71), 0),
        "norm_gain": jnp.clip(jax.random.uniform(splits[2], (LAYERS, 2, D), jnp.float32, 0.5, 1.5), 0.5, 1.5),
        "norm_bias": noise(splits[3], (LAYERS, 2, D), 0.3, 1.5, (), jnp.float32),
        "qkv_weight": noise(splits[4], (LAYERS, D, 3, D), D ** -0.5, 0.1875, ((3, 4),)),
        "qv_bias": noise(splits[5], (LAYERS, 2, D), 0.02, 0.1, ((2, 4),), jnp.float32),
        "proj_weight": noise(splits[6], (LAYERS, D, D), (max(1, 4 * D // IMG_LEN)) ** -0.5, 4.0, ((1, 4),)),
        "out_bias": noise(splits[7], (LAYERS, 2, D), 0.3, 1.5, (), jnp.float32),
        "layer_scale": jnp.clip(jax.random.uniform(splits[8], (LAYERS, 2, D), jnp.float32, 0.5, 1.5), 0.5, 1.5),
        "fc1_weight": noise(splits[9], (LAYERS, D, FF), D ** -0.5, 0.1875, ((2, 4),)),
        "fc1_bias": noise(splits[10], (LAYERS, FF), 0.3, 1.5, ((1, 4),), jnp.float32),
        "fc2_weight": noise(splits[11], (LAYERS, FF, D), (FF // 2) ** -0.5, 0.125, ((1, 4),)),
        "out_grad": noise(splits[12], (TOKENS, D), 1.0, 6.0, ((0, 128),), jnp.float32),
    }


EPS = 1e-06
NEG = -1e+30
HIGHEST = lax.Precision.HIGHEST

@jax.custom_vjp
def low(v):
    return lax.optimization_barrier(v.astype(jnp.bfloat16)).astype(jnp.float32)

@jax.custom_vjp
def low_back(v):
    return v

def low_keep(v):
    return (low(v), None)

def low_pass(kept, grad):
    return (grad,)

def back_keep(v):
    return (v, None)

def back_low(kept, grad):
    return (low(grad),)
low.defvjp(low_keep, low_pass)
low_back.defvjp(back_keep, back_low)

def layer_norm(values, gain_row, bias_row):
    average = lax.optimization_barrier(jnp.mean(values, axis=-1, keepdims=True))
    centered = values - average
    spread = lax.optimization_barrier(jnp.mean(centered * centered, axis=-1, keepdims=True))
    return centered * lax.rsqrt(spread + EPS) * gain_row + bias_row

def segment_ids(positions, image_starts, total_rows):
    starts = image_starts.astype(jnp.int32)
    started = positions[:, None] >= starts[None, :]
    inside = started & (positions[:, None] < starts[None, :] + IMG_LEN)
    passed = lax.optimization_barrier(jnp.sum(started.astype(jnp.int32), axis=1))
    within = lax.optimization_barrier(jnp.sum(inside.astype(jnp.int32), axis=1))
    in_range = (positions >= 0) & (positions < total_rows)
    return jnp.where(in_range, 2 * passed - within, -1).astype(jnp.int32)

def attention(queries, keys, values, image_id):
    total_rows = queries.shape[0]
    halo_rows = IMG_LEN - 1
    span_rows = STRETCH + 2 * halo_rows
    factor = HEAD_DIM ** (-0.5)
    query_heads = queries.reshape(total_rows, HEADS, HEAD_DIM)
    key_pad = jnp.pad(keys, ((halo_rows, halo_rows), (0, 0))).reshape(-1, HEADS, HEAD_DIM)
    val_pad = jnp.pad(values, ((halo_rows, halo_rows), (0, 0))).reshape(-1, HEADS, HEAD_DIM)
    id_pad = jnp.pad(image_id, (halo_rows, halo_rows), constant_values=-1)

    def one_block(block_index):
        first_row = block_index * STRETCH
        query_part = lax.dynamic_slice_in_dim(query_heads, first_row, STRETCH, 0)
        key_part = lax.dynamic_slice_in_dim(key_pad, first_row, span_rows, 0)
        val_part = lax.dynamic_slice_in_dim(val_pad, first_row, span_rows, 0)
        query_ids = lax.dynamic_slice_in_dim(image_id, first_row, STRETCH, 0)
        key_ids = lax.dynamic_slice_in_dim(id_pad, first_row, span_rows, 0)
        same_image = query_ids[:, None] == key_ids[None, :]
        scores = low_back(jnp.einsum('qhe,khe->hqk', query_part, key_part, precision=HIGHEST) * factor)
        scores = jnp.where(same_image[None], scores, NEG)
        highest = lax.optimization_barrier(jnp.max(scores, axis=-1, keepdims=True))
        raised = jnp.exp(scores - highest)
        probs = low(raised / lax.optimization_barrier(jnp.sum(raised, axis=-1, keepdims=True)))
        return jnp.einsum('hqk,khe->qhe', probs, val_part, precision=HIGHEST)
    blocks = lax.map(jax.checkpoint(one_block), jnp.arange(total_rows // STRETCH, dtype=jnp.int32))
    return blocks.reshape(total_rows, HEADS * HEAD_DIM)

def layer_forward(hidden, image_id, gain_rows, bias_rows, w_qkv, bias_qv, w_proj, offsets, scales, w_first, bias_first, w_second):
    total_rows = hidden.shape[0]
    normed_one = low(layer_norm(hidden, gain_rows[0], bias_rows[0]))
    bias_three = jnp.stack([bias_qv[0], jnp.zeros_like(bias_qv[0]), bias_qv[1]])
    projected = jnp.dot(normed_one, w_qkv.reshape(D, 3 * D), precision=HIGHEST).reshape(total_rows, 3, D) + bias_three
    projected = low(low_back(projected))
    attended = low(low_back(attention(projected[:, 0], projected[:, 1], projected[:, 2], image_id)))
    branch_one = low_back(jnp.dot(attended, w_proj, precision=HIGHEST))
    mixed = hidden + scales[0] * (branch_one + offsets[0])
    normed_two = low(layer_norm(mixed, gain_rows[1], bias_rows[1]))
    pre_act = low_back(jnp.dot(normed_two, w_first, precision=HIGHEST) + bias_first)
    activated = low(jax.nn.gelu(pre_act, approximate=False))
    branch_two = low_back(jnp.dot(activated, w_second, precision=HIGHEST))
    return mixed + scales[1] * (branch_two + offsets[1])

def reference(tokens_in, image_starts, norm_gain, norm_bias, qkv_weight, qv_bias, proj_weight, out_bias, layer_scale, fc1_weight, fc1_bias, fc2_weight, out_grad):
    image_id = segment_ids(jnp.arange(TOKENS, dtype=jnp.int32), image_starts, TOKENS)
    params = tuple((param.astype(jnp.float32) for param in (norm_gain, norm_bias, qkv_weight, qv_bias, proj_weight, out_bias, layer_scale, fc1_weight, fc1_bias, fc2_weight)))

    def forward(hidden, *layer_params):
        for layer_index in range(LAYERS):
            hidden = layer_forward(hidden, image_id, *(param[layer_index] for param in layer_params))
        return hidden
    result, pull = jax.vjp(forward, tokens_in.astype(jnp.float32), *params)
    grads = pull(out_grad.astype(jnp.float32))
    return (result.astype(jnp.bfloat16), grads[0], grads[1], grads[2], grads[3], grads[4], grads[5], grads[6], grads[7], grads[8], grads[9], grads[10])
```

```python
import functools

import jax
import jax.numpy as jnp
from jax import lax
from jax.experimental import pallas as pl
from jax.experimental.pallas import tpu as pltpu
from jax.sharding import PartitionSpec as P

MESH = pl.DeviceIdType.MESH
BF = jnp.bfloat16
F32 = jnp.float32
VM = pl.BlockSpec(memory_space=pltpu.VMEM)
SM = pl.BlockSpec(memory_space=pltpu.SMEM)

HEAD_DIM = 64
IMG_LEN = 1370
EPS = 1e-06
NEG = -1e30

R = 128
S = 512
D = 1024
LW = 256
HL = LW // HEAD_DIM
F = 1024
TOTAL = 16384
NDP = 32
FAR3 = 384
OWN0 = FAR3 + 2 * S
NW = 2 * OWN0 + S
QB = 256
KB = 256
NB = NW // KB
C = 2
RC = R // C
MB = 1 << 20


def mm(a, b):
    return jnp.dot(a, b, preferred_element_type=F32)


def mm_rt(a, b):
    return lax.dot_general(a, b, (((1,), (1,)), ((), ())), preferred_element_type=F32)


def mm_lt(a, b):
    return lax.dot_general(a, b, (((0,), (0,)), ((), ())), preferred_element_type=F32)


class Place:
    def __init__(self):
        self.t = lax.axis_index("tensor")
        self.core = lax.rem(self.t, 2)
        self.mate = self.t + 1 - 2 * self.core
        self.cp = lax.rem(self.t + 2, 4)
        self.own = pl.multiple_of(self.t * R, R)
        self.opp = pl.multiple_of(self.cp * R, R)
        self.near = pl.multiple_of((self.t - self.core) * R, 2 * R)
        self.far = pl.multiple_of(2 * R - self.near, 2 * R)
        self.dp = lax.axis_index("dp")
        self.up = lax.rem(self.dp + 1, NDP)
        self.dn = lax.rem(self.dp + NDP - 1, NDP)


def greet(devices):
    barrier = pltpu.get_barrier_semaphore()
    for device in devices:
        pl.semaphore_signal(barrier, inc=1, device_id=device, device_id_type=MESH)
    pl.semaphore_wait(barrier, len(devices))


class Wires:
    def __init__(self, send, recv):
        self.send, self.recv, self.count, self.open = send, recv, 0, []

    def push(self, src, dst, device):
        k = self.count
        self.count += 1
        copy = pltpu.make_async_remote_copy(
            src, dst, self.send.at[k], self.recv.at[k], device_id=device, device_id_type=MESH
        )
        copy.start()
        self.open.append(copy)
        return copy

    def left(self, copy):
        copy.wait_send()
        self.open = [c for c in self.open if c is not copy]

    def close(self):
        for copy in self.open:
            copy.wait_send()


AG_SEMS = 2 * C + 1
RS_SEMS = 2 * C + 1


class Gather:
    def __init__(self, wires, at, buf):
        self.wires, self.at, self.buf = wires, at, buf
        own = at.own
        self.across = []
        for c in range(C):
            part = buf.at[pl.ds(own + c * RC, RC)]
            self.across.append(wires.push(part, part, {"tensor": at.cp}))
        part = buf.at[pl.ds(own, R)]
        self.beside = wires.push(part, part, {"tensor": at.mate})

    def near(self):
        self.beside.wait_recv()

    def far(self):
        passed = []
        for c in range(C):
            self.across[c].wait_recv()
            part = self.buf.at[pl.ds(self.at.opp + c * RC, RC)]
            passed.append(self.wires.push(part, part, {"tensor": self.at.mate}))
        for copy in passed:
            copy.wait_recv()


class Scatter:
    def __init__(self, wires, at, part, send1, recv1, send2, recv2, send3, recv3):
        self.wires, self.at, self.part = wires, at, part
        self.send1, self.recv1 = send1, recv1
        self.send2, self.recv2 = send2, recv2
        self.send3, self.recv3 = send3, recv3

    def far(self):
        at, wires = self.at, self.wires
        first = []
        for c in range(C):
            rows = pl.ds(c * RC, RC)
            src = pl.ds(pl.multiple_of((1 - at.core) * R + c * RC, RC), RC)
            self.send1[rows, :] = self.part[src, :].astype(BF)
            first.append(wires.push(self.send1.at[rows], self.recv1.at[rows], {"tensor": at.mate}))
        self.second = []
        for c in range(C):
            rows = pl.ds(c * RC, RC)
            src = pl.ds(pl.multiple_of(at.core * R + c * RC, RC), RC)
            first[c].wait_recv()
            total = self.part[src, :] + self.recv1[rows, :].astype(F32)
            self.send2[rows, :] = total.astype(BF)
            self.second.append(
                wires.push(self.send2.at[rows], self.recv2.at[rows], {"tensor": at.cp})
            )

    def near(self):
        at = self.at
        src = pl.ds(pl.multiple_of((1 - at.core) * R, R), R)
        self.send3[...] = self.part[src, :].astype(BF)
        self.third = self.wires.push(self.send3, self.recv3, {"tensor": at.mate})

    def total(self):
        self.third.wait_recv()
        for copy in self.second:
            copy.wait_recv()
        own = self.part[pl.ds(pl.multiple_of(self.at.core * R, R), R), :]
        return own + self.recv3[...].astype(F32) + self.recv2[...].astype(F32)


def scatter_scratch():
    return [pltpu.VMEM((2 * R, D), F32)] + [pltpu.VMEM((R, D), BF) for _ in range(6)]


def normalized(v):
    centered = v - jnp.mean(v, axis=-1, keepdims=True)
    scale = lax.rsqrt(jnp.mean(centered * centered, axis=-1, keepdims=True) + EPS)
    return centered * scale, scale


def norm_back(v, gain, grad):
    x_hat, scale = normalized(v)
    u = grad * gain
    grad_in = scale * (
        u
        - jnp.mean(u, axis=-1, keepdims=True)
        - x_hat * jnp.mean(u * x_hat, axis=-1, keepdims=True)
    )
    return (
        grad_in,
        jnp.sum(grad * x_hat, axis=0, keepdims=True),
        jnp.sum(grad, axis=0, keepdims=True),
    )


def call(kernel, name, cid, ins, outs, scratch, sems, limit=56, specs=None):
    shapes = [jax.ShapeDtypeStruct(shape, dtype) for shape, dtype in outs]
    extra = []
    if sems:
        extra = [pltpu.SemaphoreType.DMA((sems,)), pltpu.SemaphoreType.DMA((sems,))]
    params = dict(vmem_limit_bytes=limit * MB)
    if cid is not None:
        params.update(collective_id=cid, has_side_effects=True)
    return pl.pallas_call(
        kernel,
        out_shape=shapes,
        in_specs=specs or [VM] * len(ins),
        out_specs=[VM] * len(outs),
        scratch_shapes=list(scratch) + extra,
        compiler_params=pltpu.CompilerParams(**params),
        name=name,
    )(*ins)


def inward_kernel(h, gain, bias, b3, w, rows, q, win, ss, rs):
    at = Place()
    wires = Wires(ss, rs)
    greet([{"tensor": at.mate}, {"tensor": at.cp}, {"dp": at.up}, {"dp": at.dn}])
    x_hat, _ = normalized(h[...])
    rows[pl.ds(at.own, R), :] = (x_hat * gain[...] + bias[...]).astype(BF)
    gather = Gather(wires, at, rows)

    def project(first):
        out = (mm(rows[pl.ds(first, 2 * R), :], w[...]) + b3[...]).astype(BF)
        q[pl.ds(first, 2 * R), :] = out[:, :LW]
        win[pl.ds(OWN0 + first, 2 * R), :] = out[:, LW:]

    def hop(base, step, device):
        src = win.at[pl.ds(pl.multiple_of(base, 128), 2 * R)]
        dst = win.at[pl.ds(pl.multiple_of(base + step, 128), 2 * R)]
        return wires.push(src, dst, {"dp": device})

    gather.near()
    project(at.near)
    up1, dn1 = [hop(OWN0 + at.near, -S, at.up)], [hop(OWN0 + at.near, S, at.dn)]
    gather.far()
    project(at.far)
    up1.append(hop(OWN0 + at.far, -S, at.up))
    dn1.append(hop(OWN0 + at.far, S, at.dn))
    up2, dn2 = [], []
    for k, first in enumerate((at.near, at.far)):
        up1[k].wait_recv()
        up2.append(hop(OWN0 - S + first, -S, at.up))
        dn1[k].wait_recv()
        dn2.append(hop(OWN0 + S + first, S, at.dn))
    for copy in up2:
        copy.wait_recv()
    up3 = wires.push(
        win.at[pl.ds(OWN0 - S - FAR3, FAR3)], win.at[pl.ds(0, FAR3)], {"dp": at.up}
    )
    for copy in dn2:
        copy.wait_recv()
    dn3 = wires.push(
        win.at[pl.ds(OWN0 + 2 * S, FAR3)], win.at[pl.ds(OWN0 + 3 * S, FAR3)], {"dp": at.dn}
    )
    up3.wait_recv()
    dn3.wait_recv()
    wires.close()


def inward(cid, h, gain, bias, b3, w):
    return call(
        inward_kernel,
        "inward%d" % cid,
        cid,
        [h, gain, bias, b3, w],
        [((S, D), BF), ((S, LW), BF), ((NW, 2 * LW), BF)],
        [],
        AG_SEMS + 10,
    )


def ids_of(position, starts):
    total = jnp.zeros_like(position)
    for k in range(starts.shape[0]):
        first = starts[k]
        total += (position >= first).astype(jnp.int32)
        total += (position >= first + IMG_LEN).astype(jnp.int32)
    return jnp.where((position >= 0) & (position < TOTAL), total, -1)


def key_range(base, block, starts):
    first = base + block * QB
    last = first + QB - 1
    low, high = jnp.int32(0), jnp.int32(TOTAL)
    for k in range(starts.shape[0]):
        for edge in (starts[k], starts[k] + IMG_LEN):
            low = jnp.where(edge <= first, jnp.maximum(low, edge), low)
            high = jnp.where(edge > last, jnp.minimum(high, edge), high)
    low_block = lax.div(jnp.maximum(low - base + OWN0, 0), KB)
    high_block = lax.div(jnp.minimum(high - base + OWN0, NW) + KB - 1, KB)
    return low_block, high_block


def spread_heads(value, out):
    lane = lax.broadcasted_iota(jnp.int32, (QB, LW), 1)
    for head in range(HL):
        mine = (lane >= head * HEAD_DIM) & (lane < (head + 1) * HEAD_DIM)
        out[pl.ds(head * QB, QB), :] = jnp.where(mine, value, 0.0).astype(BF)


def pick_heads(parts):
    lane = lax.broadcasted_iota(jnp.int32, (QB, LW), 1)
    out = parts(0)
    for head in range(1, HL):
        out = jnp.where(lane >= head * HEAD_DIM, parts(head), out)
    return out


def attend_kernel(starts, q, win, out, lt, qm, sbuf, high, low, acc):
    base = lax.axis_index("dp") * S
    for block in range(S // QB):
        spread_heads(q[pl.ds(block * QB, QB), :].astype(F32) * 0.125, qm)
        qid = ids_of(
            base + block * QB + lax.broadcasted_iota(jnp.int32, (QB, 1), 0), starts
        )
        first, end = key_range(base, block, starts)
        high[...] = jnp.full_like(high, NEG)
        low[...] = jnp.zeros_like(low)
        acc[...] = jnp.zeros_like(acc)

        def scores(kb, carry):
            at = pl.multiple_of(kb * KB, KB)
            s = mm_rt(qm[...], win[pl.ds(at, KB), :LW])
            kid = ids_of(base - OWN0 + at + lax.broadcasted_iota(jnp.int32, (1, KB), 1), starts)
            bias = jnp.where(qid == kid, 0.0, NEG)
            for head in range(HL):
                rows = pl.ds(head * QB, QB)
                one = s[head * QB : (head + 1) * QB, :] + bias
                sbuf[kb, rows, :] = one
                high[rows, :] = jnp.maximum(
                    high[rows, :], jnp.maximum(one[:, :128], one[:, 128:])
                )
            return carry

        lax.fori_loop(first, end, scores, 0)
        top = jnp.max(high[...], axis=1, keepdims=True)
        high[...] = jnp.broadcast_to(top, high.shape)

        def values(kb, carry):
            at = pl.multiple_of(kb * KB, KB)
            v = win[pl.ds(at, KB), LW:]
            for head in range(HL):
                rows = pl.ds(head * QB, QB)
                p = jnp.exp(sbuf[kb, rows, :] - high[rows, :1])
                low[rows, :] += p[:, :128] + p[:, 128:]
                acc[rows, :] += mm(p.astype(BF), v)
            return carry

        lax.fori_loop(first, end, values, 0)
        total = jnp.sum(low[...], axis=1, keepdims=True)
        inv = 1.0 / total
        out[pl.ds(block * QB, QB), :] = pick_heads(
            lambda head: acc[pl.ds(head * QB, QB), :] * inv[head * QB : (head + 1) * QB, :]
        ).astype(BF)
        flat = jnp.transpose(jnp.broadcast_to(top + jnp.log(total), (HL * QB, 128)))
        lt[pl.ds(block * 8, 8), :] = flat[:8, :]


def attend(starts, q, win):
    return call(
        attend_kernel,
        "attend",
        None,
        [starts, q, win],
        [((S, LW), BF), ((8 * (S // QB), HL * QB), F32)],
        [
            pltpu.VMEM((HL * QB, LW), BF),
            pltpu.VMEM((NB, HL * QB, KB), F32),
            pltpu.VMEM((HL * QB, 128), F32),
            pltpu.VMEM((HL * QB, 128), F32),
            pltpu.VMEM((HL * QB, LW), F32),
        ],
        0,
        specs=[SM, VM, VM],
    )


def attend_back_kernel(starts, q, win, grad, att, lt, dq, dwin, qm, gm, dqa, dkv):
    base = lax.axis_index("dp") * S
    dkv[...] = jnp.zeros_like(dkv)
    head_row = lax.broadcasted_iota(jnp.int32, (8, LW), 0)
    lane_head = lax.div(lax.broadcasted_iota(jnp.int32, (8, LW), 1), HEAD_DIM)
    sums = (head_row == lane_head).astype(F32)
    for block in range(S // QB):
        rows = pl.ds(block * QB, QB)
        spread_heads(q[rows, :].astype(F32) * 0.125, qm)
        grad_rows = grad[rows, :].astype(F32)
        spread_heads(grad_rows, gm)
        both = grad_rows * att[rows, :].astype(F32)
        by_head = lax.dot_general(
            sums,
            both,
            (((1,), (1,)), ((), ())),
            precision=lax.Precision.HIGHEST,
            preferred_element_type=F32,
        )
        inner = jnp.concatenate([by_head[h : h + 1, :] for h in range(HL)], axis=1)
        logs = lt[pl.ds(block * 8, 1), :]
        qid = ids_of(
            base + block * QB + lax.broadcasted_iota(jnp.int32, (1, QB), 1), starts
        )
        first, end = key_range(base, block, starts)
        dqa[...] = jnp.zeros_like(dqa)

        def one(kb, carry):
            at = pl.multiple_of(kb * KB, KB)
            keys = win[pl.ds(at, KB), :LW]
            vals = win[pl.ds(at, KB), LW:]
            kid = ids_of(base - OWN0 + at + lax.broadcasted_iota(jnp.int32, (KB, 1), 0), starts)
            bias = jnp.where(kid == qid, 0.0, NEG)
            st = mm_rt(keys, qm[...])
            dp = mm_rt(vals, gm[...])
            p = jnp.exp((st - logs) + jnp.concatenate([bias] * HL, axis=1))
            ds = (p * (dp - inner)).astype(BF)
            dkv[pl.ds(at, KB), LW:] += mm(p.astype(BF), gm[...])
            dkv[pl.ds(at, KB), :LW] += mm(ds, qm[...])
            dqa[...] += mm_lt(ds, keys)
            return carry

        lax.fori_loop(first, end, one, 0)
        dq[rows, :] = (pick_heads(lambda head: dqa[pl.ds(head * QB, QB), :]) * 0.125).astype(BF)
    dwin[...] = dkv[...].astype(BF)


def attend_back(starts, q, win, grad, att, lt):
    return call(
        attend_back_kernel,
        "attend_back",
        None,
        [starts, q, win, grad, att, lt],
        [((S, LW), BF), ((NW, 2 * LW), BF)],
        [
            pltpu.VMEM((HL * QB, LW), BF),
            pltpu.VMEM((HL * QB, LW), BF),
            pltpu.VMEM((HL * QB, LW), F32),
            pltpu.VMEM((NW, 2 * LW), F32),
        ],
        0,
        specs=[SM] + [VM] * 5,
    )


def outward_kernel(
    att, h, wp, sc, ob, gain, bias, w1, b1, w2,
    mixed, br1, br2, nxt, rows, act, slope,
    part, sa, ra, sb, rb, s3, r3, sa2, ra2, sb2, rb2, s32, r32, ss, rs,
):
    at = Place()
    wires = Wires(ss, rs)
    greet([{"tensor": at.mate}, {"tensor": at.cp}])
    scatter = Scatter(wires, at, part, sa, ra, sb, rb, s3, r3)
    part[...] = mm(att[pl.ds(at.far, 2 * R), :], wp[...])
    scatter.far()
    part[...] = mm(att[pl.ds(at.near, 2 * R), :], wp[...])
    scatter.near()
    one = scatter.total()
    br1[...] = one
    mix = h[...] + sc[0:1, :] * (one + ob[0:1, :])
    mixed[...] = mix
    x_hat, _ = normalized(mix)
    rows[pl.ds(at.own, R), :] = (x_hat * gain[...] + bias[...]).astype(BF)
    gather = Gather(wires, at, rows)

    def hidden(first):
        x = rows[pl.ds(first, 2 * R), :]
        for j in range(F // 256):
            cols = pl.ds(j * 256, 256)
            pre = mm(x, w1[:, cols]) + b1[:, cols]
            half = 0.5 * (1.0 + lax.erf(pre * (0.5**0.5)))
            act[pl.ds(first, 2 * R), cols] = (pre * half).astype(BF)
            bell = jnp.exp(-0.5 * pre * pre) * 0.3989422804014327
            slope[pl.ds(first, 2 * R), cols] = (half + pre * bell).astype(BF)

    gather.near()
    hidden(at.near)
    gather.far()
    hidden(at.far)
    scatter = Scatter(wires, at, part, sa2, ra2, sb2, rb2, s32, r32)
    part[...] = mm(act[pl.ds(at.far, 2 * R), :], w2[...])
    scatter.far()
    part[...] = mm(act[pl.ds(at.near, 2 * R), :], w2[...])
    scatter.near()
    two = scatter.total()
    br2[...] = two
    nxt[...] = mix + sc[1:2, :] * (two + ob[1:2, :])
    wires.close()


def outward(cid, att, h, wp, sc, ob, gain, bias, w1, b1, w2):
    one = ((R, D), F32)
    return call(
        outward_kernel,
        "outward%d" % cid,
        cid,
        [att, h, wp, sc, ob, gain, bias, w1, b1, w2],
        [one, one, one, one, ((S, D), BF), ((S, F), BF), ((S, F), BF)],
        scatter_scratch() + scatter_scratch()[1:],
        AG_SEMS + 2 * RS_SEMS,
    )


def back_out_kernel(
    g, sc, ob, gain, mixed, br1, br2, act, slope, rows, att, w1, w2, wp,
    gmix, gatt, dw2, dw1, dwp, vec, fb,
    g2, gp, g1, part, sa, ra, sb, rb, s3, r3, ss, rs,
):
    at = Place()
    wires = Wires(ss, rs)
    greet([{"tensor": at.mate}, {"tensor": at.cp}])
    grad = g[...]
    g2[pl.ds(at.own, R), :] = (grad * sc[1:2, :]).astype(BF)
    gather = Gather(wires, at, g2)
    vec[0:1, :] = jnp.sum(grad * (br2[...] + ob[1:2, :]), axis=0, keepdims=True)
    vec[1:2, :] = sc[1:2, :] * jnp.sum(grad, axis=0, keepdims=True)

    def hidden(first):
        x = g2[pl.ds(first, 2 * R), :]
        for j in range(F // 256):
            cols = pl.ds(j * 256, 256)
            up = mm_rt(x, w2[cols, :])
            gp[pl.ds(first, 2 * R), cols] = (
                up * slope[pl.ds(first, 2 * R), cols].astype(F32)
            ).astype(BF)

    gather.near()
    hidden(at.near)
    gather.far()
    hidden(at.far)
    scatter = Scatter(wires, at, part, sa, ra, sb, rb, s3, r3)
    part[...] = mm_rt(gp[pl.ds(at.far, 2 * R), :], w1[...])
    scatter.far()
    part[...] = mm_rt(gp[pl.ds(at.near, 2 * R), :], w1[...])
    scatter.near()
    for j in range(D // 256):
        cols = pl.ds(j * 256, 256)
        dw2[cols, :] = mm_lt(g2[:, cols], act[...]).astype(BF)
        dw1[cols, :] = mm_lt(rows[:, cols], gp[...]).astype(BF)
    fb[...] = jnp.broadcast_to(jnp.sum(gp[...].astype(F32), axis=0, keepdims=True), fb.shape)
    grad_in, grad_gain, grad_shift = norm_back(mixed[...], gain[...], scatter.total())
    mix = grad + grad_in
    gmix[...] = mix
    g1[pl.ds(at.own, R), :] = (mix * sc[0:1, :]).astype(BF)
    gather = Gather(wires, at, g1)
    vec[2:3, :] = grad_gain
    vec[3:4, :] = grad_shift
    vec[4:5, :] = jnp.sum(mix * (br1[...] + ob[0:1, :]), axis=0, keepdims=True)
    vec[5:6, :] = sc[0:1, :] * jnp.sum(mix, axis=0, keepdims=True)
    vec[6:8, :] = jnp.zeros((2, D), F32)
    gather.near()
    gatt[pl.ds(at.near, 2 * R), :] = mm_rt(g1[pl.ds(at.near, 2 * R), :], wp[...]).astype(BF)
    gather.far()
    gatt[pl.ds(at.far, 2 * R), :] = mm_rt(g1[pl.ds(at.far, 2 * R), :], wp[...]).astype(BF)
    dwp[...] = mm_lt(g1[...], att[...]).astype(BF)
    wires.close()


def back_out(cid, *ins):
    return call(
        back_out_kernel,
        "back_out%d" % cid,
        cid,
        list(ins),
        [
            ((R, D), F32), ((S, LW), BF), ((D, F), BF), ((D, F), BF), ((D, LW), BF),
            ((8, D), F32), ((8, F), F32),
        ],
        [pltpu.VMEM((S, D), BF), pltpu.VMEM((S, F), BF), pltpu.VMEM((S, D), BF)]
        + scatter_scratch(),
        2 * AG_SEMS + RS_SEMS,
    )


def back_in_kernel(
    dq, dwin, rows, w, gmix, h, gain,
    g, dw, vec, qb,
    proj, da, db, dc, ua, ub, uc, sdb, sdc, sub, suc, part, sa, ra, sb, rb, s3, r3, ss, rs,
):
    at = Place()
    wires = Wires(ss, rs)
    greet([{"tensor": at.mate}, {"tensor": at.cp}, {"dp": at.up}, {"dp": at.dn}])
    up, dn = {"dp": at.up}, {"dp": at.dn}
    cut = FAR3 - 256
    d1 = [
        wires.push(dwin.at[pl.ds(0, cut)], da.at[pl.ds(0, cut)], dn),
        wires.push(dwin.at[pl.ds(cut, 256)], da.at[pl.ds(cut, 256)], dn),
    ]
    top = NW - FAR3
    u1 = [
        wires.push(dwin.at[pl.ds(top, 256)], ua.at[pl.ds(0, 256)], up),
        wires.push(dwin.at[pl.ds(top + 256, cut)], ua.at[pl.ds(256, cut)], up),
    ]
    proj[:, :LW] = dq[...]
    dw[:, :LW] = mm_lt(rows[...], dq[...]).astype(BF)

    def plus(first, count, other):
        return (dwin[pl.ds(first, count), :].astype(F32) + other.astype(F32)).astype(BF)

    d2, u2 = [], []
    low2, high2 = FAR3, OWN0 + 2 * S
    d1[0].wait_recv()
    sdb[0 : 256 - cut, :] = dwin[pl.ds(low2, 256 - cut), :]
    sdb[256 - cut : 256, :] = plus(low2 + 256 - cut, cut, da[0:cut, :])
    d2.append(wires.push(sdb.at[pl.ds(0, 256)], db.at[pl.ds(0, 256)], dn))
    u1[0].wait_recv()
    sub[0:256, :] = plus(high2, 256, ua[0:256, :])
    u2.append(wires.push(sub.at[pl.ds(0, 256)], ub.at[pl.ds(0, 256)], up))
    d1[1].wait_recv()
    sdb[256:512, :] = plus(low2 + 256, 256, da[cut : cut + 256, :])
    d2.append(wires.push(sdb.at[pl.ds(256, 256)], db.at[pl.ds(256, 256)], dn))
    u1[1].wait_recv()
    sub[256 : 256 + cut, :] = plus(high2 + 256, cut, ua[256 : 256 + cut, :])
    sub[256 + cut : 512, :] = dwin[pl.ds(high2 + 256 + cut, 256 - cut), :]
    u2.append(wires.push(sub.at[pl.ds(256, 256)], ub.at[pl.ds(256, 256)], up))
    d3, u3 = [], []
    for k in range(2):
        half = pl.ds(256 * k, 256)
        d2[k].wait_recv()
        sdc[half, :] = plus(OWN0 - S + 256 * k, 256, db[half, :])
        d3.append(wires.push(sdc.at[half], dc.at[half], dn))
        u2[k].wait_recv()
        suc[half, :] = plus(OWN0 + S + 256 * k, 256, ub[half, :])
        u3.append(wires.push(suc.at[half], uc.at[half], up))
    for k in range(2):
        half = pl.ds(256 * k, 256)
        d3[k].wait_recv()
        u3[k].wait_recv()
        own = dwin[pl.ds(OWN0 + 256 * k, 256), :].astype(F32)
        proj[half, LW:] = (own + dc[half, :].astype(F32) + uc[half, :].astype(F32)).astype(BF)
    scatter = Scatter(wires, at, part, sa, ra, sb, rb, s3, r3)
    part[...] = mm_rt(proj[pl.ds(at.far, 2 * R), :], w[...])
    scatter.far()
    part[...] = mm_rt(proj[pl.ds(at.near, 2 * R), :], w[...])
    scatter.near()
    dw[:, LW:] = mm_lt(rows[...], proj[:, LW:]).astype(BF)
    qb[...] = jnp.broadcast_to(jnp.sum(proj[...].astype(F32), axis=0, keepdims=True), qb.shape)
    grad_in, grad_gain, grad_shift = norm_back(h[...], gain[...], scatter.total())
    g[...] = gmix[...] + grad_in
    vec[0:1, :] = grad_gain
    vec[1:2, :] = grad_shift
    vec[2:8, :] = jnp.zeros((6, D), F32)
    wires.close()


def back_in(cid, *ins):
    whole = pltpu.VMEM((S, 2 * LW), BF)
    three = pltpu.VMEM((FAR3, 2 * LW), BF)
    return call(
        back_in_kernel,
        "back_in%d" % cid,
        cid,
        list(ins),
        [((R, D), F32), ((D, 3 * LW), BF), ((8, D), F32), ((8, 3 * LW), F32)],
        [pltpu.VMEM((S, 3 * LW), BF), three, whole, whole, three, whole, whole]
        + [whole] * 4
        + scatter_scratch(),
        RS_SEMS + 12,
    )


class Ring:
    def __init__(self, wires, chunk, me, up, dn, bufs):
        self.wires, self.chunk, self.me, self.up, self.dn = wires, chunk, me, up, dn
        self.from_dn, self.from_up, self.send_up, self.send_dn, self.last_dn, self.last_up = bufs

    def half(self, ref, k):
        width = ref.shape[-1] // 2
        return ref.at[..., pl.ds(k * width, width)]

    def position(self, step):
        return lax.rem(self.me + step, 4)

    def start(self):
        push, chunk = self.wires.push, self.chunk
        p1, p2, p3 = self.position(1), self.position(2), self.position(3)
        self.a = push(chunk(p2, 0), self.from_dn, self.up)
        self.b = push(chunk(p2, 1), self.from_up, self.dn)
        self.c = push(chunk(p1, 1), self.half(self.last_dn, 1), self.up)
        self.d = push(chunk(p3, 0), self.half(self.last_up, 0), self.dn)

    def forward(self):
        push, chunk = self.wires.push, self.chunk
        p1, p3 = self.position(1), self.position(3)
        self.a.wait_recv()
        self.send_up[...] = (chunk(p1, 0)[...].astype(F32) + self.from_dn[...].astype(F32)).astype(
            BF
        )
        self.e = push(self.send_up, self.half(self.last_dn, 0), self.up)
        self.b.wait_recv()
        self.send_dn[...] = (chunk(p3, 1)[...].astype(F32) + self.from_up[...].astype(F32)).astype(
            BF
        )
        self.f = push(self.send_dn, self.half(self.last_up, 1), self.dn)

    def finish(self, out):
        for copy in (self.c, self.d, self.e, self.f):
            copy.wait_recv()
        for k in range(2):
            part = self.chunk(self.me, k)[...].astype(F32)
            part += self.half(self.last_dn, k)[...].astype(F32)
            part += self.half(self.last_up, k)[...].astype(F32)
            self.half(out, k)[...] = part.astype(out.dtype)


WIDTHS = (F, F, 3 * LW, LW)
MODES = (0, 1, 0, 1, 1, 0, 1, 0)


def ring_scratch(lead, width):
    half = pltpu.VMEM((*lead, width // 2), BF)
    full = pltpu.VMEM((*lead, width), BF)
    return [half, half, half, half, full, full]


PIECE_SCRATCH = 14


def piece_scratch(mode, width):
    lead = (4, 2, R // 4) if mode == 0 else (2, 4, R // 4)
    small = (2, R // 4)
    return (
        ring_scratch(lead, width)
        + [pltpu.VMEM((*lead, width), BF)]
        + ring_scratch(small, width)
        + [pltpu.VMEM((*small, width), BF)]
    )


def reduce_kernel(*refs):
    count = 2 * len(WIDTHS)
    ins, refs = refs[:count], refs[count:]
    va1, va0, vb1, vb0, fb1, fb0, qb1, qb0 = refs[:8]
    outs, vout = refs[8 : 8 + count], refs[8 + count]
    refs = refs[9 + count :]
    scratch = [refs[k * (PIECE_SCRATCH + 1) : (k + 1) * (PIECE_SCRATCH + 1)] for k in range(count)]
    vec, vmate, vcp, vy, vx, vz, ss, rs = refs[count * (PIECE_SCRATCH + 1) :]
    t = lax.axis_index("tensor")
    i = lax.axis_index("dp")
    y = lax.rem(i, 4)
    x = lax.div(i, 8)
    zh = lax.rem(lax.div(i, 4), 2)
    mate = {"tensor": t + 1 - 2 * lax.rem(t, 2)}
    cp = {"tensor": lax.rem(t + 2, 4)}
    along_y = [{"dp": i - y + lax.rem(y + k, 4)} for k in (1, 2, 3)]
    along_x = [{"dp": lax.rem(i + 8 * k, 32)} for k in (1, 2, 3)]
    beyond = {"dp": i + 4 - 8 * zh}
    greet([mate, cp, beyond] + along_y + along_x)
    wires = Wires(ss, rs)
    push = wires.push

    vec[...] = jnp.zeros_like(vec)
    for k, (va, vb) in enumerate(((va0, vb0), (va1, vb1))):
        vec[8 * k : 8 * k + 6, :] = va[0:6, :]
        vec[8 * k + 6 : 8 * k + 8, :] = vb[0:2, :]
    vec[16:17, :] = fb0[0:1, :]
    vec[17:18, :] = fb1[0:1, :]
    vec[18:19, : 3 * LW] = qb0[0:1, :]
    vec[19:20, : 3 * LW] = qb1[0:1, :]

    rings, second, rests = [], [], []
    for k in range(count):
        w, sc, mode = ins[k], scratch[k], MODES[k]
        width = w.shape[-1] // 2

        def wide(pos, half, w=w, mode=mode, width=width):
            cols = pl.ds(half * width, width)
            return w.at[:, :, pos, :, cols] if mode == 0 else w.at[pos, :, :, :, cols]

        def narrow(pos, half, acc=sc[6], mode=mode, width=width):
            cols = pl.ds(half * width, width)
            return acc.at[pos, :, :, cols] if mode == 0 else acc.at[:, pos, :, cols]

        ring_y = (y, along_y[0], along_y[2])
        ring_x = (x, along_x[0], along_x[2])
        one, two = (ring_y, ring_x) if mode == 0 else (ring_x, ring_y)
        rings.append(Ring(wires, wide, *one, sc[0:6]))
        second.append(Ring(wires, narrow, *two, sc[7:13]))

    to_mate = push(vec.at[pl.ds(0, 16)], vmate, mate)
    for ring in rings:
        ring.start()
    to_mate.wait_recv()
    wires.left(to_mate)
    vec[0:16, :] = vec[0:16, :] + vmate[...]
    to_cp = push(vec.at[pl.ds(0, 16)], vcp, cp)
    for ring in rings[:4]:
        ring.forward()
    to_cp.wait_recv()
    wires.left(to_cp)
    vy[y] = vec[...]
    vy[y, 0:16, :] = vec[0:16, :] + vcp[...]
    sent = [push(vy.at[y], vy.at[y], device) for device in along_y]
    for ring in rings[4:]:
        ring.forward()
    for k in range(4):
        rings[k].finish(scratch[k][6])
        second[k].start()
    for copy in sent:
        copy.wait_recv()
    vx[x] = vy[0] + vy[1] + vy[2] + vy[3]
    sent = [push(vx.at[x], vx.at[x], device) for device in along_x]
    for k in range(4, count):
        rings[k].finish(scratch[k][6])
        second[k].start()
    for ring in second:
        ring.forward()
    for copy in sent:
        copy.wait_recv()
    vec[...] = vx[0] + vx[1] + vx[2] + vx[3]
    to_z = push(vec, vz, beyond)
    rests = []
    for k in range(count):
        acc, rest = scratch[k][13], scratch[k][14]
        second[k].finish(acc)
        rests.append(push(acc.at[1 - zh], rest, beyond))
    to_z.wait_recv()
    vout[...] = vec[...] + vz[...]
    for k in range(count):
        acc, rest = scratch[k][13], scratch[k][14]
        rests[k].wait_recv()
        outs[k][...] = acc[zh].astype(F32) + rest[...].astype(F32)
    wires.close()


def reduce_all(cid, weights, vectors):
    ins = [w.reshape(4, 2, 4, R // 4, w.shape[-1]) for w in weights]
    widths = [w.shape[-1] for w in weights]
    scratch = []
    for width, mode in zip(widths, MODES):
        scratch += piece_scratch(mode, width) + [pltpu.VMEM((R // 4, width), BF)]
    rows = (24, D)
    scratch += [pltpu.VMEM(rows, F32), pltpu.VMEM((16, D), F32), pltpu.VMEM((16, D), F32)]
    scratch += [pltpu.VMEM((4, *rows), F32), pltpu.VMEM((4, *rows), F32), pltpu.VMEM(rows, F32)]
    return call(
        reduce_kernel,
        "reduce_all",
        cid,
        ins + list(vectors),
        [((R // 4, width), F32) for width in widths] + [(rows, F32)],
        scratch,
        13 * len(widths) + 9,
        limit=60,
    )


def shards(
    tokens_in,
    image_starts,
    norm_gain,
    norm_bias,
    qkv_weight,
    qv_bias,
    proj_weight,
    out_bias,
    layer_scale,
    fc1_weight,
    fc1_bias,
    fc2_weight,
    out_grad,
):
    layers = qkv_weight.shape[0]
    hidden = tokens_in.astype(F32)
    saved = []
    for l in range(layers):
        w_qkv = qkv_weight[l].reshape(D, 3 * LW)
        b3 = jnp.concatenate([qv_bias[l, 0], jnp.zeros((LW,), F32), qv_bias[l, 1]])[None]
        rows_one, q, win = inward(
            2 * l, hidden, norm_gain[l, 0:1], norm_bias[l, 0:1], b3, w_qkv
        )
        att, lt = attend(image_starts, q, win)
        mixed, br1, br2, nxt, rows_two, act, slope = outward(
            2 * l + 1, att, hidden, proj_weight[l], layer_scale[l], out_bias[l],
            norm_gain[l, 1:2], norm_bias[l, 1:2], fc1_weight[l], fc1_bias[l : l + 1],
            fc2_weight[l],
        )
        saved.append((w_qkv, rows_one, q, win, att, lt, hidden, mixed, br1, br2, rows_two, act, slope))
        hidden = nxt
    grad = out_grad
    weights, va, vb, fbs, qbs = [], [], [], [], []
    for l in reversed(range(layers)):
        w_qkv, rows_one, q, win, att, lt, h, mixed, br1, br2, rows_two, act, slope = saved[l]
        gmix, gatt, dw2, dw1, dwp, vec_a, fb = back_out(
            4 + 2 * l, grad, layer_scale[l], out_bias[l], norm_gain[l, 1:2], mixed, br1, br2,
            act, slope, rows_two, att, fc1_weight[l], fc2_weight[l], proj_weight[l],
        )
        dq, dwin = attend_back(image_starts, q, win, gatt, att, lt)
        grad, dwq, vec_b, qb = back_in(
            5 + 2 * l, dq, dwin, rows_one, w_qkv, gmix, h, norm_gain[l, 0:1]
        )
        weights += [dw2, dw1, dwq, dwp]
        va.append(vec_a)
        vb.append(vec_b)
        fbs.append(fb)
        qbs.append(qb)
    *sums, vec = reduce_all(8, weights, va + vb + fbs + qbs)
    g2_1, g1_1, gq_1, gp_1, g2_0, g1_0, gq_0, gp_0 = sums
    rows = vec[:16].reshape(2, 8, D)
    return (
        hidden.astype(BF),
        grad,
        jnp.stack([rows[:, 6], rows[:, 2]], 1),
        jnp.stack([rows[:, 7], rows[:, 3]], 1),
        jnp.stack([gq_0, gq_1]).reshape(2, R // 4, 3, LW),
        jnp.stack([vec[18:20, :LW], vec[18:20, 2 * LW : 3 * LW]], 1),
        jnp.stack([gp_0.T, gp_1.T]),
        jnp.stack([rows[:, 5], rows[:, 1]], 1),
        jnp.stack([rows[:, 4], rows[:, 0]], 1),
        jnp.stack([g1_0, g1_1]),
        vec[16:18],
        jnp.stack([g2_0.T, g2_1.T]),
    )


def solution(mesh):
    return jax.shard_map(
        shards,
        mesh=mesh,
        in_specs=(
            P(("dp", "tensor"), None),
            P(),
            P(),
            P(),
            P(None, None, None, "tensor"),
            P(None, None, "tensor"),
            P(None, "tensor", None),
            P(),
            P(),
            P(None, None, "tensor"),
            P(None, "tensor"),
            P(None, "tensor", None),
            P(("dp", "tensor"), None),
        ),
        out_specs=(
            P(("dp", "tensor"), None),
            P(("dp", "tensor"), None),
            P(),
            P(),
            P(None, "dp", None, "tensor"),
            P(None, None, "tensor"),
            P(None, "tensor", "dp"),
            P(),
            P(),
            P(None, "dp", "tensor"),
            P(None, "tensor"),
            P(None, "tensor", "dp"),
        ),
        check_vma=False,
    )
```

```python
import functools

import jax
import jax.numpy as jnp
from jax import lax
from jax.experimental import pallas as pl
from jax.experimental.pallas import tpu as pltpu
from jax.sharding import PartitionSpec as P

MESH = pl.DeviceIdType.MESH
BF = jnp.bfloat16
F32 = jnp.float32
VM = pl.BlockSpec(memory_space=pltpu.VMEM)
SM = pl.BlockSpec(memory_space=pltpu.SMEM)
ANY = pl.BlockSpec(memory_space=pl.ANY)

HEAD_DIM = 64
IMG_LEN = 1370
EPS = 1e-06
NEG = -1e30

R = 128
S = 512
D = 1024
LW = 256
HL = LW // HEAD_DIM
F = 1024
TOTAL = 16384
NDP = 32
FAR3 = 384
OWN0 = FAR3 + 2 * S
NW = 2 * OWN0 + S
QB = 256
KB = 256
NB = NW // KB
C = 2
RC = R // C
MB = 1 << 20


def mm(a, b):
    return jnp.dot(a, b, preferred_element_type=F32)


def mm_rt(a, b):
    return lax.dot_general(a, b, (((1,), (1,)), ((), ())), preferred_element_type=F32)


def mm_lt(a, b):
    return lax.dot_general(a, b, (((0,), (0,)), ((), ())), preferred_element_type=F32)


class Place:
    def __init__(self):
        self.t = lax.axis_index("tensor")
        self.core = lax.rem(self.t, 2)
        self.mate = self.t + 1 - 2 * self.core
        self.cp = lax.rem(self.t + 2, 4)
        self.own = pl.multiple_of(self.t * R, R)
        self.opp = pl.multiple_of(self.cp * R, R)
        self.near = pl.multiple_of((self.t - self.core) * R, 2 * R)
        self.far = pl.multiple_of(2 * R - self.near, 2 * R)
        self.dp = lax.axis_index("dp")
        self.up = lax.rem(self.dp + 1, NDP)
        self.dn = lax.rem(self.dp + NDP - 1, NDP)


def greet(devices):
    barrier = pltpu.get_barrier_semaphore()
    for device in devices:
        pl.semaphore_signal(barrier, inc=1, device_id=device, device_id_type=MESH)
    pl.semaphore_wait(barrier, len(devices))


class Wires:
    def __init__(self, send, recv):
        self.send, self.recv, self.count, self.open = send, recv, 0, []

    def push(self, src, dst, device):
        k = self.count
        self.count += 1
        copy = pltpu.make_async_remote_copy(
            src, dst, self.send.at[k], self.recv.at[k], device_id=device, device_id_type=MESH
        )
        copy.start()
        self.open.append(copy)
        return copy

    def left(self, copy):
        copy.wait_send()
        self.open = [c for c in self.open if c is not copy]

    def close(self):
        for copy in self.open:
            copy.wait_send()


class Chain:
    def __init__(self, wires, at, up, relay):
        self.wires, self.at, self.relay = wires, at, relay
        y = lax.rem(at.dp, 4)
        self.edge = (y == 3) if up else (y == 0)
        self.plain = jnp.logical_not(self.edge)
        self.device = at.up if up else at.dn
        self.items = []

    def send(self, src, dst, partner_dst=None, when=True, partner_when=True):
        wires, at = self.wires, self.at
        slot = self.relay.at[len(self.items)]
        k = wires.count
        wires.count += 2

        def copy(source, target, n, device):
            return lambda: pltpu.make_async_remote_copy(
                source, target, wires.send.at[n], wires.recv.at[n],
                device_id=device, device_id_type=MESH,
            )

        direct = copy(src, dst, k, {"dp": self.device})
        first = copy(src, slot, k + 1, {"tensor": at.cp})
        target = dst if partner_dst is None else partner_dst
        second = copy(slot, target, k, {"dp": self.device, "tensor": at.cp})
        pl.when(self.plain & when)(lambda: direct().start())
        pl.when(self.edge & when)(lambda: first().start())
        item = (direct, first, second, when, partner_when)
        self.items.append(item)
        return item

    def hand_on(self, item):
        _, first, second, _, partner_when = item

        @pl.when(self.edge & partner_when)
        def _():
            first().wait_recv()
            second().start()

    def arrive(self, item):
        pl.when(item[3])(lambda: item[0]().wait_recv())

    def close(self):
        for direct, first, second, when, partner_when in self.items:
            pl.when(self.plain & when)(lambda c=direct: c().wait_send())
            pl.when(self.edge & when)(lambda c=first: c().wait_send())
            pl.when(self.edge & partner_when)(lambda c=second: c().wait_send())


class Line:
    def __init__(self, wires, device):
        self.wires, self.device = wires, device

    def send(self, src, dst):
        return self.wires.push(src, dst, self.device)

    def arrive(self, copy):
        copy.wait_recv()


def chain_partners(at):
    return [
        {"tensor": at.mate},
        {"tensor": at.cp},
        {"dp": at.up},
        {"dp": at.dn},
        {"dp": at.up, "tensor": at.cp},
        {"dp": at.dn, "tensor": at.cp},
    ]


AG_SEMS = 2 * C + 1
RS_SEMS = 2 * C + 1


class Gather:
    def __init__(self, wires, at, buf):
        self.wires, self.at, self.buf = wires, at, buf
        own = at.own
        self.across = []
        for c in range(C):
            part = buf.at[pl.ds(own + c * RC, RC)]
            self.across.append(wires.push(part, part, {"tensor": at.cp}))
        part = buf.at[pl.ds(own, R)]
        self.beside = wires.push(part, part, {"tensor": at.mate})

    def near(self):
        self.beside.wait_recv()

    def far(self):
        passed = []
        for c in range(C):
            self.across[c].wait_recv()
            part = self.buf.at[pl.ds(self.at.opp + c * RC, RC)]
            passed.append(self.wires.push(part, part, {"tensor": self.at.mate}))
        for copy in passed:
            copy.wait_recv()


class Scatter:
    def __init__(self, wires, at, part, send1, recv1, send2, recv2, send3, recv3):
        self.wires, self.at, self.part = wires, at, part
        self.send1, self.recv1 = send1, recv1
        self.send2, self.recv2 = send2, recv2
        self.send3, self.recv3 = send3, recv3

    def far(self):
        at, wires = self.at, self.wires
        first = []
        for c in range(C):
            rows = pl.ds(c * RC, RC)
            src = pl.ds(pl.multiple_of((1 - at.core) * R + c * RC, RC), RC)
            self.send1[rows, :] = self.part[src, :].astype(BF)
            first.append(wires.push(self.send1.at[rows], self.recv1.at[rows], {"tensor": at.mate}))
        self.second = []
        for c in range(C):
            rows = pl.ds(c * RC, RC)
            src = pl.ds(pl.multiple_of(at.core * R + c * RC, RC), RC)
            first[c].wait_recv()
            total = self.part[src, :] + self.recv1[rows, :].astype(F32)
            self.send2[rows, :] = total.astype(BF)
            self.second.append(
                wires.push(self.send2.at[rows], self.recv2.at[rows], {"tensor": at.cp})
            )

    def near(self):
        at = self.at
        src = pl.ds(pl.multiple_of((1 - at.core) * R, R), R)
        self.send3[...] = self.part[src, :].astype(BF)
        self.third = self.wires.push(self.send3, self.recv3, {"tensor": at.mate})

    def total(self):
        self.third.wait_recv()
        for copy in self.second:
            copy.wait_recv()
        own = self.part[pl.ds(pl.multiple_of(self.at.core * R, R), R), :]
        return own + self.recv3[...].astype(F32) + self.recv2[...].astype(F32)


def scatter_scratch():
    return [pltpu.VMEM((2 * R, D), F32)] + [pltpu.VMEM((R, D), BF) for _ in range(6)]


def fetch(src, dst, sem):
    copy = pltpu.make_async_copy(src, dst, sem)
    copy.start()
    return copy


def fetch_qkv(layer, w, buf, ls):
    return [
        fetch(w.at[layer, k], buf.at[:, pl.ds(k * LW, LW)], ls.at[k]) for k in range(3)
    ]


def normalized(v):
    centered = v - jnp.mean(v, axis=-1, keepdims=True)
    scale = lax.rsqrt(jnp.mean(centered * centered, axis=-1, keepdims=True) + EPS)
    return centered * scale, scale


def norm_back(v, gain, grad):
    x_hat, scale = normalized(v)
    u = grad * gain
    grad_in = scale * (
        u
        - jnp.mean(u, axis=-1, keepdims=True)
        - x_hat * jnp.mean(u * x_hat, axis=-1, keepdims=True)
    )
    return (
        grad_in,
        jnp.sum(grad * x_hat, axis=0, keepdims=True),
        jnp.sum(grad, axis=0, keepdims=True),
    )


def call(kernel, name, cid, ins, outs, scratch, sems, limit, specs=None, local=0, out_specs=None):
    shapes = [jax.ShapeDtypeStruct(shape, dtype) for shape, dtype in outs]
    extra = []
    if sems:
        extra = [pltpu.SemaphoreType.DMA((sems,)), pltpu.SemaphoreType.DMA((sems,))]
    if local:
        extra.append(pltpu.SemaphoreType.DMA((local,)))
    params = dict(vmem_limit_bytes=limit * MB)
    if cid is not None:
        params.update(collective_id=cid, has_side_effects=True)
    return pl.pallas_call(
        kernel,
        out_shape=shapes,
        in_specs=specs or [VM] * len(ins),
        out_specs=out_specs or [VM] * len(outs),
        scratch_shapes=list(scratch) + extra,
        compiler_params=pltpu.CompilerParams(**params),
        name=name,
    )(*ins)


def inward_kernel(layer, h, gain, bias, b2, w_hbm, rows, q, win, w, relay, ss, rs, ls):
    at = Place()
    wires = Wires(ss, rs)
    loads = fetch_qkv(layer, w_hbm, w, ls)
    x_hat, _ = normalized(h[...].astype(F32))
    mine = (x_hat * gain[layer, 0:1, :] + bias[layer, 0:1, :]).astype(BF)
    greet(chain_partners(at))
    rows[pl.ds(at.own, R), :] = mine
    gather = Gather(wires, at, rows)

    def project(first):
        out = mm(rows[pl.ds(first, 2 * R), :], w[...])
        q[pl.ds(first, 2 * R), :] = (out[:, :LW] + b2[layer, 0:1, :]).astype(BF)
        win[pl.ds(OWN0 + first, 2 * R), :LW] = out[:, LW : 2 * LW].astype(BF)
        win[pl.ds(OWN0 + first, 2 * R), LW:] = (out[:, 2 * LW :] + b2[layer, 1:2, :]).astype(BF)

    def part(first):
        return win.at[pl.ds(pl.multiple_of(first, R), R)]

    offs = [at.near, at.near + R, at.far, at.far + R]
    others = offs[2:] + offs[:2]
    chain_up, chain_dn = Chain(wires, at, True, relay), Chain(wires, at, False, relay)
    ups, dns = {}, {}

    def hop(n, k):
        own, other = offs[k], others[k]
        low, high = OWN0 - n * S, OWN0 + n * S
        if n < 3:
            ups[n, k] = chain_up.send(part(low + S + own), part(low + own), part(low + other))
            dns[n, k] = chain_dn.send(part(high - S + own), part(high + own), part(high + other))
            return
        ups[n, k] = chain_up.send(
            part(low + S + own),
            part(jnp.maximum(low + own, 0)),
            part(jnp.maximum(low + other, 0)),
            own > 0,
            other > 0,
        )
        dns[n, k] = chain_dn.send(
            part(high - S + own),
            part(jnp.minimum(high + own, NW - R)),
            part(jnp.minimum(high + other, NW - R)),
            own < S - R,
            other < S - R,
        )

    def onward(n, *ks):
        for k in ks:
            chain_up.arrive(ups[n, k])
            chain_dn.arrive(dns[n, k])
            if n < 3:
                hop(n + 1, k)

    def hand_on(n, *ks):
        for k in ks:
            chain_up.hand_on(ups[n, k])
            chain_dn.hand_on(dns[n, k])

    for copy in loads:
        copy.wait()
    gather.near()
    project(at.near)
    hop(1, 0)
    hop(1, 1)
    gather.far()
    hand_on(1, 0, 1)
    project(at.far)
    hop(1, 2)
    hop(1, 3)
    onward(1, 0, 1)
    hand_on(1, 2, 3)
    hand_on(2, 0, 1)
    onward(1, 2, 3)
    onward(2, 0, 1)
    hand_on(2, 2, 3)
    hand_on(3, 0, 1)
    onward(2, 2, 3)
    hand_on(3, 2, 3)
    onward(3, 0, 1, 2, 3)
    chain_up.close()
    chain_dn.close()
    wires.close()


def inward(cid, layer, h, gain, bias, b2, w):
    return call(
        functools.partial(inward_kernel, layer),
        "inward%d" % layer,
        cid,
        [h, gain, bias, b2, w],
        [((S, D), BF), ((S, LW), BF), ((NW, 2 * LW), BF)],
        [pltpu.VMEM((D, 3 * LW), BF), pltpu.VMEM((12, R, 2 * LW), BF)],
        AG_SEMS + 48,
        limit=20,
        specs=[VM] * 4 + [ANY],
        local=3,
    )


def ids_of(position, starts):
    total = jnp.zeros_like(position)
    for k in range(starts.shape[0]):
        first = starts[k]
        total += (position >= first).astype(jnp.int32)
        total += (position >= first + IMG_LEN).astype(jnp.int32)
    return jnp.where((position >= 0) & (position < TOTAL), total, -1)


def key_range(base, block, starts):
    first = base + block * QB
    last = first + QB - 1
    low, high = jnp.int32(0), jnp.int32(TOTAL)
    for k in range(starts.shape[0]):
        for edge in (starts[k], starts[k] + IMG_LEN):
            low = jnp.where(edge <= first, jnp.maximum(low, edge), low)
            high = jnp.where(edge > last, jnp.minimum(high, edge), high)
    low_block = lax.div(jnp.maximum(low - base + OWN0, 0), KB)
    high_block = lax.div(jnp.minimum(high - base + OWN0, NW) + KB - 1, KB)
    return low_block, high_block


def spread_heads(value, out):
    lane = lax.broadcasted_iota(jnp.int32, (QB, LW), 1)
    for head in range(HL):
        mine = (lane >= head * HEAD_DIM) & (lane < (head + 1) * HEAD_DIM)
        out[pl.ds(head * QB, QB), :] = jnp.where(mine, value, 0.0).astype(BF)


def pick_heads(parts):
    lane = lax.broadcasted_iota(jnp.int32, (QB, LW), 1)
    out = parts(0)
    for head in range(1, HL):
        out = jnp.where(lane >= head * HEAD_DIM, parts(head), out)
    return out


def attend_kernel(starts, q, win, out, lt, qm, sbuf, high, low, acc):
    base = lax.axis_index("dp") * S
    for block in range(S // QB):
        spread_heads(q[pl.ds(block * QB, QB), :].astype(F32) * 0.125, qm)
        qid = ids_of(
            base + block * QB + lax.broadcasted_iota(jnp.int32, (QB, 1), 0), starts
        )
        first, end = key_range(base, block, starts)
        high[...] = jnp.full_like(high, NEG)
        low[...] = jnp.zeros_like(low)
        acc[...] = jnp.zeros_like(acc)

        def scores(kb, carry):
            at = pl.multiple_of(kb * KB, KB)
            s = mm_rt(qm[...], win[pl.ds(at, KB), :LW])
            kid = ids_of(base - OWN0 + at + lax.broadcasted_iota(jnp.int32, (1, KB), 1), starts)
            bias = jnp.where(qid == kid, 0.0, NEG)
            for head in range(HL):
                rows = pl.ds(head * QB, QB)
                one = s[head * QB : (head + 1) * QB, :] + bias
                sbuf[kb, rows, :] = one
                high[rows, :] = jnp.maximum(
                    high[rows, :], jnp.maximum(one[:, :128], one[:, 128:])
                )
            return carry

        lax.fori_loop(first, end, scores, 0)
        top = jnp.max(high[...], axis=1, keepdims=True)
        high[...] = jnp.broadcast_to(top, high.shape)

        def values(kb, carry):
            at = pl.multiple_of(kb * KB, KB)
            v = win[pl.ds(at, KB), LW:]
            for head in range(HL):
                rows = pl.ds(head * QB, QB)
                p = jnp.exp(sbuf[kb, rows, :] - high[rows, :1])
                low[rows, :] += p[:, :128] + p[:, 128:]
                acc[rows, :] += mm(p.astype(BF), v)
            return carry

        lax.fori_loop(first, end, values, 0)
        total = jnp.sum(low[...], axis=1, keepdims=True)
        inv = 1.0 / total
        out[pl.ds(block * QB, QB), :] = pick_heads(
            lambda head: acc[pl.ds(head * QB, QB), :] * inv[head * QB : (head + 1) * QB, :]
        ).astype(BF)
        flat = jnp.transpose(jnp.broadcast_to(top + jnp.log(total), (HL * QB, 128)))
        lt[pl.ds(block * 8, 8), :] = flat[:8, :]


def attend(starts, q, win):
    return call(
        attend_kernel,
        "attend",
        None,
        [starts, q, win],
        [((S, LW), BF), ((8 * (S // QB), HL * QB), F32)],
        [
            pltpu.VMEM((HL * QB, LW), BF),
            pltpu.VMEM((NB, HL * QB, KB), F32),
            pltpu.VMEM((HL * QB, 128), F32),
            pltpu.VMEM((HL * QB, 128), F32),
            pltpu.VMEM((HL * QB, LW), F32),
        ],
        0,
        limit=30,
        specs=[SM, VM, VM],
    )


def attend_back_kernel(starts, q, win, grad, att, lt, dq, dwin, qm, gm, dqa, dkv):
    base = lax.axis_index("dp") * S
    dkv[...] = jnp.zeros_like(dkv)
    head_row = lax.broadcasted_iota(jnp.int32, (8, LW), 0)
    lane_head = lax.div(lax.broadcasted_iota(jnp.int32, (8, LW), 1), HEAD_DIM)
    sums = (head_row == lane_head).astype(F32)
    for block in range(S // QB):
        rows = pl.ds(block * QB, QB)
        spread_heads(q[rows, :].astype(F32) * 0.125, qm)
        grad_rows = grad[rows, :].astype(F32)
        spread_heads(grad_rows, gm)
        both = grad_rows * att[rows, :].astype(F32)
        by_head = lax.dot_general(
            sums,
            both,
            (((1,), (1,)), ((), ())),
            precision=lax.Precision.HIGHEST,
            preferred_element_type=F32,
        )
        inner = jnp.concatenate([by_head[h : h + 1, :] for h in range(HL)], axis=1)
        logs = lt[pl.ds(block * 8, 1), :]
        qid = ids_of(
            base + block * QB + lax.broadcasted_iota(jnp.int32, (1, QB), 1), starts
        )
        first, end = key_range(base, block, starts)
        dqa[...] = jnp.zeros_like(dqa)

        def one(kb, carry):
            at = pl.multiple_of(kb * KB, KB)
            keys = win[pl.ds(at, KB), :LW]
            vals = win[pl.ds(at, KB), LW:]
            kid = ids_of(base - OWN0 + at + lax.broadcasted_iota(jnp.int32, (KB, 1), 0), starts)
            bias = jnp.where(kid == qid, 0.0, NEG)
            st = mm_rt(keys, qm[...])
            dp = mm_rt(vals, gm[...])
            p = jnp.exp((st - logs) + jnp.concatenate([bias] * HL, axis=1))
            ds = (p * (dp - inner)).astype(BF)
            dkv[pl.ds(at, KB), LW:] += mm(p.astype(BF), gm[...])
            dkv[pl.ds(at, KB), :LW] += mm(ds, qm[...])
            dqa[...] += mm_lt(ds, keys)
            return carry

        lax.fori_loop(first, end, one, 0)
        dq[rows, :] = (pick_heads(lambda head: dqa[pl.ds(head * QB, QB), :]) * 0.125).astype(BF)
    dwin[...] = dkv[...].astype(BF)


def attend_back(starts, q, win, grad, att, lt):
    return call(
        attend_back_kernel,
        "attend_back",
        None,
        [starts, q, win, grad, att, lt],
        [((S, LW), BF), ((NW, 2 * LW), BF)],
        [
            pltpu.VMEM((HL * QB, LW), BF),
            pltpu.VMEM((HL * QB, LW), BF),
            pltpu.VMEM((HL * QB, LW), F32),
            pltpu.VMEM((NW, 2 * LW), F32),
        ],
        0,
        limit=28,
        specs=[SM] + [VM] * 5,
    )


def outward_kernel(
    layer, att, h, sc, ob, gain, bias, b1, wp_hbm, w1_hbm, w2_hbm,
    mixed, br1, br2, nxt, rows, act, slope,
    wp, w1, w2, part, sa, ra, sb, rb, s3, r3, sa2, ra2, sb2, rb2, s32, r32, ss, rs, ls,
):
    at = Place()
    wires = Wires(ss, rs)
    load_p = fetch(wp_hbm.at[layer], wp, ls.at[0])
    load_1 = fetch(w1_hbm.at[layer], w1, ls.at[1])
    load_2 = fetch(w2_hbm.at[layer], w2, ls.at[2])
    greet([{"tensor": at.mate}, {"tensor": at.cp}])
    scatter = Scatter(wires, at, part, sa, ra, sb, rb, s3, r3)
    load_p.wait()
    part[...] = mm(att[pl.ds(at.far, 2 * R), :], wp[...])
    scatter.far()
    part[...] = mm(att[pl.ds(at.near, 2 * R), :], wp[...])
    scatter.near()
    one = scatter.total()
    br1[...] = one
    mix = h[...].astype(F32) + sc[layer, 0:1, :] * (one + ob[layer, 0:1, :])
    mixed[...] = mix
    x_hat, _ = normalized(mix)
    rows[pl.ds(at.own, R), :] = (x_hat * gain[layer, 1:2, :] + bias[layer, 1:2, :]).astype(BF)
    gather = Gather(wires, at, rows)

    def hidden(first):
        x = rows[pl.ds(first, 2 * R), :]
        for j in range(F // 256):
            cols = pl.ds(j * 256, 256)
            pre = mm(x, w1[:, cols]) + b1[layer : layer + 1, cols]
            half = 0.5 * (1.0 + lax.erf(pre * (0.5**0.5)))
            act[pl.ds(first, 2 * R), cols] = (pre * half).astype(BF)
            bell = jnp.exp(-0.5 * pre * pre) * 0.3989422804014327
            slope[pl.ds(first, 2 * R), cols] = (half + pre * bell).astype(BF)

    load_1.wait()
    gather.near()
    hidden(at.near)
    gather.far()
    hidden(at.far)
    load_2.wait()
    scatter = Scatter(wires, at, part, sa2, ra2, sb2, rb2, s32, r32)
    part[...] = mm(act[pl.ds(at.far, 2 * R), :], w2[...])
    scatter.far()
    part[...] = mm(act[pl.ds(at.near, 2 * R), :], w2[...])
    scatter.near()
    two = scatter.total()
    br2[...] = two
    nxt[...] = (mix + sc[layer, 1:2, :] * (two + ob[layer, 1:2, :])).astype(nxt.dtype)
    wires.close()


def outward(cid, layer, last, *ins):
    one = ((R, D), F32)
    return call(
        functools.partial(outward_kernel, layer),
        "outward%d" % layer,
        cid,
        list(ins),
        [one, one, one, ((R, D), last), ((S, D), BF), ((S, F), BF), ((S, F), BF)],
        [pltpu.VMEM((LW, D), BF), pltpu.VMEM((D, F), BF), pltpu.VMEM((F, D), BF)]
        + scatter_scratch()
        + scatter_scratch()[1:],
        AG_SEMS + 2 * RS_SEMS,
        limit=28,
        specs=[VM] * 7 + [ANY] * 3,
        local=3,
    )


def back_out_kernel(layer, carry, *refs):
    g, sc, ob, gain, mixed, br1, br2, act, slope, rows, att, w1_hbm, w2_hbm, wp_hbm = refs[:14]
    refs = refs[14:]
    given, refs = refs[: 3 * carry], refs[3 * carry :]
    gmix, gatt, dw2_hbm, dw1_hbm, dwp, vec, fb = refs[:7]
    refs = refs[7:]
    sums, refs = refs[: NP * carry], refs[NP * carry :]
    wp, w1, w2, dw2, dw1, g2, gp, g1, part, sa, ra, sb, rb, s3, r3 = refs[:15]
    bufs = refs[15:-3]
    ss, rs, ls = refs[-3:]
    at = Place()
    wires = Wires(ss, rs)
    load_2 = fetch(w2_hbm.at[layer], w2, ls.at[0])
    load_1 = fetch(w1_hbm.at[layer], w1, ls.at[1])
    load_p = fetch(wp_hbm.at[layer], wp, ls.at[2])
    rings = Rings()
    wide = Wide(wires, rings, given, bufs, ls, 5) if carry else None
    greet([{"tensor": at.mate}, {"tensor": at.cp}] + rings.next_to() * carry)
    grad = g[...]
    g2[pl.ds(at.own, R), :] = (grad * sc[layer, 1:2, :]).astype(BF)
    gather = Gather(wires, at, g2)
    if carry:
        wide.start(*range(NP))
    vec[0:1, :] = jnp.sum(grad * (br2[...] + ob[layer, 1:2, :]), axis=0, keepdims=True)
    vec[1:2, :] = sc[layer, 1:2, :] * jnp.sum(grad, axis=0, keepdims=True)

    def hidden(first):
        x = g2[pl.ds(first, 2 * R), :]
        for j in range(F // 256):
            cols = pl.ds(j * 256, 256)
            up = mm_rt(x, w2[cols, :])
            gp[pl.ds(first, 2 * R), cols] = (
                up * slope[pl.ds(first, 2 * R), cols].astype(F32)
            ).astype(BF)

    load_2.wait()
    gather.near()
    hidden(at.near)
    gather.far()
    hidden(at.far)
    load_1.wait()
    scatter = Scatter(wires, at, part, sa, ra, sb, rb, s3, r3)
    part[...] = mm_rt(gp[pl.ds(at.far, 2 * R), :], w1[...])
    scatter.far()
    part[...] = mm_rt(gp[pl.ds(at.near, 2 * R), :], w1[...])
    scatter.near()
    if carry:
        wide.forward(*range(NP))
    for j in range(D // 256):
        cols = pl.ds(j * 256, 256)
        dw2[cols, :] = mm_lt(g2[:, cols], act[...]).astype(BF)
    write_2 = fetch(dw2, dw2_hbm, ls.at[3])
    for j in range(D // 256):
        cols = pl.ds(j * 256, 256)
        dw1[cols, :] = mm_lt(rows[:, cols], gp[...]).astype(BF)
    write_1 = fetch(dw1, dw1_hbm, ls.at[4])
    fb[...] = jnp.broadcast_to(jnp.sum(gp[...].astype(F32), axis=0, keepdims=True), fb.shape)
    grad_in, grad_gain, grad_shift = norm_back(
        mixed[...], gain[layer, 1:2, :], scatter.total()
    )
    mix = grad + grad_in
    gmix[...] = mix
    g1[pl.ds(at.own, R), :] = (mix * sc[layer, 0:1, :]).astype(BF)
    gather = Gather(wires, at, g1)
    vec[2:3, :] = grad_gain
    vec[3:4, :] = grad_shift
    vec[4:5, :] = jnp.sum(mix * (br1[...] + ob[layer, 0:1, :]), axis=0, keepdims=True)
    vec[5:6, :] = sc[layer, 0:1, :] * jnp.sum(mix, axis=0, keepdims=True)
    vec[6:8, :] = jnp.zeros((2, D), F32)
    load_p.wait()
    gather.near()
    gatt[pl.ds(at.near, 2 * R), :] = mm_rt(g1[pl.ds(at.near, 2 * R), :], wp[...]).astype(BF)
    gather.far()
    gatt[pl.ds(at.far, 2 * R), :] = mm_rt(g1[pl.ds(at.far, 2 * R), :], wp[...]).astype(BF)
    dwp[...] = mm_lt(g1[...], att[...]).astype(BF)
    if carry:
        wide.finish(sums, *range(NP))
    write_2.wait()
    write_1.wait()
    wires.close()


def back_out(cid, layer, given, *ins):
    carry = int(bool(given))
    return call(
        functools.partial(back_out_kernel, layer, carry),
        "back_out%d" % layer,
        cid,
        [*ins, *given],
        [
            ((R, D), F32), ((S, LW), BF), ((D, F), BF), ((D, F), BF), ((D, LW), BF),
            ((8, D), F32), ((8, F), F32),
        ]
        + [wide_shape(width, mode) for _, _, width, mode in PIECES] * carry,
        [pltpu.VMEM((LW, D), BF), pltpu.VMEM((D, F), BF), pltpu.VMEM((F, D), BF)]
        + [pltpu.VMEM((D, F), BF), pltpu.VMEM((D, F), BF)]
        + [pltpu.VMEM((S, D), BF), pltpu.VMEM((S, F), BF), pltpu.VMEM((S, D), BF)]
        + scatter_scratch()
        + wide_scratch() * carry,
        2 * AG_SEMS + RS_SEMS + carry * 6 * NP,
        limit=30 + 20 * carry,
        specs=[VM] * 11 + [ANY] * (3 + 3 * carry),
        out_specs=[VM, VM, ANY, ANY, VM, VM, VM] + [VM] * (carry * NP),
        local=5 + carry * 3 * NP,
    )


def back_in_kernel(layer, last, *refs):
    dq, dwin, rows, gmix, h, gain, dwp, w_hbm = refs[:8]
    refs = refs[8:]
    if last:
        dw2, dw1 = refs[:2]
        accs1 = refs[2 : 2 + NP]
        va1, va0, vb1, fb1, fb0, qb1 = refs[2 + NP : 8 + NP]
        refs = refs[8 + NP :]
        g = refs[0]
        sums1, sums0 = refs[1 : 1 + NP], refs[1 + NP : 1 + 2 * NP]
        vout, dw, vec, qb = refs[1 + 2 * NP : 5 + 2 * NP]
        refs = refs[5 + 2 * NP :]
    else:
        g, dw, vec, qb = refs[:4]
        refs = refs[4:]
    w, proj, da, db, dc, ua, ub, uc, sdb, sdc, sub, suc = refs[:12]
    part, sa, ra, sb, rb, s3, r3 = refs[12:19]
    bufs = refs[19:-3]
    ss, rs, ls = refs[-3:]
    at = Place()
    wires = Wires(ss, rs)
    loads = fetch_qkv(layer, w_hbm, w, ls)
    partners = [{"tensor": at.mate}, {"tensor": at.cp}, {"dp": at.up}, {"dp": at.dn}]
    if last:
        rings = Rings()
        accs0, bufs = bufs[:NP], bufs[NP:]
        wide = Wide(wires, rings, (dw2, dw1, dw), bufs[: NP * WIDE_REFS], ls, 3)
        bufs = bufs[NP * WIDE_REFS :]
        narrow1 = Narrow(wires, rings, accs1, bufs[: NP * NARROW_REFS])
        bufs = bufs[NP * NARROW_REFS :]
        narrow0 = Narrow(wires, rings, accs0, bufs[: NP * NARROW_REFS])
        vectors = Vectors(wires, at, rings, bufs[NP * NARROW_REFS :])
        partners += [*rings.along_y, *rings.along_x, rings.other]
    greet(partners)
    chain_up, chain_dn = Line(wires, {"dp": at.up}), Line(wires, {"dp": at.dn})
    low3, low2, low1 = OWN0 - 3 * S, OWN0 - 2 * S, OWN0 - S
    high1, high2, high3 = OWN0 + S, OWN0 + 2 * S, OWN0 + 3 * S

    def chunk(ref, k, base=0):
        return ref.at[pl.ds(base + k * R, R)]

    def plus(base, k, other):
        mine = dwin[pl.ds(base + k * R, R), :].astype(F32)
        return (mine + other[pl.ds(k * R, R), :].astype(F32)).astype(BF)

    ups, dns = {}, {}

    def send(n, k, down, up):
        dns[n, k] = chain_dn.send(*down)
        ups[n, k] = chain_up.send(*up)

    def arrive(n, k):
        chain_dn.arrive(dns[n, k])
        chain_up.arrive(ups[n, k])

    def first(k):
        j = 3 - k
        send(
            1, k, (chunk(dwin, k, low3), chunk(da, k)), (chunk(dwin, j, high3), chunk(ua, j))
        )

    def second(k):
        j = 3 - k
        arrive(1, k)
        sdb[pl.ds(k * R, R), :] = plus(low2, k, da)
        sub[pl.ds(j * R, R), :] = plus(high2, j, ua)
        send(2, k, (chunk(sdb, k), chunk(db, k)), (chunk(sub, j), chunk(ub, j)))

    def third(k):
        j = 3 - k
        arrive(2, k)
        sdc[pl.ds(k * R, R), :] = plus(low1, k, db)
        suc[pl.ds(j * R, R), :] = plus(high1, j, ub)
        send(3, k, (chunk(sdc, k), chunk(dc, k)), (chunk(suc, j), chunk(uc, j)))

    for k in (1, 2, 3):
        first(k)
    send(2, 0, (chunk(dwin, 0, low2), chunk(db, 0)), (chunk(dwin, 3, high2), chunk(ub, 3)))
    def into(first, value):
        dw[:, :, :, :, pl.ds(first, value.shape[-1])] = as_blocks(value)

    proj[:, :LW] = dq[...]
    into(3 * LW, dwp[...])
    into(0, mm_lt(rows[...], dq[...]).astype(BF))
    for k in (1, 2, 3):
        second(k)
    for k in range(4):
        third(k)
    for k in range(4):
        arrive(3, k)
    if last:
        wide.start(0, 1)
    own = dwin[pl.ds(OWN0, S), :].astype(F32)
    proj[:, LW:] = (own + dc[...].astype(F32) + uc[...].astype(F32)).astype(BF)
    for copy in loads:
        copy.wait()
    scatter = Scatter(wires, at, part, sa, ra, sb, rb, s3, r3)
    part[...] = mm_rt(proj[pl.ds(at.far, 2 * R), :], w[...])
    scatter.far()
    part[...] = mm_rt(proj[pl.ds(at.near, 2 * R), :], w[...])
    scatter.near()
    into(LW, mm_lt(rows[...], proj[:, LW:]).astype(BF))
    if last:
        wide.start(2, 3)
        wide.forward(1)
        narrow1.start(*range(NP))
    qb[...] = jnp.broadcast_to(jnp.sum(proj[...].astype(F32), axis=0, keepdims=True), qb.shape)
    grad_in, grad_gain, grad_shift = norm_back(
        h[...].astype(F32), gain[layer, 0:1, :], scatter.total()
    )
    g[...] = gmix[...] + grad_in
    vec[0:1, :] = grad_gain
    vec[1:2, :] = grad_shift
    vec[2:8, :] = jnp.zeros((6, D), F32)
    if last:
        vectors.fill(((va0, vec, fb0, qb), (va1, vb1, fb1, qb1)))
        wide.forward(0)
        narrow1.forward(*range(NP))
        wide.finish(accs0, 1)
        narrow0.start(1)
        vectors.over_core()
        wide.forward(2, 3)
        narrow1.beyond(*range(NP))
        vectors.over_chip()
        wide.finish(accs0, 0)
        narrow0.start(0)
        narrow0.forward(1)
        vectors.over_y()
        wide.finish(accs0, 2, 3)
        narrow0.start(2, 3)
        narrow0.forward(0)
        vectors.over_x()
        narrow0.beyond(1)
        narrow0.forward(2, 3)
        narrow0.beyond(0, 2, 3)
        vectors.finish(vout)
        narrow1.finish(sums1)
        narrow0.finish(sums0)
    wires.close()


def back_in(cid, layer, final, *ins):
    last = bool(final)
    whole = pltpu.VMEM((S, 2 * LW), BF)
    blocks, eight, wide8 = (4, 2, 4, RP, 4 * LW), (8, D), (8, 3 * LW)
    outs = [((R, D), F32)]
    scratch = []
    if last:
        outs += reduced_shapes() * 2 + [(VEC, F32)]
        scratch += [pltpu.VMEM(blocks, BF), pltpu.VMEM(eight, F32), pltpu.VMEM(wide8, F32)]
    else:
        outs += [(blocks, BF), (eight, F32), (wide8, F32)]
    scratch += [pltpu.VMEM((D, 3 * LW), BF), pltpu.VMEM((S, 3 * LW), BF)]
    scratch += [whole] * 10 + scatter_scratch()
    if last:
        scratch += [pltpu.VMEM(*wide_shape(width, mode)) for _, _, width, mode in PIECES]
        scratch += wide_scratch() + narrow_scratch() * 2 + vector_scratch()
    return call(
        functools.partial(back_in_kernel, layer, last),
        "back_in%d" % layer,
        cid,
        [*ins, *final],
        outs,
        scratch,
        RS_SEMS + 22 + last * (6 * NP + 14 * NP + 9),
        limit=48 if last else 28,
        specs=[VM] * 7 + [ANY] + ([ANY] * 2 + [VM] * (NP + 6)) * last,
        local=3 + last * 3 * NP,
    )


class Ring:
    def __init__(self, wires, chunk, mine, side_up, side_dn, place, bufs):
        self.wires, self.chunk = wires, chunk
        self.mine, self.side_up, self.side_dn = mine, side_up, side_dn
        self.me, self.up, self.dn = place
        self.from_dn, self.from_up, self.send_up, self.send_dn, self.last_dn, self.last_up = bufs

    def half(self, ref, k):
        width = ref.shape[-1] // 2
        return ref.at[..., pl.ds(k * width, width)]

    def position(self, step):
        return lax.rem(self.me + step, 4)

    def start(self):
        push, chunk = self.wires.push, self.chunk
        p1, p2, p3 = self.position(1), self.position(2), self.position(3)
        self.a = push(chunk(p2, 0), self.from_dn, self.up)
        self.b = push(chunk(p2, 1), self.from_up, self.dn)
        self.c = push(chunk(p1, 1), self.half(self.last_dn, 1), self.up)
        self.d = push(chunk(p3, 0), self.half(self.last_up, 0), self.dn)

    def forward(self):
        push = self.wires.push
        self.a.wait_recv()
        total = self.side_up()[...].astype(F32) + self.from_dn[...].astype(F32)
        self.send_up[...] = total.astype(BF)
        self.e = push(self.send_up, self.half(self.last_dn, 0), self.up)
        self.b.wait_recv()
        total = self.side_dn()[...].astype(F32) + self.from_up[...].astype(F32)
        self.send_dn[...] = total.astype(BF)
        self.f = push(self.send_dn, self.half(self.last_up, 1), self.dn)

    def finish(self, out):
        for copy in (self.c, self.d, self.e, self.f):
            copy.wait_recv()
        part = self.mine()[...].astype(F32)
        out[...] = (
            part + self.last_dn[...].astype(F32) + self.last_up[...].astype(F32)
        ).astype(out.dtype)


PIECES = ((0, 0, F, 0), (1, 0, F, 1), (2, 0, 2 * LW, 0), (2, 2 * LW, 2 * LW, 1))
RP = R // 4
NP = len(PIECES)


class Rings:
    def __init__(self):
        i = lax.axis_index("dp")
        self.y = y = lax.rem(i, 4)
        self.x = lax.div(i, 8)
        self.zh = zh = lax.rem(lax.div(i, 4), 2)
        self.along_y = [{"dp": i - y + lax.rem(y + k, 4)} for k in (1, 2, 3)]
        self.along_x = [{"dp": lax.rem(i + 8 * k, 32)} for k in (1, 2, 3)]
        self.other = {"dp": i + 4 - 8 * zh}
        ring_y = (y, self.along_y[0], self.along_y[2])
        ring_x = (self.x, self.along_x[0], self.along_x[2])
        self.order = [(ring_y, ring_x), (ring_x, ring_y)]

    def next_to(self):
        return [*self.along_y[::2], *self.along_x[::2]]


def ring_scratch(lead, width):
    half = pltpu.VMEM((*lead, width // 2), BF)
    full = pltpu.VMEM((*lead, width), BF)
    return [half, half, half, half, full, full]


def wide_shape(width, mode):
    return ((4, 2, RP, width) if mode == 0 else (2, 4, RP, width), BF)


WIDE_REFS, NARROW_REFS = 9, 8


def wide_scratch():
    out = []
    for _, _, width, mode in PIECES:
        lead = wide_shape(width, mode)[0][:3]
        half = pltpu.VMEM((*lead, width // 2), BF)
        out += ring_scratch(lead, width) + [pltpu.VMEM((*lead, width), BF), half, half]
    return out


def narrow_scratch():
    out = []
    for _, _, width, _ in PIECES:
        small, rest = pltpu.VMEM((2, RP, width), BF), pltpu.VMEM((RP, width), BF)
        out += ring_scratch((2, RP), width) + [small, rest]
    return out


def reduced_shapes():
    return [((RP, width), F32) for _, _, width, _ in PIECES]


def as_blocks(w):
    return w.reshape(4, 2, 4, RP, w.shape[-1])


class Wide:
    def __init__(self, wires, rings, ins, bufs, ls, first_sem):
        self.rings, self.loads = [], []
        for k, (which, column, width, mode) in enumerate(PIECES):
            refs = bufs[k * WIDE_REFS : (k + 1) * WIDE_REFS]
            mine, side_up, side_dn = refs[6:9]
            w = ins[which]

            def chunk(pos, half, w=w, mode=mode, column=column, size=width // 2):
                cols = pl.ds(column + half * size, size)
                return w.at[:, :, pos, :, cols] if mode == 0 else w.at[pos, :, :, :, cols]

            place = rings.order[mode][0]
            me = place[0]
            cols = pl.ds(column, width)
            whole = w.at[:, :, me, :, cols] if mode == 0 else w.at[me, :, :, :, cols]
            parts = (
                (chunk(lax.rem(me + 1, 4), 0), side_up),
                (chunk(lax.rem(me + 3, 4), 1), side_dn),
                (whole, mine),
            )
            sems = [ls.at[first_sem + 3 * k + j] for j in range(3)]
            self.loads.append(
                [pltpu.make_async_copy(src, dst, sem) for (src, dst), sem in zip(parts, sems)]
            )
            self.rings.append(
                Ring(
                    wires, chunk, lambda r=mine: r, lambda r=side_up: r, lambda r=side_dn: r,
                    place, refs[0:6],
                )
            )

    def start(self, *ks):
        for k in ks:
            for copy in self.loads[k]:
                copy.start()
            self.rings[k].start()

    def forward(self, *ks):
        for k in ks:
            for copy in self.loads[k]:
                copy.wait()
            self.rings[k].forward()

    def finish(self, accs, *ks):
        for k in ks:
            self.rings[k].finish(accs[k])


class Narrow:
    def __init__(self, wires, rings, accs, bufs):
        self.wires, self.rings, self.parts, self.last = wires, [], [], {}
        self.zh, self.other = rings.zh, rings.other
        for k, (_, _, width, mode) in enumerate(PIECES):
            refs = bufs[k * NARROW_REFS : (k + 1) * NARROW_REFS]
            acc = accs[k]
            place = rings.order[mode][1]

            def chunk(pos, half, acc=acc, mode=mode, size=width // 2):
                cols = pl.ds(half * size, size)
                return acc.at[pos, :, :, cols] if mode == 0 else acc.at[:, pos, :, cols]

            def mine(acc=acc, mode=mode, pos=place[0]):
                return acc.at[pos] if mode == 0 else acc.at[:, pos]

            self.rings.append(
                Ring(
                    wires, chunk, mine,
                    lambda n=chunk, p=lax.rem(place[0] + 1, 4): n(p, 0),
                    lambda n=chunk, p=lax.rem(place[0] + 3, 4): n(p, 1),
                    place, refs[0:6],
                )
            )
            self.parts.append(refs[6:8])

    def start(self, *ks):
        for k in ks:
            self.rings[k].start()

    def forward(self, *ks):
        for k in ks:
            self.rings[k].forward()

    def beyond(self, *ks):
        for k in ks:
            small, rest = self.parts[k]
            self.rings[k].finish(small)
            self.last[k] = self.wires.push(small.at[1 - self.zh], rest, self.other)

    def finish(self, outs):
        for k, out in enumerate(outs):
            small, rest = self.parts[k]
            self.last[k].wait_recv()
            out[...] = small[self.zh].astype(F32) + rest[...].astype(F32)


VEC = (24, D)


def vector_scratch():
    few, whole, four = (
        pltpu.VMEM((16, D), F32), pltpu.VMEM(VEC, F32), pltpu.VMEM((4, *VEC), F32),
    )
    return [whole, few, few, four, four, whole]


class Vectors:
    def __init__(self, wires, at, rings, bufs):
        self.wires, self.at, self.rings = wires, at, rings
        self.vec, self.vmate, self.vcp, self.vy, self.vx, self.vz = bufs

    def fill(self, layers):
        vec = self.vec
        vec[...] = jnp.zeros_like(vec)
        for k, (va, vb, fb, qb) in enumerate(layers):
            vec[8 * k : 8 * k + 6, :] = va[0:6, :]
            vec[8 * k + 6 : 8 * k + 8, :] = vb[0:2, :]
            vec[16 + k : 17 + k, :] = fb[0:1, :]
            vec[18 + k : 19 + k, : 3 * LW] = qb[0:1, :]
        self.one = self.wires.push(vec.at[pl.ds(0, 16)], self.vmate, {"tensor": self.at.mate})

    def over_core(self):
        vec = self.vec
        self.one.wait_recv()
        self.wires.left(self.one)
        vec[0:16, :] = vec[0:16, :] + self.vmate[...]
        self.two = self.wires.push(vec.at[pl.ds(0, 16)], self.vcp, {"tensor": self.at.cp})

    def over_chip(self):
        vec, vy, y = self.vec, self.vy, self.rings.y
        self.two.wait_recv()
        vy[y] = vec[...]
        vy[y, 0:16, :] = vec[0:16, :] + self.vcp[...]
        self.sent = [self.wires.push(vy.at[y], vy.at[y], d) for d in self.rings.along_y]

    def over_y(self):
        vx, vy, x = self.vx, self.vy, self.rings.x
        for copy in self.sent:
            copy.wait_recv()
        vx[x] = vy[0] + vy[1] + vy[2] + vy[3]
        self.sent = [self.wires.push(vx.at[x], vx.at[x], d) for d in self.rings.along_x]

    def over_x(self):
        vec, vx = self.vec, self.vx
        for copy in self.sent:
            copy.wait_recv()
        self.wires.left(self.two)
        vec[...] = vx[0] + vx[1] + vx[2] + vx[3]
        self.last = self.wires.push(vec, self.vz, self.rings.other)

    def finish(self, out):
        self.last.wait_recv()
        out[...] = self.vec[...] + self.vz[...]


def shards(
    tokens_in,
    image_starts,
    norm_gain,
    norm_bias,
    qkv_weight,
    qv_bias,
    proj_weight,
    out_bias,
    layer_scale,
    fc1_weight,
    fc1_bias,
    fc2_weight,
    out_grad,
):
    layers = qkv_weight.shape[0]
    w_qkv = jnp.transpose(qkv_weight, (0, 2, 1, 3))
    hidden = tokens_in
    saved = []
    for l in range(layers):
        rows_one, q, win = inward(2 * l, l, hidden, norm_gain, norm_bias, qv_bias, w_qkv)
        att, lt = attend(image_starts, q, win)
        mixed, br1, br2, nxt, rows_two, act, slope = outward(
            2 * l + 1, l, BF if l == layers - 1 else F32, att, hidden, layer_scale, out_bias,
            norm_gain, norm_bias, fc1_bias, proj_weight, fc1_weight, fc2_weight,
        )
        saved.append((rows_one, q, win, att, lt, hidden, mixed, br1, br2, rows_two, act, slope))
        hidden = nxt
    grad = out_grad
    given, accs, kept = (), (), None
    for l in reversed(range(layers)):
        rows_one, q, win, att, lt, h, mixed, br1, br2, rows_two, act, slope = saved[l]
        gmix, gatt, dw2, dw1, dwp, va, fb, *accs = back_out(
            4 + 2 * l, l, given, grad, layer_scale, out_bias, norm_gain, mixed, br1, br2,
            act, slope, rows_two, att, fc1_weight, fc2_weight, proj_weight,
        )
        dq, dwin = attend_back(image_starts, q, win, gatt, att, lt)
        final = ()
        if l == 0:
            va1, vb1, fb1, qb1 = kept
            final = (as_blocks(dw2), as_blocks(dw1), *accs, va1, va, vb1, fb1, fb, qb1)
        grad, *rest = back_in(
            5 + 2 * l, l, final, dq, dwin, rows_one, gmix, h, norm_gain, dwp, w_qkv
        )
        if l:
            dw, vb, qb = rest
            given = (as_blocks(dw2), as_blocks(dw1), dw)
            kept = (va, vb, fb, qb)
    a1, b1, c1, d1, a0, b0, c0, d0, vec = rest
    rows = vec[:16].reshape(2, 8, D)
    qkv = jnp.stack(
        [jnp.concatenate([c0, d0[:, :LW]], 1), jnp.concatenate([c1, d1[:, :LW]], 1)]
    )
    return (
        hidden,
        grad,
        jnp.stack([rows[:, 6], rows[:, 2]], 1),
        jnp.stack([rows[:, 7], rows[:, 3]], 1),
        qkv.reshape(2, RP, 3, LW),
        jnp.stack([vec[18:20, :LW], vec[18:20, 2 * LW : 3 * LW]], 1),
        jnp.stack([d0[:, LW:].T, d1[:, LW:].T]),
        jnp.stack([rows[:, 5], rows[:, 1]], 1),
        jnp.stack([rows[:, 4], rows[:, 0]], 1),
        jnp.stack([b0, b1]),
        vec[16:18],
        jnp.stack([a0.T, a1.T]),
    )


def solution(mesh):
    return jax.shard_map(
        shards,
        mesh=mesh,
        in_specs=(
            P(("dp", "tensor"), None),
            P(),
            P(),
            P(),
            P(None, None, None, "tensor"),
            P(None, None, "tensor"),
            P(None, "tensor", None),
            P(),
            P(),
            P(None, None, "tensor"),
            P(None, "tensor"),
            P(None, "tensor", None),
            P(("dp", "tensor"), None),
        ),
        out_specs=(
            P(("dp", "tensor"), None),
            P(("dp", "tensor"), None),
            P(),
            P(),
            P(None, "dp", None, "tensor"),
            P(None, None, "tensor"),
            P(None, "tensor", "dp"),
            P(),
            P(),
            P(None, "dp", "tensor"),
            P(None, "tensor"),
            P(None, "tensor", "dp"),
        ),
        check_vma=False,
    )
```

```python
import functools

import jax
import jax.numpy as jnp
from jax import lax
from jax.experimental import pallas as pl
from jax.experimental.pallas import tpu as pltpu
from jax.sharding import PartitionSpec as P

MESH = pl.DeviceIdType.MESH
BF = jnp.bfloat16
F32 = jnp.float32
VM = pl.BlockSpec(memory_space=pltpu.VMEM)
SM = pl.BlockSpec(memory_space=pltpu.SMEM)
ANY = pl.BlockSpec(memory_space=pl.ANY)

HEAD_DIM = 64
IMG_LEN = 1370
EPS = 1e-06
NEG = -1e30

R = 128
S = 512
D = 1024
LW = 256
HL = LW // HEAD_DIM
F = 1024
TOTAL = 16384
NDP = 32
FAR3 = 384
OWN0 = FAR3 + 2 * S
NW = 2 * OWN0 + S
QB = 256
KB = 256
NB = NW // KB
C = 2
RC = R // C
MB = 1 << 20


def mm(a, b):
    return jnp.dot(a, b, preferred_element_type=F32)


def mm_rt(a, b):
    return lax.dot_general(a, b, (((1,), (1,)), ((), ())), preferred_element_type=F32)


def mm_lt(a, b):
    return lax.dot_general(a, b, (((0,), (0,)), ((), ())), preferred_element_type=F32)


class Place:
    def __init__(self):
        self.t = lax.axis_index("tensor")
        self.core = lax.rem(self.t, 2)
        self.mate = self.t + 1 - 2 * self.core
        self.cp = lax.rem(self.t + 2, 4)
        self.own = pl.multiple_of(self.t * R, R)
        self.opp = pl.multiple_of(self.cp * R, R)
        self.near = pl.multiple_of((self.t - self.core) * R, 2 * R)
        self.far = pl.multiple_of(2 * R - self.near, 2 * R)
        self.dp = lax.axis_index("dp")
        self.up = lax.rem(self.dp + 1, NDP)
        self.dn = lax.rem(self.dp + NDP - 1, NDP)


def greet(devices):
    barrier = pltpu.get_barrier_semaphore()
    for device in devices:
        pl.semaphore_signal(barrier, inc=1, device_id=device, device_id_type=MESH)
    pl.semaphore_wait(barrier, len(devices))


class Wires:
    def __init__(self, send, recv):
        self.send, self.recv, self.count, self.open = send, recv, 0, []

    def push(self, src, dst, device):
        k = self.count
        self.count += 1
        copy = pltpu.make_async_remote_copy(
            src, dst, self.send.at[k], self.recv.at[k], device_id=device, device_id_type=MESH
        )
        copy.start()
        self.open.append(copy)
        return copy

    def left(self, copy):
        copy.wait_send()
        self.open = [c for c in self.open if c is not copy]

    def close(self):
        for copy in self.open:
            copy.wait_send()


class Chain:
    def __init__(self, wires, at, up, relay):
        self.wires, self.at, self.relay = wires, at, relay
        y = lax.rem(at.dp, 4)
        self.edge = (y == 3) if up else (y == 0)
        self.plain = jnp.logical_not(self.edge)
        self.device = at.up if up else at.dn
        self.items = []

    def plan(self, src, dst, partner_dst=None, when=True, partner_when=True):
        wires, at = self.wires, self.at
        slot = self.relay.at[len(self.items)]
        k = wires.count
        wires.count += 2

        def copy(source, target, n, device):
            return lambda: pltpu.make_async_remote_copy(
                source, target, wires.send.at[n], wires.recv.at[n],
                device_id=device, device_id_type=MESH,
            )

        direct = copy(src, dst, k, {"dp": self.device})
        first = copy(src, slot, k + 1, {"tensor": at.cp})
        target = dst if partner_dst is None else partner_dst
        second = copy(slot, target, k, {"dp": self.device, "tensor": at.cp})
        item = (direct, first, second, when, partner_when)
        self.items.append(item)
        return item

    def send(self, item):
        direct, first, _, when, _ = item
        pl.when(self.plain & when)(lambda: direct().start())
        pl.when(self.edge & when)(lambda: first().start())

    def hand_on(self, item):
        _, first, second, _, partner_when = item

        @pl.when(self.edge & partner_when)
        def _():
            first().wait_recv()
            second().start()

    def arrive(self, item):
        pl.when(item[3])(lambda: item[0]().wait_recv())

    def close(self):
        for direct, first, second, when, partner_when in self.items:
            pl.when(self.plain & when)(lambda c=direct: c().wait_send())
            pl.when(self.edge & when)(lambda c=first: c().wait_send())
            pl.when(self.edge & partner_when)(lambda c=second: c().wait_send())


class Line:
    def __init__(self, wires, device):
        self.wires, self.device = wires, device

    def send(self, src, dst):
        return self.wires.push(src, dst, self.device)

    def arrive(self, copy):
        copy.wait_recv()


def chain_partners(at):
    return [
        {"tensor": at.mate},
        {"tensor": at.cp},
        {"dp": at.up},
        {"dp": at.dn},
        {"dp": at.up, "tensor": at.cp},
        {"dp": at.dn, "tensor": at.cp},
    ]


AG_SEMS = 2 * C + 1
RS_SEMS = 2 * C + 1


class Gather:
    def __init__(self, wires, at, buf):
        self.wires, self.at, self.buf = wires, at, buf
        own = at.own
        self.across, self.passed = [], []
        for c in range(C):
            part = buf.at[pl.ds(own + c * RC, RC)]
            self.across.append(wires.push(part, part, {"tensor": at.cp}))
        part = buf.at[pl.ds(own, R)]
        self.beside = wires.push(part, part, {"tensor": at.mate})

    def near(self):
        self.beside.wait_recv()

    def take(self, c):
        self.across[c].wait_recv()
        part = self.buf.at[pl.ds(self.at.opp + c * RC, RC)]
        self.passed.append(self.wires.push(part, part, {"tensor": self.at.mate}))

    def arrived(self, c):
        self.passed[c].wait_recv()

    def far(self):
        for c in range(C):
            self.take(c)
        for c in range(C):
            self.arrived(c)


class Rows:
    def __init__(self, at, chunk=None):
        if chunk is None:
            self.parts = [(at.near, 2 * R)]
        else:
            self.parts = [
                (pl.multiple_of(at.far + core * R + chunk * RC, RC), RC) for core in range(2)
            ]

    def load(self, ref, cols=slice(None)):
        parts = [ref[pl.ds(first, count), cols] for first, count in self.parts]
        return parts[0] if len(parts) == 1 else jnp.concatenate(parts, axis=0)

    def store(self, ref, value, cols=slice(None)):
        at = 0
        for first, count in self.parts:
            ref[pl.ds(first, count), cols] = value[at : at + count]
            at += count


class Scatter:
    def __init__(self, wires, at, bufs):
        self.wires, self.at = wires, at
        self.far, self.near = bufs[:2]
        self.send1, self.recv1, self.send2, self.recv2, self.send3, self.recv3 = bufs[2:]
        self.ones, self.twos = [], []

    def put(self, c, value):
        for core in range(2):
            self.far[pl.ds(core * R + c * RC, RC), :] = value[core * RC : (core + 1) * RC]

    def first(self, c):
        at = self.at
        rows = pl.ds(c * RC, RC)
        src = pl.ds(pl.multiple_of((1 - at.core) * R + c * RC, RC), RC)
        self.send1[rows, :] = self.far[src, :].astype(BF)
        self.ones.append(
            self.wires.push(self.send1.at[rows], self.recv1.at[rows], {"tensor": at.mate})
        )

    def second(self, c):
        at = self.at
        rows = pl.ds(c * RC, RC)
        src = pl.ds(pl.multiple_of(at.core * R + c * RC, RC), RC)
        self.ones[c].wait_recv()
        total = self.far[src, :] + self.recv1[rows, :].astype(F32)
        self.send2[rows, :] = total.astype(BF)
        self.twos.append(
            self.wires.push(self.send2.at[rows], self.recv2.at[rows], {"tensor": at.cp})
        )

    def third(self):
        at = self.at
        src = pl.ds(pl.multiple_of((1 - at.core) * R, R), R)
        self.send3[...] = self.near[src, :].astype(BF)
        self.three = self.wires.push(self.send3, self.recv3, {"tensor": at.mate})

    def everything(self, product):
        self.far[...] = product(self.at.far)
        for c in range(C):
            self.first(c)
        self.near[...] = product(self.at.near)
        for c in range(C):
            self.second(c)
        self.third()

    def total(self):
        self.three.wait_recv()
        for copy in self.twos:
            copy.wait_recv()
        own = self.near[pl.ds(pl.multiple_of(self.at.core * R, R), R), :]
        return own + self.recv3[...].astype(F32) + self.recv2[...].astype(F32)


def gather_hidden_scatter(at, gather, scatter, hidden, product, ready):
    gather.near()
    hidden(Rows(at))
    ready()
    gather.take(0)
    gather.arrived(0)
    rows = [Rows(at, c) for c in range(C)]
    hidden(rows[0])
    gather.take(1)
    scatter.put(0, product(rows[0]))
    scatter.first(0)
    gather.arrived(1)
    hidden(rows[1])
    scatter.second(0)
    scatter.put(1, product(rows[1]))
    scatter.first(1)
    scatter.near[...] = product(Rows(at))
    scatter.second(1)
    scatter.third()


SCATTER_REFS = 6


def scatter_scratch(count):
    return [pltpu.VMEM((2 * R, D), F32)] * 2 + [pltpu.VMEM((R, D), BF)] * (6 * count)


def scatter_refs(bufs, which):
    first = 2 + SCATTER_REFS * which
    return [*bufs[:2], *bufs[first : first + SCATTER_REFS]]


class Refs:
    def __init__(self, refs):
        self.refs = list(refs)

    def take(self, count):
        out, self.refs = self.refs[:count], self.refs[count:]
        return out


def fetch(src, dst, sem):
    copy = pltpu.make_async_copy(src, dst, sem)
    copy.start()
    return copy


def fetch_qkv(layer, w, buf, ls, base=0):
    return [
        fetch(w.at[layer, k], buf.at[:, pl.ds(k * LW, LW)], ls.at[base + k]) for k in range(3)
    ]


def normalized(v):
    centered = v - jnp.mean(v, axis=-1, keepdims=True)
    scale = lax.rsqrt(jnp.mean(centered * centered, axis=-1, keepdims=True) + EPS)
    return centered * scale, scale


def norm_back(v, gain, grad):
    x_hat, scale = normalized(v)
    u = grad * gain
    grad_in = scale * (
        u
        - jnp.mean(u, axis=-1, keepdims=True)
        - x_hat * jnp.mean(u * x_hat, axis=-1, keepdims=True)
    )
    return (
        grad_in,
        jnp.sum(grad * x_hat, axis=0, keepdims=True),
        jnp.sum(grad, axis=0, keepdims=True),
    )


def call(kernel, name, cid, ins, outs, scratch, sems, limit, specs=None, local=0, out_specs=None):
    shapes = [jax.ShapeDtypeStruct(shape, dtype) for shape, dtype in outs]
    extra = []
    if sems:
        extra = [pltpu.SemaphoreType.DMA((sems,)), pltpu.SemaphoreType.DMA((sems,))]
    if local:
        extra.append(pltpu.SemaphoreType.DMA((local,)))
    params = dict(vmem_limit_bytes=limit * MB)
    if cid is not None:
        params.update(collective_id=cid, has_side_effects=True)
    return pl.pallas_call(
        kernel,
        out_shape=shapes,
        in_specs=specs or [VM] * len(ins),
        out_specs=out_specs or [VM] * len(outs),
        scratch_shapes=list(scratch) + extra,
        compiler_params=pltpu.CompilerParams(**params),
        name=name,
    )(*ins)


class Ring:
    def __init__(self, wires, chunk, mine, side_up, side_dn, place, bufs):
        self.wires, self.chunk = wires, chunk
        self.mine, self.side_up, self.side_dn = mine, side_up, side_dn
        self.me, self.up, self.dn = place
        self.from_dn, self.from_up, self.send_up, self.send_dn, self.last_dn, self.last_up = bufs

    def half(self, ref, k):
        width = ref.shape[-1] // 2
        return ref.at[..., pl.ds(k * width, width)]

    def position(self, step):
        return lax.rem(self.me + step, 4)

    def start(self):
        push, chunk = self.wires.push, self.chunk
        p1, p2, p3 = self.position(1), self.position(2), self.position(3)
        self.a = push(chunk(p2, 0), self.from_dn, self.up)
        self.b = push(chunk(p2, 1), self.from_up, self.dn)
        self.c = push(chunk(p1, 1), self.half(self.last_dn, 1), self.up)
        self.d = push(chunk(p3, 0), self.half(self.last_up, 0), self.dn)

    def forward(self):
        push = self.wires.push
        self.a.wait_recv()
        total = self.side_up()[...].astype(F32) + self.from_dn[...].astype(F32)
        self.send_up[...] = total.astype(BF)
        self.e = push(self.send_up, self.half(self.last_dn, 0), self.up)
        self.b.wait_recv()
        total = self.side_dn()[...].astype(F32) + self.from_up[...].astype(F32)
        self.send_dn[...] = total.astype(BF)
        self.f = push(self.send_dn, self.half(self.last_up, 1), self.dn)

    def finish(self, out):
        for copy in (self.c, self.d, self.e, self.f):
            copy.wait_recv()
        part = self.mine()[...].astype(F32)
        out[...] = (
            part + self.last_dn[...].astype(F32) + self.last_up[...].astype(F32)
        ).astype(out.dtype)


PIECES = ((0, 0, F, 0), (1, 0, F, 1), (2, 0, 2 * LW, 0), (2, 2 * LW, 2 * LW, 1))
RP = R // 4
NP = len(PIECES)


class Rings:
    def __init__(self):
        i = lax.axis_index("dp")
        self.y = y = lax.rem(i, 4)
        self.x = lax.div(i, 8)
        self.zh = zh = lax.rem(lax.div(i, 4), 2)
        self.along_y = [{"dp": i - y + lax.rem(y + k, 4)} for k in (1, 2, 3)]
        self.along_x = [{"dp": lax.rem(i + 8 * k, 32)} for k in (1, 2, 3)]
        self.other = {"dp": i + 4 - 8 * zh}
        ring_y = (y, self.along_y[0], self.along_y[2])
        ring_x = (self.x, self.along_x[0], self.along_x[2])
        self.order = [(ring_y, ring_x), (ring_x, ring_y)]

    def next_to(self):
        return [*self.along_y[::2], *self.along_x[::2]]


def ring_scratch(lead, width):
    half = pltpu.VMEM((*lead, width // 2), BF)
    full = pltpu.VMEM((*lead, width), BF)
    return [half, half, half, half, full, full]


def wide_shape(width, mode):
    return ((4, 2, RP, width) if mode == 0 else (2, 4, RP, width), BF)


WIDE_REFS, NARROW_REFS = 9, 8


def wide_scratch():
    out = []
    for _, _, width, mode in PIECES:
        lead = wide_shape(width, mode)[0][:3]
        half = pltpu.VMEM((*lead, width // 2), BF)
        out += ring_scratch(lead, width) + [pltpu.VMEM((*lead, width), BF), half, half]
    return out


def narrow_scratch():
    out = []
    for _, _, width, _ in PIECES:
        small, rest = pltpu.VMEM((2, RP, width), BF), pltpu.VMEM((RP, width), BF)
        out += ring_scratch((2, RP), width) + [small, rest]
    return out


def reduced_shapes():
    return [((RP, width), F32) for _, _, width, _ in PIECES]


def as_blocks(w):
    return w.reshape(4, 2, 4, RP, w.shape[-1])


class Wide:
    def __init__(self, wires, rings, ins, bufs, ls, first_sem):
        self.rings, self.loads = [], []
        for k, (which, column, width, mode) in enumerate(PIECES):
            refs = bufs[k * WIDE_REFS : (k + 1) * WIDE_REFS]
            mine, side_up, side_dn = refs[6:9]
            w = ins[which]

            def chunk(pos, half, w=w, mode=mode, column=column, size=width // 2):
                cols = pl.ds(column + half * size, size)
                return w.at[:, :, pos, :, cols] if mode == 0 else w.at[pos, :, :, :, cols]

            place = rings.order[mode][0]
            me = place[0]
            cols = pl.ds(column, width)
            whole = w.at[:, :, me, :, cols] if mode == 0 else w.at[me, :, :, :, cols]
            parts = (
                (chunk(lax.rem(me + 1, 4), 0), side_up),
                (chunk(lax.rem(me + 3, 4), 1), side_dn),
                (whole, mine),
            )
            sems = [ls.at[first_sem + 3 * k + j] for j in range(3)]
            self.loads.append(
                [pltpu.make_async_copy(src, dst, sem) for (src, dst), sem in zip(parts, sems)]
            )
            self.rings.append(
                Ring(
                    wires, chunk, lambda r=mine: r, lambda r=side_up: r, lambda r=side_dn: r,
                    place, refs[0:6],
                )
            )

    def start(self, *ks):
        for k in ks:
            for copy in self.loads[k]:
                copy.start()
            self.rings[k].start()

    def forward(self, *ks):
        for k in ks:
            for copy in self.loads[k]:
                copy.wait()
            self.rings[k].forward()

    def finish(self, accs, *ks):
        for k in ks:
            self.rings[k].finish(accs[k])


class Narrow:
    def __init__(self, wires, rings, accs, bufs):
        self.wires, self.rings, self.parts, self.last = wires, [], [], {}
        self.zh, self.other = rings.zh, rings.other
        for k, (_, _, width, mode) in enumerate(PIECES):
            refs = bufs[k * NARROW_REFS : (k + 1) * NARROW_REFS]
            acc = accs[k]
            place = rings.order[mode][1]

            def chunk(pos, half, acc=acc, mode=mode, size=width // 2):
                cols = pl.ds(half * size, size)
                return acc.at[pos, :, :, cols] if mode == 0 else acc.at[:, pos, :, cols]

            def mine(acc=acc, mode=mode, pos=place[0]):
                return acc.at[pos] if mode == 0 else acc.at[:, pos]

            self.rings.append(
                Ring(
                    wires, chunk, mine,
                    lambda n=chunk, p=lax.rem(place[0] + 1, 4): n(p, 0),
                    lambda n=chunk, p=lax.rem(place[0] + 3, 4): n(p, 1),
                    place, refs[0:6],
                )
            )
            self.parts.append(refs[6:8])

    def start(self, *ks):
        for k in ks:
            self.rings[k].start()

    def forward(self, *ks):
        for k in ks:
            self.rings[k].forward()

    def beyond(self, *ks):
        for k in ks:
            small, rest = self.parts[k]
            self.rings[k].finish(small)
            self.last[k] = self.wires.push(small.at[1 - self.zh], rest, self.other)

    def finish(self, outs):
        for k, out in enumerate(outs):
            small, rest = self.parts[k]
            self.last[k].wait_recv()
            out[...] = small[self.zh].astype(F32) + rest[...].astype(F32)


VEC = (24, D)


def vector_scratch():
    few, whole, four = (
        pltpu.VMEM((16, D), F32), pltpu.VMEM(VEC, F32), pltpu.VMEM((4, *VEC), F32),
    )
    return [whole, few, few, four, four, whole]


class Vectors:
    def __init__(self, wires, at, rings, bufs):
        self.wires, self.at, self.rings = wires, at, rings
        self.vec, self.vmate, self.vcp, self.vy, self.vx, self.vz = bufs

    def fill(self, layers):
        vec = self.vec
        vec[...] = jnp.zeros_like(vec)
        for k, (va, vb, fb, qb) in enumerate(layers):
            vec[8 * k : 8 * k + 6, :] = va[0:6, :]
            vec[8 * k + 6 : 8 * k + 8, :] = vb[0:2, :]
            vec[16 + k : 17 + k, :] = fb[0:1, :]
            vec[18 + k : 19 + k, : 3 * LW] = qb[0:1, :]
        self.one = self.wires.push(vec.at[pl.ds(0, 16)], self.vmate, {"tensor": self.at.mate})

    def over_core(self):
        vec = self.vec
        self.one.wait_recv()
        self.wires.left(self.one)
        vec[0:16, :] = vec[0:16, :] + self.vmate[...]
        self.two = self.wires.push(vec.at[pl.ds(0, 16)], self.vcp, {"tensor": self.at.cp})

    def over_chip(self):
        vec, vy, y = self.vec, self.vy, self.rings.y
        self.two.wait_recv()
        vy[y] = vec[...]
        vy[y, 0:16, :] = vec[0:16, :] + self.vcp[...]
        self.sent = [self.wires.push(vy.at[y], vy.at[y], d) for d in self.rings.along_y]

    def over_y(self):
        vx, vy, x = self.vx, self.vy, self.rings.x
        for copy in self.sent:
            copy.wait_recv()
        vx[x] = vy[0] + vy[1] + vy[2] + vy[3]
        self.sent = [self.wires.push(vx.at[x], vx.at[x], d) for d in self.rings.along_x]

    def over_x(self):
        vec, vx = self.vec, self.vx
        for copy in self.sent:
            copy.wait_recv()
        self.wires.left(self.two)
        vec[...] = vx[0] + vx[1] + vx[2] + vx[3]
        self.last = self.wires.push(vec, self.vz, self.rings.other)

    def finish(self, out):
        self.last.wait_recv()
        out[...] = self.vec[...] + self.vz[...]


def inward_part(layer, at, wires, hidden, gain, bias, b2, w, loads, rows, q, win, relay):
    x_hat, _ = normalized(hidden)
    rows[pl.ds(at.own, R), :] = (x_hat * gain[layer, 0:1, :] + bias[layer, 0:1, :]).astype(BF)
    gather = Gather(wires, at, rows)

    def project(first):
        out = mm(rows[pl.ds(first, 2 * R), :], w[...])
        q[pl.ds(first, 2 * R), :] = (out[:, :LW] + b2[layer, 0:1, :]).astype(BF)
        win[pl.ds(OWN0 + first, 2 * R), :LW] = out[:, LW : 2 * LW].astype(BF)
        win[pl.ds(OWN0 + first, 2 * R), LW:] = (out[:, 2 * LW :] + b2[layer, 1:2, :]).astype(BF)

    def part(first):
        return win.at[pl.ds(pl.multiple_of(first, R), R)]

    offs = [at.near, at.near + R, at.far, at.far + R]
    others = offs[2:] + offs[:2]
    chain_up, chain_dn = Chain(wires, at, True, relay), Chain(wires, at, False, relay)
    ups, dns = {}, {}
    for n in range(1, 4):
        low, high = OWN0 - n * S, OWN0 + n * S
        for k, (own, other) in enumerate(zip(offs, others)):
            if n < 3:
                ups[n, k] = chain_up.plan(part(low + S + own), part(low + own), part(low + other))
                dns[n, k] = chain_dn.plan(
                    part(high - S + own), part(high + own), part(high + other)
                )
                continue
            ups[n, k] = chain_up.plan(
                part(low + S + own),
                part(jnp.maximum(low + own, 0)),
                part(jnp.maximum(low + other, 0)),
                own > 0,
                other > 0,
            )
            dns[n, k] = chain_dn.plan(
                part(high - S + own),
                part(jnp.minimum(high + own, NW - R)),
                part(jnp.minimum(high + other, NW - R)),
                own < S - R,
                other < S - R,
            )

    def hop(n, *ks):
        for k in ks:
            chain_up.send(ups[n, k])
            chain_dn.send(dns[n, k])

    for copy in loads:
        copy.wait()
    gather.near()
    project(at.near)
    hop(1, 0, 1)
    gather.far()
    for k in range(2):
        chain_up.hand_on(ups[1, k])
        chain_dn.hand_on(dns[1, k])
    project(at.far)
    hop(1, 2, 3)

    def hand_on(n, *ks):
        for k in ks:
            chain_up.hand_on(ups[n, k])
            chain_dn.hand_on(dns[n, k])

    def onward(n, *ks):
        for k in ks:
            chain_up.arrive(ups[n, k])
            chain_dn.arrive(dns[n, k])
            if n < 3:
                hop(n + 1, k)

    onward(1, 0, 1)
    hand_on(1, 2, 3)
    hand_on(2, 0, 1)
    onward(1, 2, 3)
    onward(2, 0, 1)
    hand_on(2, 2, 3)
    hand_on(3, 0, 1)
    onward(2, 2, 3)
    hand_on(3, 2, 3)
    onward(3, 0, 1, 2, 3)
    chain_up.close()
    chain_dn.close()


IN_OUTS = [((S, D), BF), ((S, LW), BF), ((NW, 2 * LW), BF)]
IN_SCRATCH = [pltpu.VMEM((D, 3 * LW), BF), pltpu.VMEM((12, R, 2 * LW), BF)]
IN_SEMS = AG_SEMS + 48


def inward_kernel(h, gain, bias, b2, w_hbm, rows, q, win, w, relay, ss, rs, ls):
    at = Place()
    wires = Wires(ss, rs)
    loads = fetch_qkv(0, w_hbm, w, ls)
    greet(chain_partners(at))
    inward_part(
        0, at, wires, h[...].astype(F32), gain, bias, b2, w, loads, rows, q, win, relay
    )
    wires.close()


def inward(cid, *ins):
    return call(
        inward_kernel, "inward", cid, ins, IN_OUTS, IN_SCRATCH, IN_SEMS,
        limit=14, specs=[VM] * 4 + [ANY], local=3,
    )


def ids_of(position, starts):
    total = jnp.zeros_like(position)
    for k in range(starts.shape[0]):
        first = starts[k]
        total += (position >= first).astype(jnp.int32)
        total += (position >= first + IMG_LEN).astype(jnp.int32)
    return jnp.where((position >= 0) & (position < TOTAL), total, -1)


def key_range(base, block, starts):
    first = base + block * QB
    last = first + QB - 1
    low, high = jnp.int32(0), jnp.int32(TOTAL)
    for k in range(starts.shape[0]):
        for edge in (starts[k], starts[k] + IMG_LEN):
            low = jnp.where(edge <= first, jnp.maximum(low, edge), low)
            high = jnp.where(edge > last, jnp.minimum(high, edge), high)
    edge = jnp.bool_(False)
    for k in range(starts.shape[0]):
        for at in (starts[k], starts[k] + IMG_LEN):
            edge = edge | ((at > first) & (at <= last))
    low, high = low - base + OWN0, high - base + OWN0
    low_block = lax.div(jnp.maximum(low, 0), KB)
    high_block = lax.div(jnp.minimum(high, NW) + KB - 1, KB)
    whole = lambda kb: jnp.logical_not(edge) & (kb * KB >= low) & (kb * KB + KB <= high)
    return low_block, high_block, whole


def spread_heads(value, out):
    lane = lax.broadcasted_iota(jnp.int32, (QB, LW), 1)
    for head in range(HL):
        mine = (lane >= head * HEAD_DIM) & (lane < (head + 1) * HEAD_DIM)
        out[pl.ds(head * QB, QB), :] = jnp.where(mine, value, 0.0).astype(BF)


def half_of(head):
    return head * HEAD_DIM // 128 * 128


def pick_heads(parts):
    lane = lax.broadcasted_iota(jnp.int32, (QB, 128), 1)
    halves = [
        jnp.where(lane < HEAD_DIM, parts(head), parts(head + 1)) for head in range(0, HL, 2)
    ]
    return jnp.concatenate(halves, axis=1)


def attend_kernel(starts, q, win, out, lt, qm, sbuf, high, low, acc):
    base = lax.axis_index("dp") * S
    for block in range(S // QB):
        spread_heads(q[pl.ds(block * QB, QB), :].astype(F32) * 0.125, qm)
        qid = ids_of(
            base + block * QB + lax.broadcasted_iota(jnp.int32, (QB, 1), 0), starts
        )
        first, end, whole = key_range(base, block, starts)
        high[...] = jnp.full_like(high, NEG)
        low[...] = jnp.zeros_like(low)
        acc[...] = jnp.zeros_like(acc)

        def scores(kb, carry):
            at = pl.multiple_of(kb * KB, KB)

            def put(masked):
                s = mm_rt(qm[...], win[pl.ds(at, KB), :LW])
                if masked:
                    kid = ids_of(
                        base - OWN0 + at + lax.broadcasted_iota(jnp.int32, (1, KB), 1), starts
                    )
                    bias = jnp.where(qid == kid, 0.0, NEG)
                for head in range(HL):
                    rows = pl.ds(head * QB, QB)
                    one = s[head * QB : (head + 1) * QB, :]
                    if masked:
                        one = one + bias
                    sbuf[kb, rows, :] = one
                    high[rows, :] = jnp.maximum(
                        high[rows, :], jnp.maximum(one[:, :128], one[:, 128:])
                    )

            pl.when(whole(kb))(lambda: put(False))
            pl.when(jnp.logical_not(whole(kb)))(lambda: put(True))
            return carry

        lax.fori_loop(first, end, scores, 0)
        top = jnp.max(high[...], axis=1, keepdims=True)
        high[...] = jnp.broadcast_to(top, high.shape)

        def values(kb, carry):
            at = pl.multiple_of(kb * KB, KB)
            for head in range(HL):
                rows = pl.ds(head * QB, QB)
                v = win[pl.ds(at, KB), pl.ds(LW + half_of(head), 128)]
                p = jnp.exp(sbuf[kb, rows, :] - high[rows, :1])
                low[rows, :] += p[:, :128] + p[:, 128:]
                acc[rows, :] += mm(p.astype(BF), v)
            return carry

        lax.fori_loop(first, end, values, 0)
        total = jnp.sum(low[...], axis=1, keepdims=True)
        inv = 1.0 / total
        out[pl.ds(block * QB, QB), :] = pick_heads(
            lambda head: acc[pl.ds(head * QB, QB), :] * inv[head * QB : (head + 1) * QB, :]
        ).astype(BF)
        flat = jnp.transpose(jnp.broadcast_to(top + jnp.log(total), (HL * QB, 128)))
        lt[pl.ds(block * 8, 8), :] = flat[:8, :]


def attend(starts, q, win):
    return call(
        attend_kernel,
        "attend",
        None,
        [starts, q, win],
        [((S, LW), BF), ((8 * (S // QB), HL * QB), F32)],
        [
            pltpu.VMEM((HL * QB, LW), BF),
            pltpu.VMEM((NB, HL * QB, KB), F32),
            pltpu.VMEM((HL * QB, 128), F32),
            pltpu.VMEM((HL * QB, 128), F32),
            pltpu.VMEM((HL * QB, 128), F32),
        ],
        0,
        limit=24,
        specs=[SM, VM, VM],
    )


def attend_back_kernel(starts, q, win, grad, att, lt, dq, dwin, qm, gm, dqa, dkv):
    base = lax.axis_index("dp") * S
    dkv[...] = jnp.zeros_like(dkv)
    head_row = lax.broadcasted_iota(jnp.int32, (8, LW), 0)
    lane_head = lax.div(lax.broadcasted_iota(jnp.int32, (8, LW), 1), HEAD_DIM)
    sums = (head_row == lane_head).astype(F32)
    for block in range(S // QB):
        rows = pl.ds(block * QB, QB)
        spread_heads(q[rows, :].astype(F32) * 0.125, qm)
        grad_rows = grad[rows, :].astype(F32)
        spread_heads(grad_rows, gm)
        both = grad_rows * att[rows, :].astype(F32)
        by_head = lax.dot_general(
            sums,
            both,
            (((1,), (1,)), ((), ())),
            precision=lax.Precision.HIGHEST,
            preferred_element_type=F32,
        )
        inner = jnp.concatenate([by_head[h : h + 1, :] for h in range(HL)], axis=1)
        logs = lt[pl.ds(block * 8, 1), :]
        qid = ids_of(
            base + block * QB + lax.broadcasted_iota(jnp.int32, (1, QB), 1), starts
        )
        first, end, whole = key_range(base, block, starts)
        dqa[...] = jnp.zeros_like(dqa)

        def one(kb, carry):
            at = pl.multiple_of(kb * KB, KB)

            def put(masked):
                keys = win[pl.ds(at, KB), :LW]
                vals = win[pl.ds(at, KB), LW:]
                st = mm_rt(keys, qm[...]) - logs
                dp = mm_rt(vals, gm[...])
                if masked:
                    kid = ids_of(
                        base - OWN0 + at + lax.broadcasted_iota(jnp.int32, (KB, 1), 0), starts
                    )
                    bias = jnp.where(kid == qid, 0.0, NEG)
                    st = st + jnp.concatenate([bias] * HL, axis=1)
                p = jnp.exp(st)
                ds = (p * (dp - inner)).astype(BF)
                dkv[pl.ds(at, KB), LW:] += mm(p.astype(BF), gm[...])
                dkv[pl.ds(at, KB), :LW] += mm(ds, qm[...])
                for head in range(HL):
                    part = keys[:, half_of(head) : half_of(head) + 128]
                    dqa[pl.ds(head * QB, QB), :] += mm_lt(ds[:, head * QB : (head + 1) * QB], part)

            pl.when(whole(kb))(lambda: put(False))
            pl.when(jnp.logical_not(whole(kb)))(lambda: put(True))
            return carry

        lax.fori_loop(first, end, one, 0)
        dq[rows, :] = (pick_heads(lambda head: dqa[pl.ds(head * QB, QB), :]) * 0.125).astype(BF)
    dwin[...] = dkv[...].astype(BF)


def attend_back(starts, q, win, grad, att, lt):
    return call(
        attend_back_kernel,
        "attend_back",
        None,
        [starts, q, win, grad, att, lt],
        [((S, LW), BF), ((NW, 2 * LW), BF)],
        [
            pltpu.VMEM((HL * QB, LW), BF),
            pltpu.VMEM((HL * QB, LW), BF),
            pltpu.VMEM((HL * QB, 128), F32),
            pltpu.VMEM((NW, 2 * LW), F32),
        ],
        0,
        limit=22,
        specs=[SM] + [VM] * 5,
    )


def outward_part(
    layer, at, wires, att, hidden_in, sc, ob, gain, bias, b1, wp, w1, w2, loads,
    mixed, br1, br2, rows, act, slope, bufs, between=None,
):
    load_p, load_1, load_2 = loads
    scatter = Scatter(wires, at, scatter_refs(bufs, 0))
    load_p.wait()
    scatter.everything(lambda first: mm(att[pl.ds(first, 2 * R), :], wp[...]))
    if between:
        between()
    one = scatter.total()
    br1[...] = one
    mix = hidden_in + sc[layer, 0:1, :] * (one + ob[layer, 0:1, :])
    mixed[...] = mix
    x_hat, _ = normalized(mix)
    rows[pl.ds(at.own, R), :] = (x_hat * gain[layer, 1:2, :] + bias[layer, 1:2, :]).astype(BF)
    gather = Gather(wires, at, rows)

    def hidden(part):
        x = part.load(rows)
        for j in range(F // 256):
            cols = pl.ds(j * 256, 256)
            pre = mm(x, w1[:, cols]) + b1[layer : layer + 1, cols]
            half = 0.5 * (1.0 + lax.erf(pre * (0.5**0.5)))
            part.store(act, (pre * half).astype(BF), cols)
            bell = jnp.exp(-0.5 * pre * pre) * 0.3989422804014327
            part.store(slope, (half + pre * bell).astype(BF), cols)

    load_1.wait()
    scatter = Scatter(wires, at, scatter_refs(bufs, 1))
    gather_hidden_scatter(
        at, gather, scatter, hidden, lambda part: mm(part.load(act), w2[...]), load_2.wait
    )
    two = scatter.total()
    br2[...] = two
    return mix + sc[layer, 1:2, :] * (two + ob[layer, 1:2, :])


OUT_SEMS = AG_SEMS + 2 * RS_SEMS
OUT_WEIGHTS = [pltpu.VMEM((LW, D), BF), pltpu.VMEM((D, F), BF), pltpu.VMEM((F, D), BF)]
OWN = ((R, D), F32)
TALL = ((S, D), BF)


def fetch_out(layer, wp_hbm, w1_hbm, w2_hbm, wp, w1, w2, ls, base):
    return [
        fetch(src.at[layer], dst, ls.at[base + k])
        for k, (src, dst) in enumerate(((wp_hbm, wp), (w1_hbm, w1), (w2_hbm, w2)))
    ]


def between_kernel(
    att, h, sc, ob, gain, bias, b1, b2, wp_hbm, w1_hbm, w2_hbm, w_hbm,
    mixed, br1, br2, nxt, rows_two, act, slope, rows_one, q, win,
    wp, w1, w2, w, relay, *rest,
):
    bufs = rest[:-3]
    ss, rs, ls = rest[-3:]
    at = Place()
    wires = Wires(ss, rs)
    loads = fetch_out(0, wp_hbm, w1_hbm, w2_hbm, wp, w1, w2, ls, 0)
    loads_qkv = fetch_qkv(1, w_hbm, w, ls, 3)
    greet(chain_partners(at))
    after = outward_part(
        0, at, wires, att, h[...].astype(F32), sc, ob, gain, bias, b1, wp, w1, w2, loads,
        mixed, br1, br2, rows_two, act, slope, bufs,
    )
    nxt[...] = after
    inward_part(
        1, at, wires, after, gain, bias, b2, w, loads_qkv, rows_one, q, win, relay
    )
    wires.close()


def between_layers(cid, *ins):
    return call(
        between_kernel, "between_layers", cid, ins,
        [OWN, OWN, OWN, OWN, TALL, TALL, TALL] + IN_OUTS,
        OUT_WEIGHTS + IN_SCRATCH + scatter_scratch(2),
        OUT_SEMS + IN_SEMS,
        limit=36, specs=[VM] * 8 + [ANY] * 4, local=6,
    )


def start_back(layer, at, wires, grad, sc, g2):
    g2[pl.ds(at.own, R), :] = (grad * sc[layer, 1:2, :]).astype(BF)
    return Gather(wires, at, g2)


def back_out_part(
    layer, at, wires, grad, gather, sc, ob, gain, mixed, br1, br2, act, slope, rows, att,
    wp, w1, w2, gmix, gatt, dw2_hbm, dw1_hbm, dwp, vec, fb, dw2, dw1, g2, gp, g1, bufs,
    ls, base, steps,
):
    vec[0:1, :] = jnp.sum(grad * (br2[...] + ob[layer, 1:2, :]), axis=0, keepdims=True)
    vec[1:2, :] = sc[layer, 1:2, :] * jnp.sum(grad, axis=0, keepdims=True)

    def hidden(part):
        x = part.load(g2)
        for j in range(F // 256):
            cols = pl.ds(j * 256, 256)
            up = mm_rt(x, w2[cols, :])
            part.store(gp, (up * part.load(slope, cols).astype(F32)).astype(BF), cols)

    scatter = Scatter(wires, at, bufs)
    gather_hidden_scatter(
        at, gather, scatter, hidden, lambda part: mm_rt(part.load(gp), w1[...]), lambda: None
    )
    steps(0)
    for j in range(D // 256):
        cols = pl.ds(j * 256, 256)
        dw2[cols, :] = mm_lt(g2[:, cols], act[...]).astype(BF)
    write_2 = fetch(dw2, dw2_hbm, ls.at[base])
    steps(1)
    for j in range(D // 256):
        cols = pl.ds(j * 256, 256)
        dw1[cols, :] = mm_lt(rows[:, cols], gp[...]).astype(BF)
    write_1 = fetch(dw1, dw1_hbm, ls.at[base + 1])
    fb[...] = jnp.broadcast_to(jnp.sum(gp[...].astype(F32), axis=0, keepdims=True), fb.shape)
    grad_in, grad_gain, grad_shift = norm_back(
        mixed[...], gain[layer, 1:2, :], scatter.total()
    )
    mix = grad + grad_in
    gmix[...] = mix
    g1[pl.ds(at.own, R), :] = (mix * sc[layer, 0:1, :]).astype(BF)
    gather = Gather(wires, at, g1)
    steps(2)
    vec[2:3, :] = grad_gain
    vec[3:4, :] = grad_shift
    vec[4:5, :] = jnp.sum(mix * (br1[...] + ob[layer, 0:1, :]), axis=0, keepdims=True)
    vec[5:6, :] = sc[layer, 0:1, :] * jnp.sum(mix, axis=0, keepdims=True)
    vec[6:8, :] = jnp.zeros((2, D), F32)
    gather.near()
    gatt[pl.ds(at.near, 2 * R), :] = mm_rt(g1[pl.ds(at.near, 2 * R), :], wp[...]).astype(BF)
    gather.far()
    steps(3)
    gatt[pl.ds(at.far, 2 * R), :] = mm_rt(g1[pl.ds(at.far, 2 * R), :], wp[...]).astype(BF)
    dwp[...] = mm_lt(g1[...], att[...]).astype(BF)
    steps(4)
    write_2.wait()
    write_1.wait()


BACK_OUTS = [
    OWN, ((S, LW), BF), ((D, F), BF), ((D, F), BF), ((D, LW), BF), ((8, D), F32), ((8, F), F32),
]
BACK_OUT_SPECS = [VM, VM, ANY, ANY, VM, VM, VM]
BACK_SCRATCH = [pltpu.VMEM((D, F), BF)] * 2 + [
    pltpu.VMEM((S, D), BF), pltpu.VMEM((S, F), BF), pltpu.VMEM((S, D), BF),
]
BACK_SEMS = 2 * AG_SEMS + RS_SEMS


def turn_kernel(
    att, h, sc, ob, gain, bias, b1, g, wp_hbm, w1_hbm, w2_hbm,
    out, gmix, gatt, dw2_hbm, dw1_hbm, dwp, vec, fb,
    wp, w1, w2, mixed, br1, br2, rows, act, slope, dw2, dw1, g2, gp, g1, *rest,
):
    bufs = rest[:-3]
    ss, rs, ls = rest[-3:]
    layer = 1
    at = Place()
    wires = Wires(ss, rs)
    loads = fetch_out(layer, wp_hbm, w1_hbm, w2_hbm, wp, w1, w2, ls, 0)
    greet([{"tensor": at.mate}, {"tensor": at.cp}])
    started = []
    after = outward_part(
        layer, at, wires, att, h[...].astype(F32), sc, ob, gain, bias, b1, wp, w1, w2, loads,
        mixed, br1, br2, rows, act, slope, bufs,
        lambda: started.append(start_back(layer, at, wires, g[...], sc, g2)),
    )
    out[...] = after.astype(BF)
    back_out_part(
        layer, at, wires, g[...], started[0], sc, ob, gain, mixed, br1, br2, act, slope, rows,
        att, wp, w1, w2, gmix, gatt, dw2_hbm, dw1_hbm, dwp, vec, fb, dw2, dw1, g2, gp, g1,
        scatter_refs(bufs, 2), ls, 3, lambda step: None,
    )
    wires.close()


def turn(cid, *ins):
    return call(
        turn_kernel, "turn", cid, ins,
        [((R, D), BF)] + BACK_OUTS,
        OUT_WEIGHTS
        + [pltpu.VMEM(*OWN)] * 3
        + [pltpu.VMEM(*TALL)] * 3
        + BACK_SCRATCH
        + scatter_scratch(3),
        OUT_SEMS + BACK_SEMS,
        limit=33, specs=[VM] * 8 + [ANY] * 3, local=5, out_specs=[VM] + BACK_OUT_SPECS,
    )


def back_in_part(
    layer, at, wires, dq, dwin, rows, gmix, h, gain, dwp, w, loads, dw, vec, qb, proj, lanes,
    bufs, steps,
):
    da, db, dc, ua, ub, uc, sdb, sdc, sub, suc = lanes
    chain_up, chain_dn = Line(wires, {"dp": at.up}), Line(wires, {"dp": at.dn})
    low3, low2, low1 = OWN0 - 3 * S, OWN0 - 2 * S, OWN0 - S
    high1, high2, high3 = OWN0 + S, OWN0 + 2 * S, OWN0 + 3 * S

    def chunk(ref, k, base=0):
        return ref.at[pl.ds(base + k * R, R)]

    def plus(base, k, other):
        mine = dwin[pl.ds(base + k * R, R), :].astype(F32)
        return (mine + other[pl.ds(k * R, R), :].astype(F32)).astype(BF)

    ups, dns = {}, {}

    def send(n, k, down, up):
        dns[n, k] = chain_dn.send(*down)
        ups[n, k] = chain_up.send(*up)

    def arrive(n, k):
        chain_dn.arrive(dns[n, k])
        chain_up.arrive(ups[n, k])

    def first(k):
        j = 3 - k
        send(
            1, k, (chunk(dwin, k, low3), chunk(da, k)), (chunk(dwin, j, high3), chunk(ua, j))
        )

    def second(k):
        j = 3 - k
        arrive(1, k)
        sdb[pl.ds(k * R, R), :] = plus(low2, k, da)
        sub[pl.ds(j * R, R), :] = plus(high2, j, ua)
        send(2, k, (chunk(sdb, k), chunk(db, k)), (chunk(sub, j), chunk(ub, j)))

    def third(k):
        j = 3 - k
        arrive(2, k)
        sdc[pl.ds(k * R, R), :] = plus(low1, k, db)
        suc[pl.ds(j * R, R), :] = plus(high1, j, ub)
        send(3, k, (chunk(sdc, k), chunk(dc, k)), (chunk(suc, j), chunk(uc, j)))

    for k in (1, 2, 3):
        first(k)
    send(2, 0, (chunk(dwin, 0, low2), chunk(db, 0)), (chunk(dwin, 3, high2), chunk(ub, 3)))
    def into(first, value):
        dw[:, :, :, :, pl.ds(first, value.shape[-1])] = as_blocks(value)

    proj[:, :LW] = dq[...]
    into(3 * LW, dwp[...])
    into(0, mm_lt(rows[...], dq[...]).astype(BF))
    for k in (1, 2, 3):
        second(k)
    for k in range(4):
        third(k)
    for k in range(4):
        arrive(3, k)
    steps(0)
    own = dwin[pl.ds(OWN0, S), :].astype(F32)
    proj[:, LW:] = (own + dc[...].astype(F32) + uc[...].astype(F32)).astype(BF)
    for copy in loads:
        copy.wait()
    scatter = Scatter(wires, at, bufs)
    scatter.everything(lambda first: mm_rt(proj[pl.ds(first, 2 * R), :], w[...]))
    into(LW, mm_lt(rows[...], proj[:, LW:]).astype(BF))
    steps(1)
    qb[...] = jnp.broadcast_to(jnp.sum(proj[...].astype(F32), axis=0, keepdims=True), qb.shape)
    grad_in, grad_gain, grad_shift = norm_back(
        h[...].astype(F32), gain[layer, 0:1, :], scatter.total()
    )
    vec[0:1, :] = grad_gain
    vec[1:2, :] = grad_shift
    vec[2:8, :] = jnp.zeros((6, D), F32)
    return gmix[...] + grad_in


BLOCKS = ((4, 2, 4, RP, 4 * LW), BF)
EIGHT, EIGHT3 = ((8, D), F32), ((8, 3 * LW), F32)
IN_BACK_SCRATCH = (
    [pltpu.VMEM((D, 3 * LW), BF), pltpu.VMEM((S, 3 * LW), BF)]
    + [pltpu.VMEM((S, 2 * LW), BF)] * 10
)
IN_BACK_SEMS = RS_SEMS + 22


def middle_kernel(*refs):
    take = Refs(refs).take
    dq, dwin, rows_one, gmix1, h, gain, dwp1, dw2_1, dw1_1 = take(9)
    sc, ob = take(2)
    late_hbm = take(7)
    wp_hbm, w1_hbm, w2_hbm, w_hbm = take(4)
    vec_in, qb, gmix, gatt, dw2_hbm, dw1_hbm, dwp, vec, fb = take(9)
    sums = take(NP)
    wp, w1, w2, dw2, dw1, g2, gp, g1 = take(8)
    w, proj = take(2)
    lanes = take(10)
    dw = take(1)[0]
    accs = take(NP)
    wide_bufs, narrow_bufs = take(NP * WIDE_REFS), take(NP * NARROW_REFS)
    bufs = take(2 + 2 * SCATTER_REFS)
    late = take(7)
    ss, rs, ls = take(3)
    at = Place()
    wires = Wires(ss, rs)
    loads = fetch_qkv(1, w_hbm, w, ls)
    loads_out = fetch_out(0, wp_hbm, w1_hbm, w2_hbm, wp, w1, w2, ls, 3)
    loads_out += [
        fetch(src, dst, ls.at[8 + 3 * NP + k]) for k, (src, dst) in enumerate(zip(late_hbm, late))
    ]
    mixed, br1, br2, act, slope, rows_two, att = late
    rings = Rings()
    wide = Wide(wires, rings, (dw2_1, dw1_1, dw), wide_bufs, ls, 8)
    narrow = Narrow(wires, rings, accs, narrow_bufs)
    greet(
        [{"tensor": at.mate}, {"tensor": at.cp}, {"dp": at.up}, {"dp": at.dn}]
        + rings.next_to()
        + [rings.other]
    )
    def steps_in(step):
        if step == 0:
            wide.start(0, 1)
        else:
            wide.start(2, 3)
            wide.forward(0, 1)

    def steps_out(step):
        if step == 0:
            wide.finish(accs, 0, 1)
            narrow.start(0, 1)
        elif step == 1:
            wide.finish(accs, 2, 3)
            narrow.start(2, 3)
            narrow.forward(0, 1)
        elif step == 2:
            narrow.forward(2, 3)
            narrow.beyond(0, 1)
        elif step == 3:
            narrow.beyond(2, 3)
        else:
            narrow.finish(sums)

    grad = back_in_part(
        1, at, wires, dq, dwin, rows_one, gmix1, h, gain, dwp1, w, loads, dw, vec_in, qb, proj,
        lanes, scatter_refs(bufs, 0), steps_in,
    )
    gather = start_back(0, at, wires, grad, sc, g2)
    wide.forward(2, 3)
    for copy in loads_out:
        copy.wait()
    back_out_part(
        0, at, wires, grad, gather, sc, ob, gain, mixed, br1, br2, act, slope, rows_two, att,
        wp, w1, w2, gmix, gatt, dw2_hbm, dw1_hbm, dwp, vec, fb, dw2, dw1, g2, gp, g1,
        scatter_refs(bufs, 1), ls, 6, steps_out,
    )
    wires.close()


def middle(cid, *ins):
    return call(
        middle_kernel, "middle", cid, ins,
        [EIGHT, EIGHT3] + BACK_OUTS + reduced_shapes(),
        OUT_WEIGHTS
        + BACK_SCRATCH
        + IN_BACK_SCRATCH
        + [pltpu.VMEM(*BLOCKS)]
        + [pltpu.VMEM(*wide_shape(width, mode)) for _, _, width, mode in PIECES]
        + wide_scratch()
        + narrow_scratch()
        + scatter_scratch(2)
        + [pltpu.VMEM(*OWN)] * 3
        + [pltpu.VMEM(*TALL)] * 3
        + [pltpu.VMEM((S, LW), BF)],
        IN_BACK_SEMS + BACK_SEMS + 13 * NP,
        limit=54,
        specs=[VM] * 7 + [ANY] * 2 + [VM] * 2 + [ANY] * 11,
        local=15 + 3 * NP,
        out_specs=[VM, VM] + BACK_OUT_SPECS + [VM] * NP,
    )


def final_kernel(*refs):
    take = Refs(refs).take
    dq, dwin, rows, gmix, h, gain, dwp = take(7)
    va1, va0, vb1, fb1, fb0, qb1 = take(6)
    dw2, dw1, w_hbm = take(3)
    g, vout = take(2)
    sums = take(NP)
    w, proj = take(2)
    lanes = take(10)
    dw, vec, qb = take(3)
    accs = take(NP)
    wide_bufs, narrow_bufs = take(NP * WIDE_REFS), take(NP * NARROW_REFS)
    vector_bufs = take(6)
    bufs = take(2 + SCATTER_REFS)
    ss, rs, ls = take(3)
    at = Place()
    wires = Wires(ss, rs)
    loads = fetch_qkv(0, w_hbm, w, ls)
    rings = Rings()
    wide = Wide(wires, rings, (dw2, dw1, dw), wide_bufs, ls, 3)
    narrow = Narrow(wires, rings, accs, narrow_bufs)
    vectors = Vectors(wires, at, rings, vector_bufs)
    greet(
        [{"tensor": at.mate}, {"tensor": at.cp}, {"dp": at.up}, {"dp": at.dn}]
        + [*rings.along_y, *rings.along_x, rings.other]
    )

    def steps(step):
        if step == 0:
            wide.start(0, 1)
        else:
            wide.forward(0, 1)
            wide.start(2, 3)

    g[...] = back_in_part(
        0, at, wires, dq, dwin, rows, gmix, h, gain, dwp, w, loads, dw, vec, qb, proj, lanes,
        bufs, steps,
    )
    vectors.fill(((va0, vec, fb0, qb), (va1, vb1, fb1, qb1)))
    wide.forward(2, 3)
    vectors.over_core()
    wide.finish(accs, 0, 1)
    narrow.start(0, 1)
    vectors.over_chip()
    wide.finish(accs, 2, 3)
    narrow.start(2, 3)
    vectors.over_y()
    narrow.forward(0, 1)
    narrow.forward(2, 3)
    vectors.over_x()
    narrow.beyond(0, 1, 2, 3)
    vectors.finish(vout)
    narrow.finish(sums)
    wires.close()


def final(cid, *ins):
    return call(
        final_kernel, "final", cid, ins,
        [OWN, (VEC, F32)] + reduced_shapes(),
        IN_BACK_SCRATCH
        + [pltpu.VMEM(*BLOCKS), pltpu.VMEM(*EIGHT), pltpu.VMEM(*EIGHT3)]
        + [pltpu.VMEM(*wide_shape(width, mode)) for _, _, width, mode in PIECES]
        + wide_scratch()
        + narrow_scratch()
        + vector_scratch()
        + scatter_scratch(1),
        IN_BACK_SEMS + 13 * NP + 9,
        limit=48,
        specs=[VM] * 13 + [ANY] * 3,
        local=3 + 3 * NP,
    )


def shards(
    tokens_in,
    image_starts,
    norm_gain,
    norm_bias,
    qkv_weight,
    qv_bias,
    proj_weight,
    out_bias,
    layer_scale,
    fc1_weight,
    fc1_bias,
    fc2_weight,
    out_grad,
):
    w_qkv = jnp.transpose(qkv_weight, (0, 2, 1, 3))
    norms = (norm_gain, norm_bias)
    out_weights = (proj_weight, fc1_weight, fc2_weight)
    one0, q0, win0 = inward(0, tokens_in, *norms, qv_bias, w_qkv)
    att0, lt0 = attend(image_starts, q0, win0)
    mixed, br1, br2, h1, two0, act, slope, one1, q1, win1 = between_layers(
        1, att0, tokens_in, layer_scale, out_bias, *norms, fc1_bias, qv_bias, *out_weights, w_qkv
    )
    att1, lt1 = attend(image_starts, q1, win1)
    hidden, gmix, gatt, dw2, dw1, dwp, va1, fb1 = turn(
        2, att1, h1, layer_scale, out_bias, *norms, fc1_bias, out_grad, *out_weights
    )
    dq, dwin = attend_back(image_starts, q1, win1, gatt, att1, lt1)
    vb1, qb1, gmix, gatt, dw2, dw1, dwp, va0, fb0, a1, b1, c1, d1 = middle(
        3, dq, dwin, one1, gmix, h1, norm_gain, dwp, as_blocks(dw2), as_blocks(dw1),
        layer_scale, out_bias, mixed, br1, br2, act, slope, two0, att0, *out_weights, w_qkv,
    )
    dq, dwin = attend_back(image_starts, q0, win0, gatt, att0, lt0)
    grad, vec, a0, b0, c0, d0 = final(
        4, dq, dwin, one0, gmix, tokens_in, norm_gain, dwp, va1, va0, vb1, fb1, fb0, qb1,
        as_blocks(dw2), as_blocks(dw1), w_qkv,
    )
    rows = vec[:16].reshape(2, 8, D)
    qkv = jnp.stack(
        [jnp.concatenate([c0, d0[:, :LW]], 1), jnp.concatenate([c1, d1[:, :LW]], 1)]
    )
    return (
        hidden,
        grad,
        jnp.stack([rows[:, 6], rows[:, 2]], 1),
        jnp.stack([rows[:, 7], rows[:, 3]], 1),
        qkv.reshape(2, RP, 3, LW),
        jnp.stack([vec[18:20, :LW], vec[18:20, 2 * LW : 3 * LW]], 1),
        jnp.stack([d0[:, LW:].T, d1[:, LW:].T]),
        jnp.stack([rows[:, 5], rows[:, 1]], 1),
        jnp.stack([rows[:, 4], rows[:, 0]], 1),
        jnp.stack([b0, b1]),
        vec[16:18],
        jnp.stack([a0.T, a1.T]),
    )


def solution(mesh):
    return jax.shard_map(
        shards,
        mesh=mesh,
        in_specs=(
            P(("dp", "tensor"), None),
            P(),
            P(),
            P(),
            P(None, None, None, "tensor"),
            P(None, None, "tensor"),
            P(None, "tensor", None),
            P(),
            P(),
            P(None, None, "tensor"),
            P(None, "tensor"),
            P(None, "tensor", None),
            P(("dp", "tensor"), None),
        ),
        out_specs=(
            P(("dp", "tensor"), None),
            P(("dp", "tensor"), None),
            P(),
            P(),
            P(None, "dp", None, "tensor"),
            P(None, None, "tensor"),
            P(None, "tensor", "dp"),
            P(),
            P(),
            P(None, "dp", "tensor"),
            P(None, "tensor"),
            P(None, "tensor", "dp"),
        ),
        check_vma=False,
    )
```

```python
import functools

import jax
import jax.numpy as jnp
from jax import lax
from jax.experimental import pallas as pl
from jax.experimental.pallas import tpu as pltpu
from jax.sharding import PartitionSpec as P

MESH = pl.DeviceIdType.MESH
BF = jnp.bfloat16
F32 = jnp.float32
VM = pl.BlockSpec(memory_space=pltpu.VMEM)
SM = pl.BlockSpec(memory_space=pltpu.SMEM)
ANY = pl.BlockSpec(memory_space=pl.ANY)

HEAD_DIM = 64
IMG_LEN = 1370
EPS = 1e-06
NEG = -1e30

R = 128
S = 512
D = 1024
LW = 256
HL = LW // HEAD_DIM
F = 1024
TOTAL = 16384
NDP = 32
FAR3 = 384
OWN0 = FAR3 + 2 * S
NW = 2 * OWN0 + S
QB = 256
KB = 256
NB = NW // KB
C = 2
RC = R // C
MB = 1 << 20


def mm(a, b):
    return jnp.dot(a, b, preferred_element_type=F32)


def mm_rt(a, b):
    return lax.dot_general(a, b, (((1,), (1,)), ((), ())), preferred_element_type=F32)


def mm_lt(a, b):
    return lax.dot_general(a, b, (((0,), (0,)), ((), ())), preferred_element_type=F32)


class Place:
    def __init__(self):
        self.t = lax.axis_index("tensor")
        self.core = lax.rem(self.t, 2)
        self.mate = self.t + 1 - 2 * self.core
        self.cp = lax.rem(self.t + 2, 4)
        self.own = pl.multiple_of(self.t * R, R)
        self.opp = pl.multiple_of(self.cp * R, R)
        self.near = pl.multiple_of((self.t - self.core) * R, 2 * R)
        self.far = pl.multiple_of(2 * R - self.near, 2 * R)
        self.dp = lax.axis_index("dp")
        self.up = lax.rem(self.dp + 1, NDP)
        self.dn = lax.rem(self.dp + NDP - 1, NDP)


def greet(devices):
    barrier = pltpu.get_barrier_semaphore()
    for device in devices:
        pl.semaphore_signal(barrier, inc=1, device_id=device, device_id_type=MESH)
    pl.semaphore_wait(barrier, len(devices))


class Wires:
    def __init__(self, send, recv):
        self.send, self.recv, self.count, self.open = send, recv, 0, []

    def push(self, src, dst, device):
        k = self.count
        self.count += 1
        copy = pltpu.make_async_remote_copy(
            src, dst, self.send.at[k], self.recv.at[k], device_id=device, device_id_type=MESH
        )
        copy.start()
        self.open.append(copy)
        return copy

    def left(self, copy):
        copy.wait_send()
        self.open = [c for c in self.open if c is not copy]

    def close(self):
        for copy in self.open:
            copy.wait_send()


class Chain:
    def __init__(self, wires, at, up, relay):
        self.wires, self.at, self.relay = wires, at, relay
        y = lax.rem(at.dp, 4)
        self.edge = (y == 3) if up else (y == 0)
        self.plain = jnp.logical_not(self.edge)
        self.device = at.up if up else at.dn
        self.items = []

    def plan(self, src, dst, partner_dst=None, when=True, partner_when=True):
        wires, at = self.wires, self.at
        slot = self.relay.at[len(self.items)]
        k = wires.count
        wires.count += 2

        def copy(source, target, n, device):
            return lambda: pltpu.make_async_remote_copy(
                source, target, wires.send.at[n], wires.recv.at[n],
                device_id=device, device_id_type=MESH,
            )

        direct = copy(src, dst, k, {"dp": self.device})
        first = copy(src, slot, k + 1, {"tensor": at.cp})
        target = dst if partner_dst is None else partner_dst
        second = copy(slot, target, k, {"dp": self.device, "tensor": at.cp})
        item = (direct, first, second, when, partner_when)
        self.items.append(item)
        return item

    def send(self, item):
        direct, first, _, when, _ = item
        pl.when(self.plain & when)(lambda: direct().start())
        pl.when(self.edge & when)(lambda: first().start())

    def hand_on(self, item):
        _, first, second, _, partner_when = item

        @pl.when(self.edge & partner_when)
        def _():
            first().wait_recv()
            second().start()

    def arrive(self, item):
        pl.when(item[3])(lambda: item[0]().wait_recv())

    def close(self):
        for direct, first, second, when, partner_when in self.items:
            pl.when(self.plain & when)(lambda c=direct: c().wait_send())
            pl.when(self.edge & when)(lambda c=first: c().wait_send())
            pl.when(self.edge & partner_when)(lambda c=second: c().wait_send())


class Line:
    def __init__(self, wires, device):
        self.wires, self.device = wires, device

    def send(self, src, dst):
        return self.wires.push(src, dst, self.device)

    def arrive(self, copy):
        copy.wait_recv()


def chain_partners(at):
    return [
        {"tensor": at.mate},
        {"tensor": at.cp},
        {"dp": at.up},
        {"dp": at.dn},
        {"dp": at.up, "tensor": at.cp},
        {"dp": at.dn, "tensor": at.cp},
    ]


AG_SEMS = 2 * C + 1
RS_SEMS = 2 * C + 1


class Gather:
    def __init__(self, wires, at, buf):
        self.wires, self.at, self.buf = wires, at, buf
        own = at.own
        self.across, self.passed = [], []
        for c in range(C):
            part = buf.at[pl.ds(own + c * RC, RC)]
            self.across.append(wires.push(part, part, {"tensor": at.cp}))
        part = buf.at[pl.ds(own, R)]
        self.beside = wires.push(part, part, {"tensor": at.mate})

    def near(self):
        self.beside.wait_recv()

    def take(self, c):
        self.across[c].wait_recv()
        part = self.buf.at[pl.ds(self.at.opp + c * RC, RC)]
        self.passed.append(self.wires.push(part, part, {"tensor": self.at.mate}))

    def arrived(self, c):
        self.passed[c].wait_recv()

    def far(self):
        for c in range(C):
            self.take(c)
        for c in range(C):
            self.arrived(c)


class Rows:
    def __init__(self, at, chunk=None):
        if chunk is None:
            self.parts = [(at.near, 2 * R)]
        else:
            self.parts = [
                (pl.multiple_of(at.far + core * R + chunk * RC, RC), RC) for core in range(2)
            ]

    def load(self, ref, cols=slice(None)):
        parts = [ref[pl.ds(first, count), cols] for first, count in self.parts]
        return parts[0] if len(parts) == 1 else jnp.concatenate(parts, axis=0)

    def store(self, ref, value, cols=slice(None)):
        at = 0
        for first, count in self.parts:
            ref[pl.ds(first, count), cols] = value[at : at + count]
            at += count


class Scatter:
    def __init__(self, wires, at, bufs):
        self.wires, self.at = wires, at
        self.far, self.near = bufs[:2]
        self.send1, self.recv1, self.send2, self.recv2, self.send3, self.recv3 = bufs[2:]
        self.ones, self.twos = [], []

    def put(self, c, value):
        for core in range(2):
            self.far[pl.ds(core * R + c * RC, RC), :] = value[core * RC : (core + 1) * RC]

    def first(self, c):
        at = self.at
        rows = pl.ds(c * RC, RC)
        src = pl.ds(pl.multiple_of((1 - at.core) * R + c * RC, RC), RC)
        self.send1[rows, :] = self.far[src, :].astype(BF)
        self.ones.append(
            self.wires.push(self.send1.at[rows], self.recv1.at[rows], {"tensor": at.mate})
        )

    def second(self, c):
        at = self.at
        rows = pl.ds(c * RC, RC)
        src = pl.ds(pl.multiple_of(at.core * R + c * RC, RC), RC)
        self.ones[c].wait_recv()
        total = self.far[src, :] + self.recv1[rows, :].astype(F32)
        self.send2[rows, :] = total.astype(BF)
        self.twos.append(
            self.wires.push(self.send2.at[rows], self.recv2.at[rows], {"tensor": at.cp})
        )

    def third(self):
        at = self.at
        src = pl.ds(pl.multiple_of((1 - at.core) * R, R), R)
        self.send3[...] = self.near[src, :].astype(BF)
        self.three = self.wires.push(self.send3, self.recv3, {"tensor": at.mate})

    def everything(self, product):
        self.far[...] = product(self.at.far)
        for c in range(C):
            self.first(c)
        self.near[...] = product(self.at.near)
        for c in range(C):
            self.second(c)
        self.third()

    def total(self):
        self.three.wait_recv()
        for copy in self.twos:
            copy.wait_recv()
        own = self.near[pl.ds(pl.multiple_of(self.at.core * R, R), R), :]
        return own + self.recv3[...].astype(F32) + self.recv2[...].astype(F32)


def gather_hidden_scatter(at, gather, scatter, hidden, product, ready):
    gather.near()
    hidden(Rows(at))
    ready()
    gather.take(0)
    gather.arrived(0)
    rows = [Rows(at, c) for c in range(C)]
    hidden(rows[0])
    gather.take(1)
    scatter.put(0, product(rows[0]))
    scatter.first(0)
    gather.arrived(1)
    hidden(rows[1])
    scatter.second(0)
    scatter.put(1, product(rows[1]))
    scatter.first(1)
    scatter.near[...] = product(Rows(at))
    scatter.second(1)
    scatter.third()


SCATTER_REFS = 6


def scatter_scratch(count):
    return [pltpu.VMEM((2 * R, D), F32)] * 2 + [pltpu.VMEM((R, D), BF)] * (6 * count)


def scatter_refs(bufs, which):
    first = 2 + SCATTER_REFS * which
    return [*bufs[:2], *bufs[first : first + SCATTER_REFS]]


class Refs:
    def __init__(self, refs):
        self.refs = list(refs)

    def take(self, count):
        out, self.refs = self.refs[:count], self.refs[count:]
        return out


def fetch(src, dst, sem):
    copy = pltpu.make_async_copy(src, dst, sem)
    copy.start()
    return copy


def fetch_qkv(layer, w, buf, ls, base=0):
    return [
        fetch(w.at[layer, k], buf.at[:, pl.ds(k * LW, LW)], ls.at[base + k]) for k in range(3)
    ]


def normalized(v):
    centered = v - jnp.mean(v, axis=-1, keepdims=True)
    scale = lax.rsqrt(jnp.mean(centered * centered, axis=-1, keepdims=True) + EPS)
    return centered * scale, scale


def norm_back(v, gain, grad):
    x_hat, scale = normalized(v)
    u = grad * gain
    grad_in = scale * (
        u
        - jnp.mean(u, axis=-1, keepdims=True)
        - x_hat * jnp.mean(u * x_hat, axis=-1, keepdims=True)
    )
    return (
        grad_in,
        jnp.sum(grad * x_hat, axis=0, keepdims=True),
        jnp.sum(grad, axis=0, keepdims=True),
    )


def call(kernel, name, cid, ins, outs, scratch, sems, limit, specs=None, local=0, out_specs=None):
    shapes = [jax.ShapeDtypeStruct(shape, dtype) for shape, dtype in outs]
    extra = []
    if sems:
        extra = [pltpu.SemaphoreType.DMA((sems,)), pltpu.SemaphoreType.DMA((sems,))]
    if local:
        extra.append(pltpu.SemaphoreType.DMA((local,)))
    params = dict(vmem_limit_bytes=limit * MB)
    if cid is not None:
        params.update(collective_id=cid, has_side_effects=True)
    return pl.pallas_call(
        kernel,
        out_shape=shapes,
        in_specs=specs or [VM] * len(ins),
        out_specs=out_specs or [VM] * len(outs),
        scratch_shapes=list(scratch) + extra,
        compiler_params=pltpu.CompilerParams(**params),
        name=name,
    )(*ins)


class Ring:
    def __init__(self, wires, chunk, mine, side_up, side_dn, place, bufs):
        self.wires, self.chunk = wires, chunk
        self.mine, self.side_up, self.side_dn = mine, side_up, side_dn
        self.me, self.up, self.dn = place
        self.from_dn, self.from_up, self.send_up, self.send_dn, self.last_dn, self.last_up = bufs

    def half(self, ref, k):
        width = ref.shape[-1] // 2
        return ref.at[..., pl.ds(k * width, width)]

    def position(self, step):
        return lax.rem(self.me + step, 4)

    def start(self):
        push, chunk = self.wires.push, self.chunk
        p1, p2, p3 = self.position(1), self.position(2), self.position(3)
        self.a = push(chunk(p2, 0), self.from_dn, self.up)
        self.b = push(chunk(p2, 1), self.from_up, self.dn)
        self.c = push(chunk(p1, 1), self.half(self.last_dn, 1), self.up)
        self.d = push(chunk(p3, 0), self.half(self.last_up, 0), self.dn)

    def forward(self):
        push = self.wires.push
        self.a.wait_recv()
        total = self.side_up()[...].astype(F32) + self.from_dn[...].astype(F32)
        self.send_up[...] = total.astype(BF)
        self.e = push(self.send_up, self.half(self.last_dn, 0), self.up)
        self.b.wait_recv()
        total = self.side_dn()[...].astype(F32) + self.from_up[...].astype(F32)
        self.send_dn[...] = total.astype(BF)
        self.f = push(self.send_dn, self.half(self.last_up, 1), self.dn)

    def finish(self, out):
        for copy in (self.c, self.d, self.e, self.f):
            copy.wait_recv()
        part = self.mine()[...].astype(F32)
        out[...] = (
            part + self.last_dn[...].astype(F32) + self.last_up[...].astype(F32)
        ).astype(out.dtype)


PIECES = ((0, 0, F, 0), (1, 0, F, 1), (2, 0, 2 * LW, 0), (2, 2 * LW, 2 * LW, 1))
RP = R // 4
NP = len(PIECES)


class Rings:
    def __init__(self):
        i = lax.axis_index("dp")
        self.y = y = lax.rem(i, 4)
        self.x = lax.div(i, 8)
        self.zh = zh = lax.rem(lax.div(i, 4), 2)
        self.along_y = [{"dp": i - y + lax.rem(y + k, 4)} for k in (1, 2, 3)]
        self.along_x = [{"dp": lax.rem(i + 8 * k, 32)} for k in (1, 2, 3)]
        self.other = {"dp": i + 4 - 8 * zh}
        ring_y = (y, self.along_y[0], self.along_y[2])
        ring_x = (self.x, self.along_x[0], self.along_x[2])
        self.order = [(ring_y, ring_x), (ring_x, ring_y)]

    def next_to(self):
        return [*self.along_y[::2], *self.along_x[::2]]


def ring_scratch(lead, width):
    half = pltpu.VMEM((*lead, width // 2), BF)
    full = pltpu.VMEM((*lead, width), BF)
    return [half, half, half, half, full, full]


def wide_shape(width, mode):
    return ((4, 2, RP, width) if mode == 0 else (2, 4, RP, width), BF)


WIDE_REFS, NARROW_REFS = 9, 8


def wide_scratch():
    out = []
    for _, _, width, mode in PIECES:
        lead = wide_shape(width, mode)[0][:3]
        half = pltpu.VMEM((*lead, width // 2), BF)
        out += ring_scratch(lead, width) + [pltpu.VMEM((*lead, width), BF), half, half]
    return out


def narrow_scratch():
    out = []
    for _, _, width, _ in PIECES:
        small, rest = pltpu.VMEM((2, RP, width), BF), pltpu.VMEM((RP, width), BF)
        out += ring_scratch((2, RP), width) + [small, rest]
    return out


def reduced_shapes():
    return [((RP, width), F32) for _, _, width, _ in PIECES]


def as_blocks(w):
    return w.reshape(4, 2, 4, RP, w.shape[-1])


class Wide:
    def __init__(self, wires, rings, ins, bufs, ls, first_sem):
        self.rings, self.loads = [], []
        for k, (which, column, width, mode) in enumerate(PIECES):
            refs = bufs[k * WIDE_REFS : (k + 1) * WIDE_REFS]
            mine, side_up, side_dn = refs[6:9]
            w = ins[which]

            def chunk(pos, half, w=w, mode=mode, column=column, size=width // 2):
                cols = pl.ds(column + half * size, size)
                return w.at[:, :, pos, :, cols] if mode == 0 else w.at[pos, :, :, :, cols]

            place = rings.order[mode][0]
            me = place[0]
            cols = pl.ds(column, width)
            whole = w.at[:, :, me, :, cols] if mode == 0 else w.at[me, :, :, :, cols]
            parts = (
                (chunk(lax.rem(me + 1, 4), 0), side_up),
                (chunk(lax.rem(me + 3, 4), 1), side_dn),
                (whole, mine),
            )
            sems = [ls.at[first_sem + 3 * k + j] for j in range(3)]
            self.loads.append(
                [pltpu.make_async_copy(src, dst, sem) for (src, dst), sem in zip(parts, sems)]
            )
            self.rings.append(
                Ring(
                    wires, chunk, lambda r=mine: r, lambda r=side_up: r, lambda r=side_dn: r,
                    place, refs[0:6],
                )
            )

    def start(self, *ks):
        for k in ks:
            for copy in self.loads[k]:
                copy.start()
            self.rings[k].start()

    def forward(self, *ks):
        for k in ks:
            for copy in self.loads[k]:
                copy.wait()
            self.rings[k].forward()

    def finish(self, accs, *ks):
        for k in ks:
            self.rings[k].finish(accs[k])


class Narrow:
    def __init__(self, wires, rings, accs, bufs):
        self.wires, self.rings, self.parts, self.last = wires, [], [], {}
        self.zh, self.other = rings.zh, rings.other
        for k, (_, _, width, mode) in enumerate(PIECES):
            refs = bufs[k * NARROW_REFS : (k + 1) * NARROW_REFS]
            acc = accs[k]
            place = rings.order[mode][1]

            def chunk(pos, half, acc=acc, mode=mode, size=width // 2):
                cols = pl.ds(half * size, size)
                return acc.at[pos, :, :, cols] if mode == 0 else acc.at[:, pos, :, cols]

            def mine(acc=acc, mode=mode, pos=place[0]):
                return acc.at[pos] if mode == 0 else acc.at[:, pos]

            self.rings.append(
                Ring(
                    wires, chunk, mine,
                    lambda n=chunk, p=lax.rem(place[0] + 1, 4): n(p, 0),
                    lambda n=chunk, p=lax.rem(place[0] + 3, 4): n(p, 1),
                    place, refs[0:6],
                )
            )
            self.parts.append(refs[6:8])

    def start(self, *ks):
        for k in ks:
            self.rings[k].start()

    def forward(self, *ks):
        for k in ks:
            self.rings[k].forward()

    def beyond(self, *ks):
        for k in ks:
            small, rest = self.parts[k]
            self.rings[k].finish(small)
            self.last[k] = self.wires.push(small.at[1 - self.zh], rest, self.other)

    def finish(self, outs):
        for k, out in enumerate(outs):
            small, rest = self.parts[k]
            self.last[k].wait_recv()
            out[...] = small[self.zh].astype(F32) + rest[...].astype(F32)


VEC = (24, D)


def vector_scratch():
    few, whole, four = (
        pltpu.VMEM((16, D), F32), pltpu.VMEM(VEC, F32), pltpu.VMEM((4, *VEC), F32),
    )
    return [whole, few, few, four, four, whole]


class Vectors:
    def __init__(self, wires, at, rings, bufs):
        self.wires, self.at, self.rings = wires, at, rings
        self.vec, self.vmate, self.vcp, self.vy, self.vx, self.vz = bufs

    def fill(self, layers):
        vec = self.vec
        vec[...] = jnp.zeros_like(vec)
        for k, (va, vb, fb, qb) in enumerate(layers):
            vec[8 * k : 8 * k + 6, :] = va[0:6, :]
            vec[8 * k + 6 : 8 * k + 8, :] = vb[0:2, :]
            vec[16 + k : 17 + k, :] = fb[0:1, :]
            vec[18 + k : 19 + k, : 3 * LW] = qb[0:1, :]
        self.one = self.wires.push(vec.at[pl.ds(0, 16)], self.vmate, {"tensor": self.at.mate})

    def over_core(self):
        vec = self.vec
        self.one.wait_recv()
        self.wires.left(self.one)
        vec[0:16, :] = vec[0:16, :] + self.vmate[...]
        self.two = self.wires.push(vec.at[pl.ds(0, 16)], self.vcp, {"tensor": self.at.cp})

    def over_chip(self):
        vec, vy, y = self.vec, self.vy, self.rings.y
        self.two.wait_recv()
        vy[y] = vec[...]
        vy[y, 0:16, :] = vec[0:16, :] + self.vcp[...]
        self.sent = [self.wires.push(vy.at[y], vy.at[y], d) for d in self.rings.along_y]

    def over_y(self):
        vx, vy, x = self.vx, self.vy, self.rings.x
        for copy in self.sent:
            copy.wait_recv()
        vx[x] = vy[0] + vy[1] + vy[2] + vy[3]
        self.sent = [self.wires.push(vx.at[x], vx.at[x], d) for d in self.rings.along_x]

    def over_x(self):
        vec, vx = self.vec, self.vx
        for copy in self.sent:
            copy.wait_recv()
        self.wires.left(self.two)
        vec[...] = vx[0] + vx[1] + vx[2] + vx[3]
        self.last = self.wires.push(vec, self.vz, self.rings.other)

    def finish(self, out):
        self.last.wait_recv()
        out[...] = self.vec[...] + self.vz[...]


def inward_part(layer, at, wires, hidden, gain, bias, b2, w, loads, rows, q, win, relay):
    x_hat, _ = normalized(hidden)
    rows[pl.ds(at.own, R), :] = (x_hat * gain[layer, 0:1, :] + bias[layer, 0:1, :]).astype(BF)
    gather = Gather(wires, at, rows)

    def project(first):
        out = mm(rows[pl.ds(first, 2 * R), :], w[...])
        q[pl.ds(first, 2 * R), :] = (out[:, :LW] + b2[layer, 0:1, :]).astype(BF)
        win[pl.ds(OWN0 + first, 2 * R), :LW] = out[:, LW : 2 * LW].astype(BF)
        win[pl.ds(OWN0 + first, 2 * R), LW:] = (out[:, 2 * LW :] + b2[layer, 1:2, :]).astype(BF)

    def part(first):
        return win.at[pl.ds(pl.multiple_of(first, R), R)]

    offs = [at.near, at.near + R, at.far, at.far + R]
    others = offs[2:] + offs[:2]
    chain_up, chain_dn = Chain(wires, at, True, relay), Chain(wires, at, False, relay)
    ups, dns = {}, {}
    for n in range(1, 4):
        low, high = OWN0 - n * S, OWN0 + n * S
        for k, (own, other) in enumerate(zip(offs, others)):
            if n < 3:
                ups[n, k] = chain_up.plan(part(low + S + own), part(low + own), part(low + other))
                dns[n, k] = chain_dn.plan(
                    part(high - S + own), part(high + own), part(high + other)
                )
                continue
            ups[n, k] = chain_up.plan(
                part(low + S + own),
                part(jnp.maximum(low + own, 0)),
                part(jnp.maximum(low + other, 0)),
                own > 0,
                other > 0,
            )
            dns[n, k] = chain_dn.plan(
                part(high - S + own),
                part(jnp.minimum(high + own, NW - R)),
                part(jnp.minimum(high + other, NW - R)),
                own < S - R,
                other < S - R,
            )

    def hop(n, *ks):
        for k in ks:
            chain_up.send(ups[n, k])
            chain_dn.send(dns[n, k])

    for copy in loads:
        copy.wait()
    gather.near()
    project(at.near)
    hop(1, 0, 1)
    gather.far()
    for k in range(2):
        chain_up.hand_on(ups[1, k])
        chain_dn.hand_on(dns[1, k])
    project(at.far)
    hop(1, 2, 3)

    def hand_on(n, *ks):
        for k in ks:
            chain_up.hand_on(ups[n, k])
            chain_dn.hand_on(dns[n, k])

    def onward(n, *ks):
        for k in ks:
            chain_up.arrive(ups[n, k])
            chain_dn.arrive(dns[n, k])
            if n < 3:
                hop(n + 1, k)

    onward(1, 0, 1)
    hand_on(1, 2, 3)
    hand_on(2, 0, 1)
    onward(1, 2, 3)
    onward(2, 0, 1)
    hand_on(2, 2, 3)
    hand_on(3, 0, 1)
    onward(2, 2, 3)
    hand_on(3, 2, 3)
    onward(3, 0, 1, 2, 3)
    chain_up.close()
    chain_dn.close()


IN_OUTS = [((S, D), BF), ((S, LW), BF), ((NW, 2 * LW), BF)]
IN_SCRATCH = [pltpu.VMEM((D, 3 * LW), BF), pltpu.VMEM((12, R, 2 * LW), BF)]
IN_SEMS = AG_SEMS + 48


def inward_kernel(h, gain, bias, b2, w_hbm, rows, q, win, w, relay, ss, rs, ls):
    at = Place()
    wires = Wires(ss, rs)
    loads = fetch_qkv(0, w_hbm, w, ls)
    greet(chain_partners(at))
    inward_part(
        0, at, wires, h[...].astype(F32), gain, bias, b2, w, loads, rows, q, win, relay
    )
    wires.close()


def inward(cid, *ins):
    return call(
        inward_kernel, "inward", cid, ins, IN_OUTS, IN_SCRATCH, IN_SEMS,
        limit=14, specs=[VM] * 4 + [ANY], local=3,
    )


def ids_of(position, starts):
    total = jnp.zeros_like(position)
    for k in range(starts.shape[0]):
        first = starts[k]
        total += (position >= first).astype(jnp.int32)
        total += (position >= first + IMG_LEN).astype(jnp.int32)
    return jnp.where((position >= 0) & (position < TOTAL), total, -1)


def key_range(base, block, starts):
    first = base + block * QB
    last = first + QB - 1
    low, high = jnp.int32(0), jnp.int32(TOTAL)
    for k in range(starts.shape[0]):
        for edge in (starts[k], starts[k] + IMG_LEN):
            low = jnp.where(edge <= first, jnp.maximum(low, edge), low)
            high = jnp.where(edge > last, jnp.minimum(high, edge), high)
    edge = jnp.bool_(False)
    for k in range(starts.shape[0]):
        for at in (starts[k], starts[k] + IMG_LEN):
            edge = edge | ((at > first) & (at <= last))
    low = jnp.maximum(low - base + OWN0, 0)
    high = jnp.minimum(high - base + OWN0, NW)
    start = lax.div(low, 128) * 128
    tiles = lax.div(high - start + KB - 1, KB)
    start = jnp.minimum(start, NW - tiles * KB)
    whole = lambda at: jnp.logical_not(edge) & (at >= low) & (at + KB <= high)
    return start, tiles, whole


def spread_heads(value, out):
    lane = lax.broadcasted_iota(jnp.int32, (QB, LW), 1)
    for head in range(HL):
        mine = (lane >= head * HEAD_DIM) & (lane < (head + 1) * HEAD_DIM)
        out[pl.ds(head * QB, QB), :] = jnp.where(mine, value, 0.0).astype(BF)


def half_of(head):
    return head * HEAD_DIM // 128 * 128


def pick_heads(parts):
    lane = lax.broadcasted_iota(jnp.int32, (QB, 128), 1)
    halves = [
        jnp.where(lane < HEAD_DIM, parts(head), parts(head + 1)) for head in range(0, HL, 2)
    ]
    return jnp.concatenate(halves, axis=1)


def attend_kernel(starts, q, win, out, lt, qm, sbuf, high, low, acc):
    base = lax.axis_index("dp") * S
    for block in range(S // QB):
        spread_heads(q[pl.ds(block * QB, QB), :].astype(F32) * 0.125, qm)
        qid = ids_of(
            base + block * QB + lax.broadcasted_iota(jnp.int32, (QB, 1), 0), starts
        )
        start, tiles, whole = key_range(base, block, starts)
        high[...] = jnp.full_like(high, NEG)
        low[...] = jnp.zeros_like(low)
        acc[...] = jnp.zeros_like(acc)

        def scores(kb, carry):
            at = pl.multiple_of(start + kb * KB, 128)

            def put(masked):
                s = mm_rt(qm[...], win[pl.ds(at, KB), :LW])
                if masked:
                    kid = ids_of(
                        base - OWN0 + at + lax.broadcasted_iota(jnp.int32, (1, KB), 1), starts
                    )
                    bias = jnp.where(qid == kid, 0.0, NEG)
                for head in range(HL):
                    rows = pl.ds(head * QB, QB)
                    one = s[head * QB : (head + 1) * QB, :]
                    if masked:
                        one = one + bias
                    sbuf[kb, rows, :] = one
                    high[rows, :] = jnp.maximum(
                        high[rows, :], jnp.maximum(one[:, :128], one[:, 128:])
                    )

            pl.when(whole(at))(lambda: put(False))
            pl.when(jnp.logical_not(whole(at)))(lambda: put(True))
            return carry

        lax.fori_loop(0, tiles, scores, 0)
        top = jnp.max(high[...], axis=1, keepdims=True)
        high[...] = jnp.broadcast_to(top, high.shape)

        def values(kb, carry):
            at = pl.multiple_of(start + kb * KB, 128)
            for head in range(HL):
                rows = pl.ds(head * QB, QB)
                v = win[pl.ds(at, KB), pl.ds(LW + half_of(head), 128)]
                p = jnp.exp(sbuf[kb, rows, :] - high[rows, :1])
                low[rows, :] += p[:, :128] + p[:, 128:]
                acc[rows, :] += mm(p.astype(BF), v)
            return carry

        lax.fori_loop(0, tiles, values, 0)
        total = jnp.sum(low[...], axis=1, keepdims=True)
        inv = 1.0 / total
        out[pl.ds(block * QB, QB), :] = pick_heads(
            lambda head: acc[pl.ds(head * QB, QB), :] * inv[head * QB : (head + 1) * QB, :]
        ).astype(BF)
        flat = jnp.transpose(jnp.broadcast_to(top + jnp.log(total), (HL * QB, 128)))
        lt[pl.ds(block * 8, 8), :] = flat[:8, :]


def attend(starts, q, win):
    return call(
        attend_kernel,
        "attend",
        None,
        [starts, q, win],
        [((S, LW), BF), ((8 * (S // QB), HL * QB), F32)],
        [
            pltpu.VMEM((HL * QB, LW), BF),
            pltpu.VMEM((NB, HL * QB, KB), F32),
            pltpu.VMEM((HL * QB, 128), F32),
            pltpu.VMEM((HL * QB, 128), F32),
            pltpu.VMEM((HL * QB, 128), F32),
        ],
        0,
        limit=24,
        specs=[SM, VM, VM],
    )


def attend_back_kernel(starts, q, win, grad, att, lt, dq, dwin, qm, gm, dqa, dkv):
    base = lax.axis_index("dp") * S
    dkv[...] = jnp.zeros_like(dkv)
    head_row = lax.broadcasted_iota(jnp.int32, (8, LW), 0)
    lane_head = lax.div(lax.broadcasted_iota(jnp.int32, (8, LW), 1), HEAD_DIM)
    sums = (head_row == lane_head).astype(F32)
    for block in range(S // QB):
        rows = pl.ds(block * QB, QB)
        spread_heads(q[rows, :].astype(F32) * 0.125, qm)
        grad_rows = grad[rows, :].astype(F32)
        spread_heads(grad_rows, gm)
        both = grad_rows * att[rows, :].astype(F32)
        by_head = lax.dot_general(
            sums,
            both,
            (((1,), (1,)), ((), ())),
            precision=lax.Precision.HIGHEST,
            preferred_element_type=F32,
        )
        inner = jnp.concatenate([by_head[h : h + 1, :] for h in range(HL)], axis=1)
        logs = lt[pl.ds(block * 8, 1), :]
        qid = ids_of(
            base + block * QB + lax.broadcasted_iota(jnp.int32, (1, QB), 1), starts
        )
        start, tiles, whole = key_range(base, block, starts)
        dqa[...] = jnp.zeros_like(dqa)

        def one(kb, carry):
            at = pl.multiple_of(start + kb * KB, 128)

            def put(masked):
                keys = win[pl.ds(at, KB), :LW]
                vals = win[pl.ds(at, KB), LW:]
                st = mm_rt(keys, qm[...]) - logs
                dp = mm_rt(vals, gm[...])
                if masked:
                    kid = ids_of(
                        base - OWN0 + at + lax.broadcasted_iota(jnp.int32, (KB, 1), 0), starts
                    )
                    bias = jnp.where(kid == qid, 0.0, NEG)
                    st = st + jnp.concatenate([bias] * HL, axis=1)
                p = jnp.exp(st)
                ds = (p * (dp - inner)).astype(BF)
                dkv[pl.ds(at, KB), LW:] += mm(p.astype(BF), gm[...])
                dkv[pl.ds(at, KB), :LW] += mm(ds, qm[...])
                for head in range(HL):
                    part = keys[:, half_of(head) : half_of(head) + 128]
                    dqa[pl.ds(head * QB, QB), :] += mm_lt(ds[:, head * QB : (head + 1) * QB], part)

            pl.when(whole(at))(lambda: put(False))
            pl.when(jnp.logical_not(whole(at)))(lambda: put(True))
            return carry

        lax.fori_loop(0, tiles, one, 0)
        dq[rows, :] = (pick_heads(lambda head: dqa[pl.ds(head * QB, QB), :]) * 0.125).astype(BF)
    dwin[...] = dkv[...].astype(BF)


def attend_back(starts, q, win, grad, att, lt):
    return call(
        attend_back_kernel,
        "attend_back",
        None,
        [starts, q, win, grad, att, lt],
        [((S, LW), BF), ((NW, 2 * LW), BF)],
        [
            pltpu.VMEM((HL * QB, LW), BF),
            pltpu.VMEM((HL * QB, LW), BF),
            pltpu.VMEM((HL * QB, 128), F32),
            pltpu.VMEM((NW, 2 * LW), F32),
        ],
        0,
        limit=22,
        specs=[SM] + [VM] * 5,
    )


def outward_part(
    layer, at, wires, att, hidden_in, sc, ob, gain, bias, b1, wp, w1, w2, loads,
    mixed, br1, br2, rows, act, slope, bufs, between=None,
):
    load_p, load_1, load_2 = loads
    scatter = Scatter(wires, at, scatter_refs(bufs, 0))
    load_p.wait()
    scatter.everything(lambda first: mm(att[pl.ds(first, 2 * R), :], wp[...]))
    if between:
        between()
    one = scatter.total()
    br1[...] = one
    mix = hidden_in + sc[layer, 0:1, :] * (one + ob[layer, 0:1, :])
    mixed[...] = mix
    x_hat, _ = normalized(mix)
    rows[pl.ds(at.own, R), :] = (x_hat * gain[layer, 1:2, :] + bias[layer, 1:2, :]).astype(BF)
    gather = Gather(wires, at, rows)

    def hidden(part):
        x = part.load(rows)
        for j in range(F // 256):
            cols = pl.ds(j * 256, 256)
            pre = mm(x, w1[:, cols]) + b1[layer : layer + 1, cols]
            half = 0.5 * (1.0 + lax.erf(pre * (0.5**0.5)))
            part.store(act, (pre * half).astype(BF), cols)
            bell = jnp.exp(-0.5 * pre * pre) * 0.3989422804014327
            part.store(slope, (half + pre * bell).astype(BF), cols)

    load_1.wait()
    scatter = Scatter(wires, at, scatter_refs(bufs, 1))
    gather_hidden_scatter(
        at, gather, scatter, hidden, lambda part: mm(part.load(act), w2[...]), load_2.wait
    )
    two = scatter.total()
    br2[...] = two
    return mix + sc[layer, 1:2, :] * (two + ob[layer, 1:2, :])


OUT_SEMS = AG_SEMS + 2 * RS_SEMS
OUT_WEIGHTS = [pltpu.VMEM((LW, D), BF), pltpu.VMEM((D, F), BF), pltpu.VMEM((F, D), BF)]
OWN = ((R, D), F32)
TALL = ((S, D), BF)


def fetch_out(layer, wp_hbm, w1_hbm, w2_hbm, wp, w1, w2, ls, base):
    return [
        fetch(src.at[layer], dst, ls.at[base + k])
        for k, (src, dst) in enumerate(((wp_hbm, wp), (w1_hbm, w1), (w2_hbm, w2)))
    ]


def between_kernel(
    att, h, sc, ob, gain, bias, b1, b2, wp_hbm, w1_hbm, w2_hbm, w_hbm,
    mixed, br1, br2, nxt, rows_two, act, slope, rows_one, q, win,
    wp, w1, w2, w, relay, *rest,
):
    bufs = rest[:-3]
    ss, rs, ls = rest[-3:]
    at = Place()
    wires = Wires(ss, rs)
    loads = fetch_out(0, wp_hbm, w1_hbm, w2_hbm, wp, w1, w2, ls, 0)
    loads_qkv = fetch_qkv(1, w_hbm, w, ls, 3)
    greet(chain_partners(at))
    after = outward_part(
        0, at, wires, att, h[...].astype(F32), sc, ob, gain, bias, b1, wp, w1, w2, loads,
        mixed, br1, br2, rows_two, act, slope, bufs,
    )
    nxt[...] = after
    inward_part(
        1, at, wires, after, gain, bias, b2, w, loads_qkv, rows_one, q, win, relay
    )
    wires.close()


def between_layers(cid, *ins):
    return call(
        between_kernel, "between_layers", cid, ins,
        [OWN, OWN, OWN, OWN, TALL, TALL, TALL] + IN_OUTS,
        OUT_WEIGHTS + IN_SCRATCH + scatter_scratch(2),
        OUT_SEMS + IN_SEMS,
        limit=36, specs=[VM] * 8 + [ANY] * 4, local=6,
    )


def start_back(layer, at, wires, grad, sc, g2):
    g2[pl.ds(at.own, R), :] = (grad * sc[layer, 1:2, :]).astype(BF)
    return Gather(wires, at, g2)


def back_out_part(
    layer, at, wires, grad, gather, sc, ob, gain, mixed, br1, br2, act, slope, rows, att,
    wp, w1, w2, gmix, gatt, dw2_hbm, dw1_hbm, dwp, vec, fb, dw2, dw1, g2, gp, g1, bufs,
    ls, base, steps,
):
    vec[0:1, :] = jnp.sum(grad * (br2[...] + ob[layer, 1:2, :]), axis=0, keepdims=True)
    vec[1:2, :] = sc[layer, 1:2, :] * jnp.sum(grad, axis=0, keepdims=True)

    def hidden(part):
        x = part.load(g2)
        for j in range(F // 256):
            cols = pl.ds(j * 256, 256)
            up = mm_rt(x, w2[cols, :])
            part.store(gp, (up * part.load(slope, cols).astype(F32)).astype(BF), cols)

    scatter = Scatter(wires, at, bufs)
    gather_hidden_scatter(
        at, gather, scatter, hidden, lambda part: mm_rt(part.load(gp), w1[...]), lambda: None
    )
    steps(0)
    for j in range(D // 256):
        cols = pl.ds(j * 256, 256)
        dw2[cols, :] = mm_lt(g2[:, cols], act[...]).astype(BF)
    write_2 = fetch(dw2, dw2_hbm, ls.at[base])
    steps(1)
    for j in range(D // 256):
        cols = pl.ds(j * 256, 256)
        dw1[cols, :] = mm_lt(rows[:, cols], gp[...]).astype(BF)
    write_1 = fetch(dw1, dw1_hbm, ls.at[base + 1])
    fb[...] = jnp.broadcast_to(jnp.sum(gp[...].astype(F32), axis=0, keepdims=True), fb.shape)
    grad_in, grad_gain, grad_shift = norm_back(
        mixed[...], gain[layer, 1:2, :], scatter.total()
    )
    mix = grad + grad_in
    gmix[...] = mix
    g1[pl.ds(at.own, R), :] = (mix * sc[layer, 0:1, :]).astype(BF)
    gather = Gather(wires, at, g1)
    steps(2)
    vec[2:3, :] = grad_gain
    vec[3:4, :] = grad_shift
    vec[4:5, :] = jnp.sum(mix * (br1[...] + ob[layer, 0:1, :]), axis=0, keepdims=True)
    vec[5:6, :] = sc[layer, 0:1, :] * jnp.sum(mix, axis=0, keepdims=True)
    vec[6:8, :] = jnp.zeros((2, D), F32)
    gather.near()
    gatt[pl.ds(at.near, 2 * R), :] = mm_rt(g1[pl.ds(at.near, 2 * R), :], wp[...]).astype(BF)
    gather.far()
    steps(3)
    gatt[pl.ds(at.far, 2 * R), :] = mm_rt(g1[pl.ds(at.far, 2 * R), :], wp[...]).astype(BF)
    dwp[...] = mm_lt(g1[...], att[...]).astype(BF)
    steps(4)
    write_2.wait()
    write_1.wait()


BACK_OUTS = [
    OWN, ((S, LW), BF), ((D, F), BF), ((D, F), BF), ((D, LW), BF), ((8, D), F32), ((8, F), F32),
]
BACK_OUT_SPECS = [VM, VM, ANY, ANY, VM, VM, VM]
BACK_SCRATCH = [pltpu.VMEM((D, F), BF)] * 2 + [
    pltpu.VMEM((S, D), BF), pltpu.VMEM((S, F), BF), pltpu.VMEM((S, D), BF),
]
BACK_SEMS = 2 * AG_SEMS + RS_SEMS


def turn_kernel(
    att, h, sc, ob, gain, bias, b1, g, wp_hbm, w1_hbm, w2_hbm,
    out, gmix, gatt, dw2_hbm, dw1_hbm, dwp, vec, fb,
    wp, w1, w2, mixed, br1, br2, rows, act, slope, dw2, dw1, g2, gp, g1, *rest,
):
    bufs = rest[:-3]
    ss, rs, ls = rest[-3:]
    layer = 1
    at = Place()
    wires = Wires(ss, rs)
    loads = fetch_out(layer, wp_hbm, w1_hbm, w2_hbm, wp, w1, w2, ls, 0)
    greet([{"tensor": at.mate}, {"tensor": at.cp}])
    started = []
    after = outward_part(
        layer, at, wires, att, h[...].astype(F32), sc, ob, gain, bias, b1, wp, w1, w2, loads,
        mixed, br1, br2, rows, act, slope, bufs,
        lambda: started.append(start_back(layer, at, wires, g[...], sc, g2)),
    )
    out[...] = after.astype(BF)
    back_out_part(
        layer, at, wires, g[...], started[0], sc, ob, gain, mixed, br1, br2, act, slope, rows,
        att, wp, w1, w2, gmix, gatt, dw2_hbm, dw1_hbm, dwp, vec, fb, dw2, dw1, g2, gp, g1,
        scatter_refs(bufs, 2), ls, 3, lambda step: None,
    )
    wires.close()


def turn(cid, *ins):
    return call(
        turn_kernel, "turn", cid, ins,
        [((R, D), BF)] + BACK_OUTS,
        OUT_WEIGHTS
        + [pltpu.VMEM(*OWN)] * 3
        + [pltpu.VMEM(*TALL)] * 3
        + BACK_SCRATCH
        + scatter_scratch(3),
        OUT_SEMS + BACK_SEMS,
        limit=44, specs=[VM] * 8 + [ANY] * 3, local=5, out_specs=[VM] + BACK_OUT_SPECS,
    )


def back_in_part(
    layer, at, wires, dq, dwin, rows, gmix, h, gain, dwp, w, loads, dw, vec, qb, proj, lanes,
    bufs, steps,
):
    da, db, dc, ua, ub, uc, sdb, sdc, sub, suc = lanes
    chain_up, chain_dn = Line(wires, {"dp": at.up}), Line(wires, {"dp": at.dn})
    low3, low2, low1 = OWN0 - 3 * S, OWN0 - 2 * S, OWN0 - S
    high1, high2, high3 = OWN0 + S, OWN0 + 2 * S, OWN0 + 3 * S

    def chunk(ref, k, base=0):
        return ref.at[pl.ds(base + k * R, R)]

    def plus(base, k, other):
        mine = dwin[pl.ds(base + k * R, R), :].astype(F32)
        return (mine + other[pl.ds(k * R, R), :].astype(F32)).astype(BF)

    ups, dns = {}, {}

    def send(n, k, down, up):
        dns[n, k] = chain_dn.send(*down)
        ups[n, k] = chain_up.send(*up)

    def arrive(n, k):
        chain_dn.arrive(dns[n, k])
        chain_up.arrive(ups[n, k])

    def first(k):
        j = 3 - k
        send(
            1, k, (chunk(dwin, k, low3), chunk(da, k)), (chunk(dwin, j, high3), chunk(ua, j))
        )

    def second(k):
        j = 3 - k
        arrive(1, k)
        sdb[pl.ds(k * R, R), :] = plus(low2, k, da)
        sub[pl.ds(j * R, R), :] = plus(high2, j, ua)
        send(2, k, (chunk(sdb, k), chunk(db, k)), (chunk(sub, j), chunk(ub, j)))

    def third(k):
        j = 3 - k
        arrive(2, k)
        sdc[pl.ds(k * R, R), :] = plus(low1, k, db)
        suc[pl.ds(j * R, R), :] = plus(high1, j, ub)
        send(3, k, (chunk(sdc, k), chunk(dc, k)), (chunk(suc, j), chunk(uc, j)))

    for k in (1, 2, 3):
        first(k)
    send(2, 0, (chunk(dwin, 0, low2), chunk(db, 0)), (chunk(dwin, 3, high2), chunk(ub, 3)))
    def into(first, value):
        dw[:, :, :, :, pl.ds(first, value.shape[-1])] = as_blocks(value)

    proj[:, :LW] = dq[...]
    into(3 * LW, dwp[...])
    into(0, mm_lt(rows[...], dq[...]).astype(BF))
    for k in (1, 2, 3):
        second(k)
    for k in range(4):
        third(k)
    for k in range(4):
        arrive(3, k)
    steps(0)
    own = dwin[pl.ds(OWN0, S), :].astype(F32)
    proj[:, LW:] = (own + dc[...].astype(F32) + uc[...].astype(F32)).astype(BF)
    for copy in loads:
        copy.wait()
    scatter = Scatter(wires, at, bufs)
    scatter.everything(lambda first: mm_rt(proj[pl.ds(first, 2 * R), :], w[...]))
    into(LW, mm_lt(rows[...], proj[:, LW:]).astype(BF))
    steps(1)
    qb[...] = jnp.broadcast_to(jnp.sum(proj[...].astype(F32), axis=0, keepdims=True), qb.shape)
    grad_in, grad_gain, grad_shift = norm_back(
        h[...].astype(F32), gain[layer, 0:1, :], scatter.total()
    )
    vec[0:1, :] = grad_gain
    vec[1:2, :] = grad_shift
    vec[2:8, :] = jnp.zeros((6, D), F32)
    return gmix[...] + grad_in


BLOCKS = ((4, 2, 4, RP, 4 * LW), BF)
EIGHT, EIGHT3 = ((8, D), F32), ((8, 3 * LW), F32)
IN_BACK_SCRATCH = (
    [pltpu.VMEM((D, 3 * LW), BF), pltpu.VMEM((S, 3 * LW), BF)]
    + [pltpu.VMEM((S, 2 * LW), BF)] * 10
)
IN_BACK_SEMS = RS_SEMS + 22


def middle_kernel(*refs):
    take = Refs(refs).take
    dq, dwin, rows_one, gmix1, h, gain, dwp1, dw2_1, dw1_1 = take(9)
    sc, ob = take(2)
    late_hbm = take(7)
    wp_hbm, w1_hbm, w2_hbm, w_hbm = take(4)
    vec_in, qb, gmix, gatt, dw2_hbm, dw1_hbm, dwp, vec, fb = take(9)
    sums = take(NP)
    wp, w1, w2, dw2, dw1, g2, gp, g1 = take(8)
    w, proj = take(2)
    lanes = take(10)
    dw = take(1)[0]
    accs = take(NP)
    wide_bufs, narrow_bufs = take(NP * WIDE_REFS), take(NP * NARROW_REFS)
    bufs = take(2 + 2 * SCATTER_REFS)
    late = take(7)
    ss, rs, ls = take(3)
    at = Place()
    wires = Wires(ss, rs)
    loads = fetch_qkv(1, w_hbm, w, ls)
    loads_out = fetch_out(0, wp_hbm, w1_hbm, w2_hbm, wp, w1, w2, ls, 3)
    loads_out += [
        fetch(src, dst, ls.at[8 + 3 * NP + k]) for k, (src, dst) in enumerate(zip(late_hbm, late))
    ]
    mixed, br1, br2, act, slope, rows_two, att = late
    rings = Rings()
    wide = Wide(wires, rings, (dw2_1, dw1_1, dw), wide_bufs, ls, 8)
    narrow = Narrow(wires, rings, accs, narrow_bufs)
    greet(
        [{"tensor": at.mate}, {"tensor": at.cp}, {"dp": at.up}, {"dp": at.dn}]
        + rings.next_to()
        + [rings.other]
    )
    def steps_in(step):
        if step == 0:
            wide.start(0, 1)
        else:
            wide.start(2, 3)
            wide.forward(0, 1)

    def steps_out(step):
        if step == 0:
            wide.finish(accs, 0, 1)
            narrow.start(0, 1)
        elif step == 1:
            wide.finish(accs, 2, 3)
            narrow.start(2, 3)
            narrow.forward(0, 1)
        elif step == 2:
            narrow.forward(2, 3)
            narrow.beyond(0, 1)
        elif step == 3:
            narrow.beyond(2, 3)
        else:
            narrow.finish(sums)

    grad = back_in_part(
        1, at, wires, dq, dwin, rows_one, gmix1, h, gain, dwp1, w, loads, dw, vec_in, qb, proj,
        lanes, scatter_refs(bufs, 0), steps_in,
    )
    gather = start_back(0, at, wires, grad, sc, g2)
    wide.forward(2, 3)
    for copy in loads_out:
        copy.wait()
    back_out_part(
        0, at, wires, grad, gather, sc, ob, gain, mixed, br1, br2, act, slope, rows_two, att,
        wp, w1, w2, gmix, gatt, dw2_hbm, dw1_hbm, dwp, vec, fb, dw2, dw1, g2, gp, g1,
        scatter_refs(bufs, 1), ls, 6, steps_out,
    )
    wires.close()


def middle(cid, *ins):
    return call(
        middle_kernel, "middle", cid, ins,
        [EIGHT, EIGHT3] + BACK_OUTS + reduced_shapes(),
        OUT_WEIGHTS
        + BACK_SCRATCH
        + IN_BACK_SCRATCH
        + [pltpu.VMEM(*BLOCKS)]
        + [pltpu.VMEM(*wide_shape(width, mode)) for _, _, width, mode in PIECES]
        + wide_scratch()
        + narrow_scratch()
        + scatter_scratch(2)
        + [pltpu.VMEM(*OWN)] * 3
        + [pltpu.VMEM(*TALL)] * 3
        + [pltpu.VMEM((S, LW), BF)],
        IN_BACK_SEMS + BACK_SEMS + 13 * NP,
        limit=51,
        specs=[VM] * 7 + [ANY] * 2 + [VM] * 2 + [ANY] * 11,
        local=15 + 3 * NP,
        out_specs=[VM, VM] + BACK_OUT_SPECS + [VM] * NP,
    )


def final_kernel(*refs):
    take = Refs(refs).take
    dq, dwin, rows, gmix, h, gain, dwp = take(7)
    va1, va0, vb1, fb1, fb0, qb1 = take(6)
    dw2, dw1, w_hbm = take(3)
    g, vout = take(2)
    sums = take(NP)
    w, proj = take(2)
    lanes = take(10)
    dw, vec, qb = take(3)
    accs = take(NP)
    wide_bufs, narrow_bufs = take(NP * WIDE_REFS), take(NP * NARROW_REFS)
    vector_bufs = take(6)
    bufs = take(2 + SCATTER_REFS)
    ss, rs, ls = take(3)
    at = Place()
    wires = Wires(ss, rs)
    loads = fetch_qkv(0, w_hbm, w, ls)
    rings = Rings()
    wide = Wide(wires, rings, (dw2, dw1, dw), wide_bufs, ls, 3)
    narrow = Narrow(wires, rings, accs, narrow_bufs)
    vectors = Vectors(wires, at, rings, vector_bufs)
    greet(
        [{"tensor": at.mate}, {"tensor": at.cp}, {"dp": at.up}, {"dp": at.dn}]
        + [*rings.along_y, *rings.along_x, rings.other]
    )

    def steps(step):
        if step == 0:
            wide.start(0, 1)
        else:
            wide.forward(0, 1)
            wide.start(2, 3)

    g[...] = back_in_part(
        0, at, wires, dq, dwin, rows, gmix, h, gain, dwp, w, loads, dw, vec, qb, proj, lanes,
        bufs, steps,
    )
    vectors.fill(((va0, vec, fb0, qb), (va1, vb1, fb1, qb1)))
    wide.forward(2, 3)
    vectors.over_core()
    wide.finish(accs, 0, 1)
    narrow.start(0, 1)
    vectors.over_chip()
    wide.finish(accs, 2, 3)
    narrow.start(2, 3)
    vectors.over_y()
    narrow.forward(0, 1)
    narrow.forward(2, 3)
    vectors.over_x()
    narrow.beyond(0, 1, 2, 3)
    vectors.finish(vout)
    narrow.finish(sums)
    wires.close()


def final(cid, *ins):
    return call(
        final_kernel, "final", cid, ins,
        [OWN, (VEC, F32)] + reduced_shapes(),
        IN_BACK_SCRATCH
        + [pltpu.VMEM(*BLOCKS), pltpu.VMEM(*EIGHT), pltpu.VMEM(*EIGHT3)]
        + [pltpu.VMEM(*wide_shape(width, mode)) for _, _, width, mode in PIECES]
        + wide_scratch()
        + narrow_scratch()
        + vector_scratch()
        + scatter_scratch(1),
        IN_BACK_SEMS + 13 * NP + 9,
        limit=48,
        specs=[VM] * 13 + [ANY] * 3,
        local=3 + 3 * NP,
    )


def shards(
    tokens_in,
    image_starts,
    norm_gain,
    norm_bias,
    qkv_weight,
    qv_bias,
    proj_weight,
    out_bias,
    layer_scale,
    fc1_weight,
    fc1_bias,
    fc2_weight,
    out_grad,
):
    w_qkv = jnp.transpose(qkv_weight, (0, 2, 1, 3))
    norms = (norm_gain, norm_bias)
    out_weights = (proj_weight, fc1_weight, fc2_weight)
    one0, q0, win0 = inward(0, tokens_in, *norms, qv_bias, w_qkv)
    att0, lt0 = attend(image_starts, q0, win0)
    mixed, br1, br2, h1, two0, act, slope, one1, q1, win1 = between_layers(
        1, att0, tokens_in, layer_scale, out_bias, *norms, fc1_bias, qv_bias, *out_weights, w_qkv
    )
    att1, lt1 = attend(image_starts, q1, win1)
    hidden, gmix, gatt, dw2, dw1, dwp, va1, fb1 = turn(
        2, att1, h1, layer_scale, out_bias, *norms, fc1_bias, out_grad, *out_weights
    )
    dq, dwin = attend_back(image_starts, q1, win1, gatt, att1, lt1)
    vb1, qb1, gmix, gatt, dw2, dw1, dwp, va0, fb0, a1, b1, c1, d1 = middle(
        3, dq, dwin, one1, gmix, h1, norm_gain, dwp, as_blocks(dw2), as_blocks(dw1),
        layer_scale, out_bias, mixed, br1, br2, act, slope, two0, att0, *out_weights, w_qkv,
    )
    dq, dwin = attend_back(image_starts, q0, win0, gatt, att0, lt0)
    grad, vec, a0, b0, c0, d0 = final(
        4, dq, dwin, one0, gmix, tokens_in, norm_gain, dwp, va1, va0, vb1, fb1, fb0, qb1,
        as_blocks(dw2), as_blocks(dw1), w_qkv,
    )
    rows = vec[:16].reshape(2, 8, D)
    qkv = jnp.stack(
        [jnp.concatenate([c0, d0[:, :LW]], 1), jnp.concatenate([c1, d1[:, :LW]], 1)]
    )
    return (
        hidden,
        grad,
        jnp.stack([rows[:, 6], rows[:, 2]], 1),
        jnp.stack([rows[:, 7], rows[:, 3]], 1),
        qkv.reshape(2, RP, 3, LW),
        jnp.stack([vec[18:20, :LW], vec[18:20, 2 * LW : 3 * LW]], 1),
        jnp.stack([d0[:, LW:].T, d1[:, LW:].T]),
        jnp.stack([rows[:, 5], rows[:, 1]], 1),
        jnp.stack([rows[:, 4], rows[:, 0]], 1),
        jnp.stack([b0, b1]),
        vec[16:18],
        jnp.stack([a0.T, a1.T]),
    )


def solution(mesh):
    return jax.shard_map(
        shards,
        mesh=mesh,
        in_specs=(
            P(("dp", "tensor"), None),
            P(),
            P(),
            P(),
            P(None, None, None, "tensor"),
            P(None, None, "tensor"),
            P(None, "tensor", None),
            P(),
            P(),
            P(None, None, "tensor"),
            P(None, "tensor"),
            P(None, "tensor", None),
            P(("dp", "tensor"), None),
        ),
        out_specs=(
            P(("dp", "tensor"), None),
            P(("dp", "tensor"), None),
            P(),
            P(),
            P(None, "dp", None, "tensor"),
            P(None, None, "tensor"),
            P(None, "tensor", "dp"),
            P(),
            P(),
            P(None, "dp", "tensor"),
            P(None, "tensor"),
            P(None, "tensor", "dp"),
        ),
        check_vma=False,
    )
```

```python
import functools

import jax
import jax.numpy as jnp
from jax import lax
from jax.experimental import pallas as pl
from jax.experimental.pallas import tpu as pltpu
from jax.sharding import PartitionSpec as P

MESH = pl.DeviceIdType.MESH
BF = jnp.bfloat16
F32 = jnp.float32
VM = pl.BlockSpec(memory_space=pltpu.VMEM)
SM = pl.BlockSpec(memory_space=pltpu.SMEM)
ANY = pl.BlockSpec(memory_space=pl.ANY)

HEAD_DIM = 64
IMG_LEN = 1370
EPS = 1e-06
NEG = -1e30

R = 128
S = 512
D = 1024
LW = 256
HL = LW // HEAD_DIM
F = 1024
TOTAL = 16384
NDP = 32
FAR3 = 384
OWN0 = FAR3 + 2 * S
NW = 2 * OWN0 + S
QB = 256
KB = 256
NB = NW // KB
C = 2
RC = R // C
MB = 1 << 20


def mm(a, b):
    return jnp.dot(a, b, preferred_element_type=F32)


def mm_rt(a, b):
    return lax.dot_general(a, b, (((1,), (1,)), ((), ())), preferred_element_type=F32)


def mm_lt(a, b):
    return lax.dot_general(a, b, (((0,), (0,)), ((), ())), preferred_element_type=F32)


class Place:
    def __init__(self):
        self.t = lax.axis_index("tensor")
        self.core = lax.rem(self.t, 2)
        self.mate = self.t + 1 - 2 * self.core
        self.cp = lax.rem(self.t + 2, 4)
        self.own = pl.multiple_of(self.t * R, R)
        self.opp = pl.multiple_of(self.cp * R, R)
        self.near = pl.multiple_of((self.t - self.core) * R, 2 * R)
        self.far = pl.multiple_of(2 * R - self.near, 2 * R)
        self.dp = lax.axis_index("dp")
        self.up = lax.rem(self.dp + 1, NDP)
        self.dn = lax.rem(self.dp + NDP - 1, NDP)


def greet(devices):
    barrier = pltpu.get_barrier_semaphore()
    for device in devices:
        pl.semaphore_signal(barrier, inc=1, device_id=device, device_id_type=MESH)
    pl.semaphore_wait(barrier, len(devices))


class Wires:
    def __init__(self, send, recv):
        self.send, self.recv, self.count, self.open = send, recv, 0, []

    def push(self, src, dst, device):
        k = self.count
        self.count += 1
        copy = pltpu.make_async_remote_copy(
            src, dst, self.send.at[k], self.recv.at[k], device_id=device, device_id_type=MESH
        )
        copy.start()
        self.open.append(copy)
        return copy

    def left(self, copy):
        copy.wait_send()
        self.open = [c for c in self.open if c is not copy]

    def close(self):
        for copy in self.open:
            copy.wait_send()


class Chain:
    def __init__(self, wires, at, up, relay):
        self.wires, self.at, self.relay = wires, at, relay
        y = lax.rem(at.dp, 4)
        self.edge = (y == 3) if up else (y == 0)
        self.plain = jnp.logical_not(self.edge)
        self.device = at.up if up else at.dn
        self.items = []

    def plan(self, src, dst, partner_dst=None, when=True, partner_when=True):
        wires, at = self.wires, self.at
        slot = self.relay.at[len(self.items)]
        k = wires.count
        wires.count += 2

        def copy(source, target, n, device):
            return lambda: pltpu.make_async_remote_copy(
                source, target, wires.send.at[n], wires.recv.at[n],
                device_id=device, device_id_type=MESH,
            )

        direct = copy(src, dst, k, {"dp": self.device})
        first = copy(src, slot, k + 1, {"tensor": at.cp})
        target = dst if partner_dst is None else partner_dst
        second = copy(slot, target, k, {"dp": self.device, "tensor": at.cp})
        item = (direct, first, second, when, partner_when)
        self.items.append(item)
        return item

    def send(self, item):
        direct, first, _, when, _ = item
        pl.when(self.plain & when)(lambda: direct().start())
        pl.when(self.edge & when)(lambda: first().start())

    def hand_on(self, item):
        _, first, second, _, partner_when = item

        @pl.when(self.edge & partner_when)
        def _():
            first().wait_recv()
            second().start()

    def arrive(self, item):
        pl.when(item[3])(lambda: item[0]().wait_recv())

    def close(self):
        for direct, first, second, when, partner_when in self.items:
            pl.when(self.plain & when)(lambda c=direct: c().wait_send())
            pl.when(self.edge & when)(lambda c=first: c().wait_send())
            pl.when(self.edge & partner_when)(lambda c=second: c().wait_send())


class Line:
    def __init__(self, wires, device):
        self.wires, self.device = wires, device

    def send(self, src, dst):
        return self.wires.push(src, dst, self.device)

    def arrive(self, copy):
        copy.wait_recv()


def chain_partners(at):
    return [
        {"tensor": at.mate},
        {"tensor": at.cp},
        {"dp": at.up},
        {"dp": at.dn},
        {"dp": at.up, "tensor": at.cp},
        {"dp": at.dn, "tensor": at.cp},
    ]


AG_SEMS = 2 * C + 1
RS_SEMS = 2 * C + 1


class Gather:
    def __init__(self, wires, at, buf):
        self.wires, self.at, self.buf = wires, at, buf
        own = at.own
        self.across, self.passed = [], []
        for c in range(C):
            part = buf.at[pl.ds(own + c * RC, RC)]
            self.across.append(wires.push(part, part, {"tensor": at.cp}))
        part = buf.at[pl.ds(own, R)]
        self.beside = wires.push(part, part, {"tensor": at.mate})

    def near(self):
        self.beside.wait_recv()

    def take(self, c):
        self.across[c].wait_recv()
        part = self.buf.at[pl.ds(self.at.opp + c * RC, RC)]
        self.passed.append(self.wires.push(part, part, {"tensor": self.at.mate}))

    def arrived(self, c):
        self.passed[c].wait_recv()

    def far(self):
        for c in range(C):
            self.take(c)
        for c in range(C):
            self.arrived(c)


class Rows:
    def __init__(self, at, chunk=None):
        if chunk is None:
            self.parts = [(at.near, 2 * R)]
        else:
            self.parts = [
                (pl.multiple_of(at.far + core * R + chunk * RC, RC), RC) for core in range(2)
            ]

    def load(self, ref, cols=slice(None)):
        parts = [ref[pl.ds(first, count), cols] for first, count in self.parts]
        return parts[0] if len(parts) == 1 else jnp.concatenate(parts, axis=0)

    def store(self, ref, value, cols=slice(None)):
        at = 0
        for first, count in self.parts:
            ref[pl.ds(first, count), cols] = value[at : at + count]
            at += count


class Scatter:
    def __init__(self, wires, at, bufs):
        self.wires, self.at = wires, at
        self.far, self.near = bufs[:2]
        self.send1, self.recv1, self.send2, self.recv2, self.send3, self.recv3 = bufs[2:]
        self.ones, self.twos = [], []

    def put(self, c, value):
        for core in range(2):
            self.far[pl.ds(core * R + c * RC, RC), :] = value[core * RC : (core + 1) * RC]

    def first(self, c):
        at = self.at
        rows = pl.ds(c * RC, RC)
        src = pl.ds(pl.multiple_of((1 - at.core) * R + c * RC, RC), RC)
        self.send1[rows, :] = self.far[src, :].astype(BF)
        self.ones.append(
            self.wires.push(self.send1.at[rows], self.recv1.at[rows], {"tensor": at.mate})
        )

    def second(self, c):
        at = self.at
        rows = pl.ds(c * RC, RC)
        src = pl.ds(pl.multiple_of(at.core * R + c * RC, RC), RC)
        self.ones[c].wait_recv()
        total = self.far[src, :] + self.recv1[rows, :].astype(F32)
        self.send2[rows, :] = total.astype(BF)
        self.twos.append(
            self.wires.push(self.send2.at[rows], self.recv2.at[rows], {"tensor": at.cp})
        )

    def third(self):
        at = self.at
        src = pl.ds(pl.multiple_of((1 - at.core) * R, R), R)
        self.send3[...] = self.near[src, :].astype(BF)
        self.three = self.wires.push(self.send3, self.recv3, {"tensor": at.mate})

    def everything(self, product):
        self.far[...] = product(self.at.far)
        for c in range(C):
            self.first(c)
        self.near[...] = product(self.at.near)
        for c in range(C):
            self.second(c)
        self.third()

    def total(self):
        self.three.wait_recv()
        for copy in self.twos:
            copy.wait_recv()
        own = self.near[pl.ds(pl.multiple_of(self.at.core * R, R), R), :]
        return own + self.recv3[...].astype(F32) + self.recv2[...].astype(F32)


def gather_hidden_scatter(at, gather, scatter, hidden, product, ready):
    gather.near()
    hidden(Rows(at))
    ready()
    gather.take(0)
    gather.arrived(0)
    rows = [Rows(at, c) for c in range(C)]
    hidden(rows[0])
    gather.take(1)
    scatter.put(0, product(rows[0]))
    scatter.first(0)
    gather.arrived(1)
    hidden(rows[1])
    scatter.second(0)
    scatter.put(1, product(rows[1]))
    scatter.first(1)
    scatter.near[...] = product(Rows(at))
    scatter.second(1)
    scatter.third()


SCATTER_REFS = 6


def scatter_scratch(count):
    return [pltpu.VMEM((2 * R, D), F32)] * 2 + [pltpu.VMEM((R, D), BF)] * (6 * count)


def scatter_refs(bufs, which):
    first = 2 + SCATTER_REFS * which
    return [*bufs[:2], *bufs[first : first + SCATTER_REFS]]


class Refs:
    def __init__(self, refs):
        self.refs = list(refs)

    def take(self, count):
        out, self.refs = self.refs[:count], self.refs[count:]
        return out


def fetch(src, dst, sem):
    copy = pltpu.make_async_copy(src, dst, sem)
    copy.start()
    return copy


def fetch_qkv(layer, w, buf, ls, base=0):
    return [
        fetch(w.at[layer, k], buf.at[:, pl.ds(k * LW, LW)], ls.at[base + k]) for k in range(3)
    ]


def normalized(v):
    centered = v - jnp.mean(v, axis=-1, keepdims=True)
    scale = lax.rsqrt(jnp.mean(centered * centered, axis=-1, keepdims=True) + EPS)
    return centered * scale, scale


def norm_back(v, gain, grad):
    x_hat, scale = normalized(v)
    u = grad * gain
    grad_in = scale * (
        u
        - jnp.mean(u, axis=-1, keepdims=True)
        - x_hat * jnp.mean(u * x_hat, axis=-1, keepdims=True)
    )
    return (
        grad_in,
        jnp.sum(grad * x_hat, axis=0, keepdims=True),
        jnp.sum(grad, axis=0, keepdims=True),
    )


def call(kernel, name, cid, ins, outs, scratch, sems, limit, specs=None, local=0, out_specs=None):
    shapes = [jax.ShapeDtypeStruct(shape, dtype) for shape, dtype in outs]
    extra = []
    if sems:
        extra = [pltpu.SemaphoreType.DMA((sems,)), pltpu.SemaphoreType.DMA((sems,))]
    if local:
        extra.append(pltpu.SemaphoreType.DMA((local,)))
    params = dict(vmem_limit_bytes=limit * MB)
    if cid is not None:
        params.update(collective_id=cid, has_side_effects=True)
    return pl.pallas_call(
        kernel,
        out_shape=shapes,
        in_specs=specs or [VM] * len(ins),
        out_specs=out_specs or [VM] * len(outs),
        scratch_shapes=list(scratch) + extra,
        compiler_params=pltpu.CompilerParams(**params),
        name=name,
    )(*ins)


class Ring:
    def __init__(self, wires, chunk, mine, side_up, side_dn, place, bufs):
        self.wires, self.chunk = wires, chunk
        self.mine, self.side_up, self.side_dn = mine, side_up, side_dn
        self.me, self.up, self.dn = place
        self.from_dn, self.from_up, self.send_up, self.send_dn, self.last_dn, self.last_up = bufs

    def half(self, ref, k):
        width = ref.shape[-1] // 2
        return ref.at[..., pl.ds(k * width, width)]

    def position(self, step):
        return lax.rem(self.me + step, 4)

    def start(self):
        push, chunk = self.wires.push, self.chunk
        p1, p2, p3 = self.position(1), self.position(2), self.position(3)
        self.a = push(chunk(p2, 0), self.from_dn, self.up)
        self.b = push(chunk(p2, 1), self.from_up, self.dn)
        self.c = push(chunk(p1, 1), self.half(self.last_dn, 1), self.up)
        self.d = push(chunk(p3, 0), self.half(self.last_up, 0), self.dn)

    def forward(self):
        push = self.wires.push
        self.a.wait_recv()
        total = self.side_up()[...].astype(F32) + self.from_dn[...].astype(F32)
        self.send_up[...] = total.astype(BF)
        self.e = push(self.send_up, self.half(self.last_dn, 0), self.up)
        self.b.wait_recv()
        total = self.side_dn()[...].astype(F32) + self.from_up[...].astype(F32)
        self.send_dn[...] = total.astype(BF)
        self.f = push(self.send_dn, self.half(self.last_up, 1), self.dn)

    def finish(self, out):
        for copy in (self.c, self.d, self.e, self.f):
            copy.wait_recv()
        part = self.mine()[...].astype(F32)
        out[...] = (
            part + self.last_dn[...].astype(F32) + self.last_up[...].astype(F32)
        ).astype(out.dtype)


PIECES = ((0, 0, F, 0), (1, 0, F, 1), (2, 0, 2 * LW, 0), (2, 2 * LW, 2 * LW, 1))
RP = R // 4
NP = len(PIECES)


class Rings:
    def __init__(self):
        i = lax.axis_index("dp")
        self.y = y = lax.rem(i, 4)
        self.x = lax.div(i, 8)
        self.zh = zh = lax.rem(lax.div(i, 4), 2)
        self.along_y = [{"dp": i - y + lax.rem(y + k, 4)} for k in (1, 2, 3)]
        self.along_x = [{"dp": lax.rem(i + 8 * k, 32)} for k in (1, 2, 3)]
        self.other = {"dp": i + 4 - 8 * zh}
        ring_y = (y, self.along_y[0], self.along_y[2])
        ring_x = (self.x, self.along_x[0], self.along_x[2])
        self.order = [(ring_y, ring_x), (ring_x, ring_y)]

    def next_to(self):
        return [*self.along_y[::2], *self.along_x[::2]]


def ring_scratch(lead, width):
    half = pltpu.VMEM((*lead, width // 2), BF)
    full = pltpu.VMEM((*lead, width), BF)
    return [half, half, half, half, full, full]


def wide_shape(width, mode):
    return ((4, 2, RP, width) if mode == 0 else (2, 4, RP, width), BF)


WIDE_REFS, NARROW_REFS = 9, 8


def wide_scratch():
    out = []
    for _, _, width, mode in PIECES:
        lead = wide_shape(width, mode)[0][:3]
        half = pltpu.VMEM((*lead, width // 2), BF)
        out += ring_scratch(lead, width) + [pltpu.VMEM((*lead, width), BF), half, half]
    return out


def narrow_scratch():
    out = []
    for _, _, width, _ in PIECES:
        small, rest = pltpu.VMEM((2, RP, width), BF), pltpu.VMEM((RP, width), BF)
        out += ring_scratch((2, RP), width) + [small, rest]
    return out


def reduced_shapes():
    return [((RP, width), F32) for _, _, width, _ in PIECES]


def as_blocks(w):
    return w.reshape(4, 2, 4, RP, w.shape[-1])


class Wide:
    def __init__(self, wires, rings, ins, bufs, ls, first_sem):
        self.rings, self.loads = [], []
        for k, (which, column, width, mode) in enumerate(PIECES):
            refs = bufs[k * WIDE_REFS : (k + 1) * WIDE_REFS]
            mine, side_up, side_dn = refs[6:9]
            w = ins[which]

            def chunk(pos, half, w=w, mode=mode, column=column, size=width // 2):
                cols = pl.ds(column + half * size, size)
                return w.at[:, :, pos, :, cols] if mode == 0 else w.at[pos, :, :, :, cols]

            place = rings.order[mode][0]
            me = place[0]
            cols = pl.ds(column, width)
            whole = w.at[:, :, me, :, cols] if mode == 0 else w.at[me, :, :, :, cols]
            parts = (
                (chunk(lax.rem(me + 1, 4), 0), side_up),
                (chunk(lax.rem(me + 3, 4), 1), side_dn),
                (whole, mine),
            )
            sems = [ls.at[first_sem + 3 * k + j] for j in range(3)]
            self.loads.append(
                [pltpu.make_async_copy(src, dst, sem) for (src, dst), sem in zip(parts, sems)]
            )
            self.rings.append(
                Ring(
                    wires, chunk, lambda r=mine: r, lambda r=side_up: r, lambda r=side_dn: r,
                    place, refs[0:6],
                )
            )

    def start(self, *ks):
        for k in ks:
            for copy in self.loads[k]:
                copy.start()
            self.rings[k].start()

    def forward(self, *ks):
        for k in ks:
            for copy in self.loads[k]:
                copy.wait()
            self.rings[k].forward()

    def finish(self, accs, *ks):
        for k in ks:
            self.rings[k].finish(accs[k])


class Narrow:
    def __init__(self, wires, rings, accs, bufs):
        self.wires, self.rings, self.parts, self.last = wires, [], [], {}
        self.zh, self.other = rings.zh, rings.other
        for k, (_, _, width, mode) in enumerate(PIECES):
            refs = bufs[k * NARROW_REFS : (k + 1) * NARROW_REFS]
            acc = accs[k]
            place = rings.order[mode][1]

            def chunk(pos, half, acc=acc, mode=mode, size=width // 2):
                cols = pl.ds(half * size, size)
                return acc.at[pos, :, :, cols] if mode == 0 else acc.at[:, pos, :, cols]

            def mine(acc=acc, mode=mode, pos=place[0]):
                return acc.at[pos] if mode == 0 else acc.at[:, pos]

            self.rings.append(
                Ring(
                    wires, chunk, mine,
                    lambda n=chunk, p=lax.rem(place[0] + 1, 4): n(p, 0),
                    lambda n=chunk, p=lax.rem(place[0] + 3, 4): n(p, 1),
                    place, refs[0:6],
                )
            )
            self.parts.append(refs[6:8])

    def start(self, *ks):
        for k in ks:
            self.rings[k].start()

    def forward(self, *ks):
        for k in ks:
            self.rings[k].forward()

    def beyond(self, *ks):
        for k in ks:
            small, rest = self.parts[k]
            self.rings[k].finish(small)
            self.last[k] = self.wires.push(small.at[1 - self.zh], rest, self.other)

    def finish(self, outs):
        for k, out in enumerate(outs):
            small, rest = self.parts[k]
            self.last[k].wait_recv()
            out[...] = small[self.zh].astype(F32) + rest[...].astype(F32)


VEC = (24, D)


def vector_scratch():
    few, whole, four = (
        pltpu.VMEM((16, D), F32), pltpu.VMEM(VEC, F32), pltpu.VMEM((4, *VEC), F32),
    )
    return [whole, few, few, four, four, whole]


class Vectors:
    def __init__(self, wires, at, rings, bufs):
        self.wires, self.at, self.rings = wires, at, rings
        self.vec, self.vmate, self.vcp, self.vy, self.vx, self.vz = bufs

    def fill(self, layers):
        vec = self.vec
        vec[...] = jnp.zeros_like(vec)
        for k, (va, vb, fb, qb) in enumerate(layers):
            vec[8 * k : 8 * k + 6, :] = va[0:6, :]
            vec[8 * k + 6 : 8 * k + 8, :] = vb[0:2, :]
            vec[16 + k : 17 + k, :] = fb[0:1, :]
            vec[18 + k : 19 + k, : 3 * LW] = qb[0:1, :]
        self.one = self.wires.push(vec.at[pl.ds(0, 16)], self.vmate, {"tensor": self.at.mate})

    def over_core(self):
        vec = self.vec
        self.one.wait_recv()
        self.wires.left(self.one)
        vec[0:16, :] = vec[0:16, :] + self.vmate[...]
        self.two = self.wires.push(vec.at[pl.ds(0, 16)], self.vcp, {"tensor": self.at.cp})

    def over_chip(self):
        vec, vy, y = self.vec, self.vy, self.rings.y
        self.two.wait_recv()
        vy[y] = vec[...]
        vy[y, 0:16, :] = vec[0:16, :] + self.vcp[...]
        self.sent = [self.wires.push(vy.at[y], vy.at[y], d) for d in self.rings.along_y]

    def over_y(self):
        vx, vy, x = self.vx, self.vy, self.rings.x
        for copy in self.sent:
            copy.wait_recv()
        vx[x] = vy[0] + vy[1] + vy[2] + vy[3]
        self.sent = [self.wires.push(vx.at[x], vx.at[x], d) for d in self.rings.along_x]

    def over_x(self):
        vec, vx = self.vec, self.vx
        for copy in self.sent:
            copy.wait_recv()
        self.wires.left(self.two)
        vec[...] = vx[0] + vx[1] + vx[2] + vx[3]
        self.last = self.wires.push(vec, self.vz, self.rings.other)

    def finish(self, out):
        self.last.wait_recv()
        out[...] = self.vec[...] + self.vz[...]


def inward_part(layer, at, wires, hidden, gain, bias, b2, w, loads, rows, q, win, relay):
    x_hat, _ = normalized(hidden)
    rows[pl.ds(at.own, R), :] = (x_hat * gain[layer, 0:1, :] + bias[layer, 0:1, :]).astype(BF)
    gather = Gather(wires, at, rows)

    def project(first):
        out = mm(rows[pl.ds(first, 2 * R), :], w[...])
        q[pl.ds(first, 2 * R), :] = (out[:, :LW] + b2[layer, 0:1, :]).astype(BF)
        win[pl.ds(OWN0 + first, 2 * R), :LW] = out[:, LW : 2 * LW].astype(BF)
        win[pl.ds(OWN0 + first, 2 * R), LW:] = (out[:, 2 * LW :] + b2[layer, 1:2, :]).astype(BF)

    def part(first):
        return win.at[pl.ds(pl.multiple_of(first, R), R)]

    offs = [at.near, at.near + R, at.far, at.far + R]
    others = offs[2:] + offs[:2]
    chain_up, chain_dn = Chain(wires, at, True, relay), Chain(wires, at, False, relay)
    ups, dns = {}, {}
    for n in range(1, 4):
        low, high = OWN0 - n * S, OWN0 + n * S
        for k, (own, other) in enumerate(zip(offs, others)):
            if n < 3:
                ups[n, k] = chain_up.plan(part(low + S + own), part(low + own), part(low + other))
                dns[n, k] = chain_dn.plan(
                    part(high - S + own), part(high + own), part(high + other)
                )
                continue
            ups[n, k] = chain_up.plan(
                part(low + S + own),
                part(jnp.maximum(low + own, 0)),
                part(jnp.maximum(low + other, 0)),
                own > 0,
                other > 0,
            )
            dns[n, k] = chain_dn.plan(
                part(high - S + own),
                part(jnp.minimum(high + own, NW - R)),
                part(jnp.minimum(high + other, NW - R)),
                own < S - R,
                other < S - R,
            )

    def hop(n, *ks):
        for k in ks:
            chain_up.send(ups[n, k])
            chain_dn.send(dns[n, k])

    for copy in loads:
        copy.wait()
    gather.near()
    project(at.near)
    hop(1, 0, 1)
    gather.far()
    for k in range(2):
        chain_up.hand_on(ups[1, k])
        chain_dn.hand_on(dns[1, k])
    project(at.far)
    hop(1, 2, 3)

    def hand_on(n, *ks):
        for k in ks:
            chain_up.hand_on(ups[n, k])
            chain_dn.hand_on(dns[n, k])

    def onward(n, *ks):
        for k in ks:
            chain_up.arrive(ups[n, k])
            chain_dn.arrive(dns[n, k])
            if n < 3:
                hop(n + 1, k)

    onward(1, 0, 1)
    hand_on(1, 2, 3)
    hand_on(2, 0, 1)
    onward(1, 2, 3)
    onward(2, 0, 1)
    hand_on(2, 2, 3)
    hand_on(3, 0, 1)
    onward(2, 2, 3)
    hand_on(3, 2, 3)
    onward(3, 0, 1, 2, 3)
    chain_up.close()
    chain_dn.close()


IN_OUTS = [((S, D), BF), ((S, LW), BF), ((NW, 2 * LW), BF)]
IN_SCRATCH = [pltpu.VMEM((D, 3 * LW), BF), pltpu.VMEM((12, R, 2 * LW), BF)]
IN_SEMS = AG_SEMS + 48


def inward_kernel(h, gain, bias, b2, w_hbm, rows, q, win, w, relay, ss, rs, ls):
    at = Place()
    wires = Wires(ss, rs)
    loads = fetch_qkv(0, w_hbm, w, ls)
    greet(chain_partners(at))
    inward_part(
        0, at, wires, h[...].astype(F32), gain, bias, b2, w, loads, rows, q, win, relay
    )
    wires.close()


def inward(cid, *ins):
    return call(
        inward_kernel, "inward", cid, ins, IN_OUTS, IN_SCRATCH, IN_SEMS,
        limit=14, specs=[VM] * 4 + [ANY], local=3,
    )


def ids_of(position, starts):
    total = jnp.zeros_like(position)
    for k in range(starts.shape[0]):
        first = starts[k]
        total += (position >= first).astype(jnp.int32)
        total += (position >= first + IMG_LEN).astype(jnp.int32)
    return jnp.where((position >= 0) & (position < TOTAL), total, -1)


def key_range(base, block, starts):
    first = base + block * QB
    last = first + QB - 1
    low, high = jnp.int32(0), jnp.int32(TOTAL)
    for k in range(starts.shape[0]):
        for edge in (starts[k], starts[k] + IMG_LEN):
            low = jnp.where(edge <= first, jnp.maximum(low, edge), low)
            high = jnp.where(edge > last, jnp.minimum(high, edge), high)
    edge = jnp.bool_(False)
    for k in range(starts.shape[0]):
        for at in (starts[k], starts[k] + IMG_LEN):
            edge = edge | ((at > first) & (at <= last))
    low = jnp.maximum(low - base + OWN0, 0)
    high = jnp.minimum(high - base + OWN0, NW)
    start = lax.div(low, 128) * 128
    tiles = lax.div(high - start + KB - 1, KB)
    start = jnp.minimum(start, NW - tiles * KB)
    whole = lambda at: jnp.logical_not(edge) & (at >= low) & (at + KB <= high)
    return start, tiles, whole


def spread_heads(value, out):
    lane = lax.broadcasted_iota(jnp.int32, (QB, LW), 1)
    for head in range(HL):
        mine = (lane >= head * HEAD_DIM) & (lane < (head + 1) * HEAD_DIM)
        out[pl.ds(head * QB, QB), :] = jnp.where(mine, value, 0.0).astype(BF)


def half_of(head):
    return head * HEAD_DIM // 128 * 128


def pick_heads(parts):
    lane = lax.broadcasted_iota(jnp.int32, (QB, 128), 1)
    halves = [
        jnp.where(lane < HEAD_DIM, parts(head), parts(head + 1)) for head in range(0, HL, 2)
    ]
    return jnp.concatenate(halves, axis=1)


def attend_kernel(starts, q, win, out, lt, qm, sbuf, high, low, acc):
    base = lax.axis_index("dp") * S
    for block in range(S // QB):
        spread_heads(q[pl.ds(block * QB, QB), :].astype(F32) * 0.125, qm)
        qid = ids_of(
            base + block * QB + lax.broadcasted_iota(jnp.int32, (QB, 1), 0), starts
        )
        start, tiles, whole = key_range(base, block, starts)
        high[...] = jnp.full_like(high, NEG)
        low[...] = jnp.zeros_like(low)
        acc[...] = jnp.zeros_like(acc)

        def scores(kb, carry):
            at = pl.multiple_of(start + kb * KB, 128)

            def put(masked):
                s = mm_rt(qm[...], win[pl.ds(at, KB), :LW])
                if masked:
                    kid = ids_of(
                        base - OWN0 + at + lax.broadcasted_iota(jnp.int32, (1, KB), 1), starts
                    )
                    bias = jnp.where(qid == kid, 0.0, NEG)
                for head in range(HL):
                    rows = pl.ds(head * QB, QB)
                    one = s[head * QB : (head + 1) * QB, :]
                    if masked:
                        one = one + bias
                    sbuf[kb, rows, :] = one
                    high[rows, :] = jnp.maximum(
                        high[rows, :], jnp.maximum(one[:, :128], one[:, 128:])
                    )

            pl.when(whole(at))(lambda: put(False))
            pl.when(jnp.logical_not(whole(at)))(lambda: put(True))
            return carry

        lax.fori_loop(0, tiles, scores, 0)
        top = jnp.max(high[...], axis=1, keepdims=True)
        high[...] = jnp.broadcast_to(top, high.shape)

        def values(kb, carry):
            at = pl.multiple_of(start + kb * KB, 128)
            for head in range(HL):
                rows = pl.ds(head * QB, QB)
                v = win[pl.ds(at, KB), pl.ds(LW + half_of(head), 128)]
                p = jnp.exp(sbuf[kb, rows, :] - high[rows, :1])
                low[rows, :] += p[:, :128] + p[:, 128:]
                acc[rows, :] += mm(p.astype(BF), v)
            return carry

        lax.fori_loop(0, tiles, values, 0)
        total = jnp.sum(low[...], axis=1, keepdims=True)
        inv = 1.0 / total
        out[pl.ds(block * QB, QB), :] = pick_heads(
            lambda head: acc[pl.ds(head * QB, QB), :] * inv[head * QB : (head + 1) * QB, :]
        ).astype(BF)
        flat = jnp.transpose(jnp.broadcast_to(top + jnp.log(total), (HL * QB, 128)))
        lt[pl.ds(block * 8, 8), :] = flat[:8, :]


def attend(starts, q, win):
    return call(
        attend_kernel,
        "attend",
        None,
        [starts, q, win],
        [((S, LW), BF), ((8 * (S // QB), HL * QB), F32)],
        [
            pltpu.VMEM((HL * QB, LW), BF),
            pltpu.VMEM((NB, HL * QB, KB), F32),
            pltpu.VMEM((HL * QB, 128), F32),
            pltpu.VMEM((HL * QB, 128), F32),
            pltpu.VMEM((HL * QB, 128), F32),
        ],
        0,
        limit=24,
        specs=[SM, VM, VM],
    )


def attend_back_kernel(starts, q, win, grad, att, lt, dq, dwin, qm, gm, dqa, dkv):
    base = lax.axis_index("dp") * S
    dkv[...] = jnp.zeros_like(dkv)
    head_row = lax.broadcasted_iota(jnp.int32, (8, LW), 0)
    lane_head = lax.div(lax.broadcasted_iota(jnp.int32, (8, LW), 1), HEAD_DIM)
    sums = (head_row == lane_head).astype(F32)
    for block in range(S // QB):
        rows = pl.ds(block * QB, QB)
        spread_heads(q[rows, :].astype(F32) * 0.125, qm)
        grad_rows = grad[rows, :].astype(F32)
        spread_heads(grad_rows, gm)
        both = grad_rows * att[rows, :].astype(F32)
        by_head = lax.dot_general(
            sums,
            both,
            (((1,), (1,)), ((), ())),
            precision=lax.Precision.HIGHEST,
            preferred_element_type=F32,
        )
        inner = jnp.concatenate([by_head[h : h + 1, :] for h in range(HL)], axis=1)
        logs = lt[pl.ds(block * 8, 1), :]
        qid = ids_of(
            base + block * QB + lax.broadcasted_iota(jnp.int32, (1, QB), 1), starts
        )
        start, tiles, whole = key_range(base, block, starts)
        dqa[...] = jnp.zeros_like(dqa)

        def one(kb, carry):
            at = pl.multiple_of(start + kb * KB, 128)

            def put(masked):
                keys = win[pl.ds(at, KB), :LW]
                vals = win[pl.ds(at, KB), LW:]
                st = mm_rt(keys, qm[...]) - logs
                dp = mm_rt(vals, gm[...])
                if masked:
                    kid = ids_of(
                        base - OWN0 + at + lax.broadcasted_iota(jnp.int32, (KB, 1), 0), starts
                    )
                    bias = jnp.where(kid == qid, 0.0, NEG)
                    st = st + jnp.concatenate([bias] * HL, axis=1)
                p = jnp.exp(st)
                ds = (p * (dp - inner)).astype(BF)
                dkv[pl.ds(at, KB), LW:] += mm(p.astype(BF), gm[...])
                dkv[pl.ds(at, KB), :LW] += mm(ds, qm[...])
                for head in range(HL):
                    part = keys[:, half_of(head) : half_of(head) + 128]
                    dqa[pl.ds(head * QB, QB), :] += mm_lt(ds[:, head * QB : (head + 1) * QB], part)

            pl.when(whole(at))(lambda: put(False))
            pl.when(jnp.logical_not(whole(at)))(lambda: put(True))
            return carry

        lax.fori_loop(0, tiles, one, 0)
        dq[rows, :] = (pick_heads(lambda head: dqa[pl.ds(head * QB, QB), :]) * 0.125).astype(BF)
    dwin[...] = dkv[...].astype(BF)


def attend_back(starts, q, win, grad, att, lt):
    return call(
        attend_back_kernel,
        "attend_back",
        None,
        [starts, q, win, grad, att, lt],
        [((S, LW), BF), ((NW, 2 * LW), BF)],
        [
            pltpu.VMEM((HL * QB, LW), BF),
            pltpu.VMEM((HL * QB, LW), BF),
            pltpu.VMEM((HL * QB, 128), F32),
            pltpu.VMEM((NW, 2 * LW), F32),
        ],
        0,
        limit=22,
        specs=[SM] + [VM] * 5,
    )


def outward_part(
    layer, at, wires, att, hidden_in, sc, ob, gain, bias, b1, wp, w1, w2, loads,
    mixed, br1, br2, rows, act, slope, bufs, between=None,
):
    load_p, load_1, load_2 = loads
    scatter = Scatter(wires, at, scatter_refs(bufs, 0))
    load_p.wait()
    scatter.everything(lambda first: mm(att[pl.ds(first, 2 * R), :], wp[...]))
    if between:
        between()
    one = scatter.total()
    br1[...] = one
    mix = hidden_in + sc[layer, 0:1, :] * (one + ob[layer, 0:1, :])
    mixed[...] = mix
    x_hat, _ = normalized(mix)
    rows[pl.ds(at.own, R), :] = (x_hat * gain[layer, 1:2, :] + bias[layer, 1:2, :]).astype(BF)
    gather = Gather(wires, at, rows)

    def hidden(part):
        x = part.load(rows)
        for j in range(F // 256):
            cols = pl.ds(j * 256, 256)
            pre = mm(x, w1[:, cols]) + b1[layer : layer + 1, cols]
            half = 0.5 * (1.0 + lax.erf(pre * (0.5**0.5)))
            part.store(act, (pre * half).astype(BF), cols)
            bell = jnp.exp(-0.5 * pre * pre) * 0.3989422804014327
            part.store(slope, (half + pre * bell).astype(BF), cols)

    load_1.wait()
    scatter = Scatter(wires, at, scatter_refs(bufs, 1))
    gather_hidden_scatter(
        at, gather, scatter, hidden, lambda part: mm(part.load(act), w2[...]), load_2.wait
    )
    two = scatter.total()
    br2[...] = two
    return mix + sc[layer, 1:2, :] * (two + ob[layer, 1:2, :])


OUT_SEMS = AG_SEMS + 2 * RS_SEMS
OUT_WEIGHTS = [pltpu.VMEM((LW, D), BF), pltpu.VMEM((D, F), BF), pltpu.VMEM((F, D), BF)]
OWN = ((R, D), F32)
TALL = ((S, D), BF)


def fetch_out(layer, wp_hbm, w1_hbm, w2_hbm, wp, w1, w2, ls, base):
    return [
        fetch(src.at[layer], dst, ls.at[base + k])
        for k, (src, dst) in enumerate(((wp_hbm, wp), (w1_hbm, w1), (w2_hbm, w2)))
    ]


def between_kernel(
    att, h, sc, ob, gain, bias, b1, b2, wp_hbm, w1_hbm, w2_hbm, w_hbm,
    mixed, br1, br2, nxt, rows_two, act, slope, rows_one, q, win,
    wp, w1, w2, w, relay, *rest,
):
    bufs = rest[:-3]
    ss, rs, ls = rest[-3:]
    at = Place()
    wires = Wires(ss, rs)
    loads = fetch_out(0, wp_hbm, w1_hbm, w2_hbm, wp, w1, w2, ls, 0)
    loads_qkv = fetch_qkv(1, w_hbm, w, ls, 3)
    greet(chain_partners(at))
    after = outward_part(
        0, at, wires, att, h[...].astype(F32), sc, ob, gain, bias, b1, wp, w1, w2, loads,
        mixed, br1, br2, rows_two, act, slope, bufs,
    )
    nxt[...] = after
    inward_part(
        1, at, wires, after, gain, bias, b2, w, loads_qkv, rows_one, q, win, relay
    )
    wires.close()


def between_layers(cid, *ins):
    return call(
        between_kernel, "between_layers", cid, ins,
        [OWN, OWN, OWN, OWN, TALL, TALL, TALL] + IN_OUTS,
        OUT_WEIGHTS + IN_SCRATCH + scatter_scratch(2),
        OUT_SEMS + IN_SEMS,
        limit=36, specs=[VM] * 8 + [ANY] * 4, local=6,
    )


def start_back(layer, at, wires, grad, sc, g2):
    g2[pl.ds(at.own, R), :] = (grad * sc[layer, 1:2, :]).astype(BF)
    return Gather(wires, at, g2)


def back_out_part(
    layer, at, wires, grad, gather, sc, ob, gain, mixed, br1, br2, act, slope, rows, att,
    wp, w1, w2, gmix, gatt, dw2_hbm, dw1_hbm, dwp, vec, fb, dw2, dw1, g2, gp, g1, bufs,
    ls, base, steps,
):
    vec[0:1, :] = jnp.sum(grad * (br2[...] + ob[layer, 1:2, :]), axis=0, keepdims=True)
    vec[1:2, :] = sc[layer, 1:2, :] * jnp.sum(grad, axis=0, keepdims=True)

    def hidden(part):
        x = part.load(g2)
        for j in range(F // 256):
            cols = pl.ds(j * 256, 256)
            up = mm_rt(x, w2[cols, :])
            part.store(gp, (up * part.load(slope, cols).astype(F32)).astype(BF), cols)

    scatter = Scatter(wires, at, bufs)
    gather_hidden_scatter(
        at, gather, scatter, hidden, lambda part: mm_rt(part.load(gp), w1[...]), lambda: None
    )
    steps(0)
    for j in range(D // 256):
        cols = pl.ds(j * 256, 256)
        dw2[cols, :] = mm_lt(g2[:, cols], act[...]).astype(BF)
    write_2 = fetch(dw2, dw2_hbm, ls.at[base])
    steps(1)
    for j in range(D // 256):
        cols = pl.ds(j * 256, 256)
        dw1[cols, :] = mm_lt(rows[:, cols], gp[...]).astype(BF)
    write_1 = fetch(dw1, dw1_hbm, ls.at[base + 1])
    fb[...] = jnp.broadcast_to(jnp.sum(gp[...].astype(F32), axis=0, keepdims=True), fb.shape)
    grad_in, grad_gain, grad_shift = norm_back(
        mixed[...], gain[layer, 1:2, :], scatter.total()
    )
    mix = grad + grad_in
    gmix[...] = mix
    g1[pl.ds(at.own, R), :] = (mix * sc[layer, 0:1, :]).astype(BF)
    gather = Gather(wires, at, g1)
    steps(2)
    vec[2:3, :] = grad_gain
    vec[3:4, :] = grad_shift
    vec[4:5, :] = jnp.sum(mix * (br1[...] + ob[layer, 0:1, :]), axis=0, keepdims=True)
    vec[5:6, :] = sc[layer, 0:1, :] * jnp.sum(mix, axis=0, keepdims=True)
    vec[6:8, :] = jnp.zeros((2, D), F32)
    gather.near()
    gatt[pl.ds(at.near, 2 * R), :] = mm_rt(g1[pl.ds(at.near, 2 * R), :], wp[...]).astype(BF)
    gather.far()
    steps(3)
    gatt[pl.ds(at.far, 2 * R), :] = mm_rt(g1[pl.ds(at.far, 2 * R), :], wp[...]).astype(BF)
    dwp[...] = mm_lt(g1[...], att[...]).astype(BF)
    steps(4)
    write_2.wait()
    write_1.wait()


BACK_OUTS = [
    OWN, ((S, LW), BF), ((D, F), BF), ((D, F), BF), ((D, LW), BF), ((8, D), F32), ((8, F), F32),
]
BACK_OUT_SPECS = [VM, VM, ANY, ANY, VM, VM, VM]
BACK_SCRATCH = [pltpu.VMEM((D, F), BF)] * 2 + [
    pltpu.VMEM((S, D), BF), pltpu.VMEM((S, F), BF), pltpu.VMEM((S, D), BF),
]
BACK_SEMS = 2 * AG_SEMS + RS_SEMS


def turn_kernel(
    att, h, sc, ob, gain, bias, b1, g, wp_hbm, w1_hbm, w2_hbm,
    out, gmix, gatt, dw2_hbm, dw1_hbm, dwp, vec, fb,
    wp, w1, w2, mixed, br1, br2, rows, act, slope, dw2, dw1, g2, gp, g1, *rest,
):
    bufs = rest[:-3]
    ss, rs, ls = rest[-3:]
    layer = 1
    at = Place()
    wires = Wires(ss, rs)
    loads = fetch_out(layer, wp_hbm, w1_hbm, w2_hbm, wp, w1, w2, ls, 0)
    greet([{"tensor": at.mate}, {"tensor": at.cp}])
    started = []
    after = outward_part(
        layer, at, wires, att, h[...].astype(F32), sc, ob, gain, bias, b1, wp, w1, w2, loads,
        mixed, br1, br2, rows, act, slope, bufs,
        lambda: started.append(start_back(layer, at, wires, g[...], sc, g2)),
    )
    out[...] = after.astype(BF)
    back_out_part(
        layer, at, wires, g[...], started[0], sc, ob, gain, mixed, br1, br2, act, slope, rows,
        att, wp, w1, w2, gmix, gatt, dw2_hbm, dw1_hbm, dwp, vec, fb, dw2, dw1, g2, gp, g1,
        scatter_refs(bufs, 2), ls, 3, lambda step: None,
    )
    wires.close()


def turn(cid, *ins):
    return call(
        turn_kernel, "turn", cid, ins,
        [((R, D), BF)] + BACK_OUTS,
        OUT_WEIGHTS
        + [pltpu.VMEM(*OWN)] * 3
        + [pltpu.VMEM(*TALL)] * 3
        + BACK_SCRATCH
        + scatter_scratch(3),
        OUT_SEMS + BACK_SEMS,
        limit=44, specs=[VM] * 8 + [ANY] * 3, local=5, out_specs=[VM] + BACK_OUT_SPECS,
    )


def back_in_part(
    layer, at, wires, dq, dwin, rows, gmix, h, gain, dwp, w, loads, dw, vec, qb, proj, lanes,
    bufs, steps,
):
    da, db, dc, ua, ub, uc, sdb, sdc, sub, suc = lanes
    chain_up, chain_dn = Line(wires, {"dp": at.up}), Line(wires, {"dp": at.dn})
    low3, low2, low1 = OWN0 - 3 * S, OWN0 - 2 * S, OWN0 - S
    high1, high2, high3 = OWN0 + S, OWN0 + 2 * S, OWN0 + 3 * S

    def chunk(ref, k, base=0):
        return ref.at[pl.ds(base + k * R, R)]

    def plus(base, k, other):
        mine = dwin[pl.ds(base + k * R, R), :].astype(F32)
        return (mine + other[pl.ds(k * R, R), :].astype(F32)).astype(BF)

    ups, dns = {}, {}

    def send(n, k, down, up):
        dns[n, k] = chain_dn.send(*down)
        ups[n, k] = chain_up.send(*up)

    def arrive(n, k):
        chain_dn.arrive(dns[n, k])
        chain_up.arrive(ups[n, k])

    def first(k):
        j = 3 - k
        send(
            1, k, (chunk(dwin, k, low3), chunk(da, k)), (chunk(dwin, j, high3), chunk(ua, j))
        )

    def second(k):
        j = 3 - k
        arrive(1, k)
        sdb[pl.ds(k * R, R), :] = plus(low2, k, da)
        sub[pl.ds(j * R, R), :] = plus(high2, j, ua)
        send(2, k, (chunk(sdb, k), chunk(db, k)), (chunk(sub, j), chunk(ub, j)))

    def third(k):
        j = 3 - k
        arrive(2, k)
        sdc[pl.ds(k * R, R), :] = plus(low1, k, db)
        suc[pl.ds(j * R, R), :] = plus(high1, j, ub)
        send(3, k, (chunk(sdc, k), chunk(dc, k)), (chunk(suc, j), chunk(uc, j)))

    for k in (1, 2, 3):
        first(k)
    send(2, 0, (chunk(dwin, 0, low2), chunk(db, 0)), (chunk(dwin, 3, high2), chunk(ub, 3)))
    def into(first, value):
        dw[:, :, :, :, pl.ds(first, value.shape[-1])] = as_blocks(value)

    proj[:, :LW] = dq[...]
    into(3 * LW, dwp[...])
    into(0, mm_lt(rows[...], dq[...]).astype(BF))
    for k in (1, 2, 3):
        second(k)
    for k in range(4):
        third(k)
    steps(0)
    for k in range(4):
        arrive(3, k)
    own = dwin[pl.ds(OWN0, S), :].astype(F32)
    proj[:, LW:] = (own + dc[...].astype(F32) + uc[...].astype(F32)).astype(BF)
    for copy in loads:
        copy.wait()
    scatter = Scatter(wires, at, bufs)
    scatter.everything(lambda first: mm_rt(proj[pl.ds(first, 2 * R), :], w[...]))
    into(LW, mm_lt(rows[...], proj[:, LW:]).astype(BF))
    steps(1)
    qb[...] = jnp.broadcast_to(jnp.sum(proj[...].astype(F32), axis=0, keepdims=True), qb.shape)
    grad_in, grad_gain, grad_shift = norm_back(
        h[...].astype(F32), gain[layer, 0:1, :], scatter.total()
    )
    vec[0:1, :] = grad_gain
    vec[1:2, :] = grad_shift
    vec[2:8, :] = jnp.zeros((6, D), F32)
    return gmix[...] + grad_in


BLOCKS = ((4, 2, 4, RP, 4 * LW), BF)
EIGHT, EIGHT3 = ((8, D), F32), ((8, 3 * LW), F32)
IN_BACK_SCRATCH = (
    [pltpu.VMEM((D, 3 * LW), BF), pltpu.VMEM((S, 3 * LW), BF)]
    + [pltpu.VMEM((S, 2 * LW), BF)] * 10
)
IN_BACK_SEMS = RS_SEMS + 22


def middle_kernel(*refs):
    take = Refs(refs).take
    dq, dwin, rows_one, gmix1, h, gain, dwp1, dw2_1, dw1_1 = take(9)
    sc, ob = take(2)
    late_hbm = take(7)
    wp_hbm, w1_hbm, w2_hbm, w_hbm = take(4)
    vec_in, qb, gmix, gatt, dw2_hbm, dw1_hbm, dwp, vec, fb = take(9)
    sums = take(NP)
    wp, w1, w2, dw2, dw1, g2, gp, g1 = take(8)
    w, proj = take(2)
    lanes = take(10)
    dw = take(1)[0]
    accs = take(NP)
    wide_bufs, narrow_bufs = take(NP * WIDE_REFS), take(NP * NARROW_REFS)
    bufs = take(2 + 2 * SCATTER_REFS)
    late = take(7)
    ss, rs, ls = take(3)
    at = Place()
    wires = Wires(ss, rs)
    loads = fetch_qkv(1, w_hbm, w, ls)
    loads_out = fetch_out(0, wp_hbm, w1_hbm, w2_hbm, wp, w1, w2, ls, 3)
    loads_out += [
        fetch(src, dst, ls.at[8 + 3 * NP + k]) for k, (src, dst) in enumerate(zip(late_hbm, late))
    ]
    mixed, br1, br2, act, slope, rows_two, att = late
    rings = Rings()
    wide = Wide(wires, rings, (dw2_1, dw1_1, dw), wide_bufs, ls, 8)
    narrow = Narrow(wires, rings, accs, narrow_bufs)
    greet(
        [{"tensor": at.mate}, {"tensor": at.cp}, {"dp": at.up}, {"dp": at.dn}]
        + rings.next_to()
        + [rings.other]
    )
    def steps_in(step):
        if step == 0:
            wide.start(0, 1)
        else:
            wide.start(2, 3)
            wide.forward(0, 1)

    def steps_out(step):
        if step == 0:
            wide.finish(accs, 0, 1)
            narrow.start(0, 1)
        elif step == 1:
            wide.finish(accs, 2, 3)
            narrow.start(2, 3)
            narrow.forward(0, 1)
        elif step == 2:
            narrow.forward(2, 3)
            narrow.beyond(0, 1)
        elif step == 3:
            narrow.beyond(2, 3)
        else:
            narrow.finish(sums)

    grad = back_in_part(
        1, at, wires, dq, dwin, rows_one, gmix1, h, gain, dwp1, w, loads, dw, vec_in, qb, proj,
        lanes, scatter_refs(bufs, 0), steps_in,
    )
    gather = start_back(0, at, wires, grad, sc, g2)
    wide.forward(2, 3)
    for copy in loads_out:
        copy.wait()
    back_out_part(
        0, at, wires, grad, gather, sc, ob, gain, mixed, br1, br2, act, slope, rows_two, att,
        wp, w1, w2, gmix, gatt, dw2_hbm, dw1_hbm, dwp, vec, fb, dw2, dw1, g2, gp, g1,
        scatter_refs(bufs, 1), ls, 6, steps_out,
    )
    wires.close()


def middle(cid, *ins):
    return call(
        middle_kernel, "middle", cid, ins,
        [EIGHT, EIGHT3] + BACK_OUTS + reduced_shapes(),
        OUT_WEIGHTS
        + BACK_SCRATCH
        + IN_BACK_SCRATCH
        + [pltpu.VMEM(*BLOCKS)]
        + [pltpu.VMEM(*wide_shape(width, mode)) for _, _, width, mode in PIECES]
        + wide_scratch()
        + narrow_scratch()
        + scatter_scratch(2)
        + [pltpu.VMEM(*OWN)] * 3
        + [pltpu.VMEM(*TALL)] * 3
        + [pltpu.VMEM((S, LW), BF)],
        IN_BACK_SEMS + BACK_SEMS + 13 * NP,
        limit=51,
        specs=[VM] * 7 + [ANY] * 2 + [VM] * 2 + [ANY] * 11,
        local=15 + 3 * NP,
        out_specs=[VM, VM] + BACK_OUT_SPECS + [VM] * NP,
    )


def final_kernel(*refs):
    take = Refs(refs).take
    dq, dwin, rows, gmix, h, gain, dwp = take(7)
    va1, va0, vb1, fb1, fb0, qb1 = take(6)
    dw2, dw1, w_hbm = take(3)
    g, vout = take(2)
    sums = take(NP)
    w, proj = take(2)
    lanes = take(10)
    dw, vec, qb = take(3)
    accs = take(NP)
    wide_bufs, narrow_bufs = take(NP * WIDE_REFS), take(NP * NARROW_REFS)
    vector_bufs = take(6)
    bufs = take(2 + SCATTER_REFS)
    ss, rs, ls = take(3)
    at = Place()
    wires = Wires(ss, rs)
    loads = fetch_qkv(0, w_hbm, w, ls)
    rings = Rings()
    wide = Wide(wires, rings, (dw2, dw1, dw), wide_bufs, ls, 3)
    narrow = Narrow(wires, rings, accs, narrow_bufs)
    vectors = Vectors(wires, at, rings, vector_bufs)
    greet(
        [{"tensor": at.mate}, {"tensor": at.cp}, {"dp": at.up}, {"dp": at.dn}]
        + [*rings.along_y, *rings.along_x, rings.other]
    )

    def steps(step):
        if step == 0:
            wide.start(0, 1)
        else:
            wide.forward(0, 1)
            wide.start(2, 3)

    g[...] = back_in_part(
        0, at, wires, dq, dwin, rows, gmix, h, gain, dwp, w, loads, dw, vec, qb, proj, lanes,
        bufs, steps,
    )
    vectors.fill(((va0, vec, fb0, qb), (va1, vb1, fb1, qb1)))
    wide.forward(2, 3)
    vectors.over_core()
    wide.finish(accs, 0, 1)
    narrow.start(0, 1)
    vectors.over_chip()
    wide.finish(accs, 2, 3)
    narrow.start(2, 3)
    narrow.forward(0, 1)
    vectors.over_y()
    narrow.forward(2, 3)
    narrow.beyond(0, 1)
    vectors.over_x()
    narrow.beyond(2, 3)
    vectors.finish(vout)
    narrow.finish(sums)
    wires.close()


def final(cid, *ins):
    return call(
        final_kernel, "final", cid, ins,
        [OWN, (VEC, F32)] + reduced_shapes(),
        IN_BACK_SCRATCH
        + [pltpu.VMEM(*BLOCKS), pltpu.VMEM(*EIGHT), pltpu.VMEM(*EIGHT3)]
        + [pltpu.VMEM(*wide_shape(width, mode)) for _, _, width, mode in PIECES]
        + wide_scratch()
        + narrow_scratch()
        + vector_scratch()
        + scatter_scratch(1),
        IN_BACK_SEMS + 13 * NP + 9,
        limit=48,
        specs=[VM] * 13 + [ANY] * 3,
        local=3 + 3 * NP,
    )


def shards(
    tokens_in,
    image_starts,
    norm_gain,
    norm_bias,
    qkv_weight,
    qv_bias,
    proj_weight,
    out_bias,
    layer_scale,
    fc1_weight,
    fc1_bias,
    fc2_weight,
    out_grad,
):
    w_qkv = jnp.transpose(qkv_weight, (0, 2, 1, 3))
    norms = (norm_gain, norm_bias)
    out_weights = (proj_weight, fc1_weight, fc2_weight)
    one0, q0, win0 = inward(0, tokens_in, *norms, qv_bias, w_qkv)
    att0, lt0 = attend(image_starts, q0, win0)
    mixed, br1, br2, h1, two0, act, slope, one1, q1, win1 = between_layers(
        1, att0, tokens_in, layer_scale, out_bias, *norms, fc1_bias, qv_bias, *out_weights, w_qkv
    )
    att1, lt1 = attend(image_starts, q1, win1)
    hidden, gmix, gatt, dw2, dw1, dwp, va1, fb1 = turn(
        2, att1, h1, layer_scale, out_bias, *norms, fc1_bias, out_grad, *out_weights
    )
    dq, dwin = attend_back(image_starts, q1, win1, gatt, att1, lt1)
    vb1, qb1, gmix, gatt, dw2, dw1, dwp, va0, fb0, a1, b1, c1, d1 = middle(
        3, dq, dwin, one1, gmix, h1, norm_gain, dwp, as_blocks(dw2), as_blocks(dw1),
        layer_scale, out_bias, mixed, br1, br2, act, slope, two0, att0, *out_weights, w_qkv,
    )
    dq, dwin = attend_back(image_starts, q0, win0, gatt, att0, lt0)
    grad, vec, a0, b0, c0, d0 = final(
        4, dq, dwin, one0, gmix, tokens_in, norm_gain, dwp, va1, va0, vb1, fb1, fb0, qb1,
        as_blocks(dw2), as_blocks(dw1), w_qkv,
    )
    rows = vec[:16].reshape(2, 8, D)
    qkv = jnp.stack(
        [jnp.concatenate([c0, d0[:, :LW]], 1), jnp.concatenate([c1, d1[:, :LW]], 1)]
    )
    return (
        hidden,
        grad,
        jnp.stack([rows[:, 6], rows[:, 2]], 1),
        jnp.stack([rows[:, 7], rows[:, 3]], 1),
        qkv.reshape(2, RP, 3, LW),
        jnp.stack([vec[18:20, :LW], vec[18:20, 2 * LW : 3 * LW]], 1),
        jnp.stack([d0[:, LW:].T, d1[:, LW:].T]),
        jnp.stack([rows[:, 5], rows[:, 1]], 1),
        jnp.stack([rows[:, 4], rows[:, 0]], 1),
        jnp.stack([b0, b1]),
        vec[16:18],
        jnp.stack([a0.T, a1.T]),
    )


def solution(mesh):
    return jax.shard_map(
        shards,
        mesh=mesh,
        in_specs=(
            P(("dp", "tensor"), None),
            P(),
            P(),
            P(),
            P(None, None, None, "tensor"),
            P(None, None, "tensor"),
            P(None, "tensor", None),
            P(),
            P(),
            P(None, None, "tensor"),
            P(None, "tensor"),
            P(None, "tensor", None),
            P(("dp", "tensor"), None),
        ),
        out_specs=(
            P(("dp", "tensor"), None),
            P(("dp", "tensor"), None),
            P(),
            P(),
            P(None, "dp", None, "tensor"),
            P(None, None, "tensor"),
            P(None, "tensor", "dp"),
            P(),
            P(),
            P(None, "dp", "tensor"),
            P(None, "tensor"),
            P(None, "tensor", "dp"),
        ),
        check_vma=False,
    )
```
